128 devices in a mesh: store: 16 (over x, y), section: 4 (over z), tp: 2 (over core).
Axes of the slice: x: 4, y: 4, z: 4, core: 2. Of those that a mesh axis runs over, the one named last changes fastest.
Arguments:
- tokens: bfloat16 [8192, 2048], P(('store', 'section')), may hold values from -32 to 32
- attn_gain: bfloat16 [2048], replicated, may hold values from 0.099609375 to 1.8984375
- w_query: bfloat16 [2048, 3072], P(None, 'tp'), may hold values from -0.125 to 0.125
- w_latent: bfloat16 [2048, 576], replicated, may hold values from -0.125 to 0.125
- kv_gain: bfloat16 [512], replicated, may hold values from 0.099609375 to 1.8984375
- w_key_up: bfloat16 [16, 512, 128], P('tp'), may hold values from -0.5 to 0.5
- w_value_up: bfloat16 [16, 512, 128], P('tp'), may hold values from -0.25 to 0.25
- w_out: bfloat16 [2048, 2048], P('tp'), may hold values from -0.125 to 0.125
- mlp_gain: bfloat16 [2048], replicated, may hold values from 0.099609375 to 1.8984375
- w_gate: bfloat16 [2048, 1408], P(None, 'tp'), may hold values from -0.125 to 0.125
- w_up: bfloat16 [2048, 1408], P(None, 'tp'), may hold values from -0.125 to 0.125
- w_down: bfloat16 [1408, 2048], P('tp'), may hold values from -0.15625 to 0.15625
- page_pool: bfloat16 [128, 256, 576], P('store'), may hold values from -96 to 96
- hit_owner: int32 [16, 24, 1], replicated, may hold values from 0 to 15; in each aligned block of 24 rows (0 to 23, 24 to 47, ..., all dimensions but the last counted through in order) at most 2 rows name the same one
- hit_slot: int32 [16, 24], replicated, may hold values from 0 to 7
- fetch_count: int32 [16], replicated, may hold values from 1 to 24, 240 in all
Outputs:
- layer_out: bfloat16 [8192, 2048], P(('store', 'section'), 'tp')
- new_latent: bfloat16 [8192, 576], P(('store', 'section'))
The draws below stay inside these ranges and needn't reach their ends.
Inputs may be any that keep to these rules, and one draw needn't show every extreme that they name: `hit_owner`: no store device holds more than 2 of the pages listed for one request. Only the first fetch_count[g] entries of request g's lists are its cached prefix, the rest are padding; the largest count is 24.
All inputs are finite; a program needn't handle non-finite values.
Results may differ from the reference program's by a relative error of at most 0.015.
Values may be sent and summed in bfloat16 or wider, within the bound.
No kernel may reach another device: no remote copies, remote signals or barrier semaphores. Data moves between devices by JAX's collectives and lax.ppermute only.
A program may use at most 128 MiB of HBM per device.

```python
import math
import jax
import jax.numpy as jnp
import numpy as np
from jax import lax

D = 2048
H = 16
NOPE = 128
ROPE = 64
KVR = 512
VDIM = 128
FF = 1408
PAGE = 256
TOK_SECTION = 128
HITS = 24
LATR = 576
GROUPS = 16
TOKENS = 8192
CAP = 2
PAGES_DEV = 8
PAGES = 128
N_STORE = 16
N_SECTION = 4


def draw_tokens(key, part):
    key = jax.random.fold_in(key, 7)
    sub_keys = jax.random.split(key, 2)
    seg_len = TOK_SECTION // 4
    centre = jax.random.normal(sub_keys[0], (TOKENS // seg_len, 1, D), jnp.float32)
    noise = jax.random.normal(sub_keys[1], (TOKENS // seg_len, seg_len, D), jnp.float32)
    row_vals = (0.7 * centre + 0.7 * noise).reshape(TOKENS, D)
    return jnp.clip(row_vals, -32.0, 32.0).astype(jnp.bfloat16)


def draw_page_pool(key, part):
    key = jax.random.fold_in(key, 11)
    sub_keys = jax.random.split(key, 3)
    centre = jax.random.normal(sub_keys[0], (PAGES, 1, KVR), jnp.float32)
    noise = jax.random.normal(sub_keys[1], (PAGES, PAGE, KVR), jnp.float32)
    latent = jnp.clip(0.7 * centre + 0.7 * noise, -8.0, 8.0)
    rotary = jax.random.normal(sub_keys[2], (PAGES, PAGE, ROPE), jnp.float32)
    rotary = jnp.clip(rotary, -96.0, 96.0)
    return jnp.concatenate([latent, rotary], axis=-1).astype(jnp.bfloat16)


def with_ends(drawn, stream_key, least, largest):
    longest = drawn.shape.index(max(drawn.shape))
    spots = []
    for shift in (0, 1):
        where = [jax.random.randint(jax.random.fold_in(stream_key, axis), (), 0, length) for axis, length in enumerate(drawn.shape)]
        where[longest] = (where[longest] + shift) % drawn.shape[longest]
        spots.append(tuple(where))
    return drawn.at[spots[0]].set(least).at[spots[1]].set(largest)


def levels(stream_key, extent, shards, low, high):
    def one(dim, blocks):
        heights = jax.random.uniform(jax.random.fold_in(jax.random.fold_in(stream_key, 6), dim), (blocks,), jnp.float32, low / len(shards), high / len(shards))
        return jnp.repeat(jnp.exp(heights), extent[dim] // blocks).reshape((-1,) + (1,) * (len(extent) - dim - 1))

    loudness = one(*shards[0])
    for cut in shards[1:]:
        loudness = loudness * one(*cut)
    return loudness


def split_up(number_of, total, limit, lean):
    weights = [(1 << 20) // math.isqrt(standing ** lean) + 1 for standing in range(2, number_of + 1)]
    rest, given = total - limit - (number_of - 1), [1] * (number_of - 1)
    while rest > 0:
        movable = [i for i in range(number_of - 1) if given[i] < limit]
        mass, left = sum([weights[i] for i in movable]), rest
        for i in movable:
            extra = min(limit - given[i], max(1, left * weights[i] // mass), rest)
            given[i] = given[i] + extra
            rest = rest - extra
    return np.array([limit] + given)


def uneven_parts(own_key, amount, total, reach, lean):
    if amount == 2:
        one = jax.random.randint(own_key, (), max(1, total - reach), min(reach, total - 1) + 1)
        return jnp.stack([one, total - one])
    tallies = jnp.asarray(split_up(amount, total, reach, lean), jnp.int32)
    pairs = (amount - 1) // 2
    giver, receiver = tallies[1:1 + 2 * pairs:2], tallies[2:2 + 2 * pairs:2]
    margin = jnp.minimum(giver - 1, reach - receiver)
    passed = jax.random.randint(jax.random.fold_in(own_key, 1), (pairs,), 0, 1 << 20) % (margin + 1)
    tallies = tallies.at[1:1 + 2 * pairs:2].set(giver - passed).at[2:2 + 2 * pairs:2].set(receiver + passed)
    return tallies[jax.random.permutation(jax.random.fold_in(own_key, 2), amount)]


def routed_block(rng, own, number, rows, count, top, limit, skew):
    ranking = jax.random.permutation(rng, count)
    packed, ordinary = load_shares(count, rows * top, limit, skew, True), load_shares(count, rows * top, limit, skew, False)
    places = jnp.arange(count)

    def named(lengths, rotation):
        used = int((lengths > 0).sum())
        fixed = max(1, used // 4)
        passed = fixed + (places - fixed + rotation * (used - fixed)) % max(1, count - fixed)
        return jnp.zeros((count,), jnp.int32).at[ranking[jnp.where(places < fixed, places, passed)]].set(jnp.asarray(lengths, jnp.int32))

    lengths = jnp.where(number % 4 == 0, named(packed, number // 4), named(ordinary, number - number // 4 - 1))
    mixed = jax.random.permutation(jax.random.fold_in(own, 3), count)
    giver, taker = mixed[0:count // 2 * 2:2], mixed[1:count // 2 * 2:2]
    margin = jnp.minimum(lengths[giver] - 1, limit - lengths[taker]) // 2
    margin = jnp.where((giver == ranking[0]) | (taker == ranking[0]) | (lengths[taker] == 0), 0, jnp.maximum(margin, 0))
    passed = jax.random.randint(jax.random.fold_in(own, 4), (count // 2,), 0, 1 << 20) % (margin + 1)
    lengths = lengths.at[giver].add(-passed).at[taker].add(passed)
    items = jnp.searchsorted(jnp.cumsum(lengths), jnp.arange(rows * top), side="right").astype(jnp.int32)
    grid = items.reshape(top, rows).T
    grid = grid[jax.random.permutation(jax.random.fold_in(own, 1), rows)]
    rotation = jax.random.randint(jax.random.fold_in(own, 2), (rows, 1), 0, top)
    return jnp.take_along_axis(grid, (jnp.arange(top)[None, :] + rotation) % top, axis=1)


def load_shares(count, total, limit, slope, full):
    weights = [(1 << 20) // math.isqrt(grade ** slope) + 1 for grade in range(1, count + 1)]
    largest = limit if full else min(limit, max(-(-total // count), total * weights[0] // sum(weights)))
    least = 1 if total - largest >= count - 1 else 0
    given, rest = [largest] + [least] * (count - 1), total - largest - least * (count - 1)
    while rest > 0:
        movable = [i for i in range(1, count) if given[i] < largest] or [i for i in range(1, count) if given[i] < limit]
        pool, remaining = sum([weights[i] for i in movable]), rest
        for i in movable:
            extra = min(limit - given[i], max(1, remaining * weights[i] // pool), rest)
            given[i] = given[i] + extra
            rest = rest - extra
    return np.array(given)


def centred(rng, shape, width, bound, pieces=(), held_as=jnp.bfloat16):
    level = levels(rng, shape, pieces, -0.22, 0.18) if pieces else 1.0
    entries = jax.random.normal(rng, shape, jnp.float32) * width * level
    return jnp.minimum(jnp.maximum(entries, -bound), bound).astype(held_as)


def setup_inputs(seed: int = 0) -> dict:
    key_of = jax.random.split(jax.random.key(seed), 17)
    tokens = draw_tokens(jax.random.fold_in(key_of[16], 71), 0)
    attn_gain = jnp.clip(1.0 + 0.18 * jax.random.normal(key_of[1], (D,), jnp.float32), 0.099609375, 1.8984375).astype(jnp.bfloat16)
    w_query = centred(key_of[2], (D, H * (NOPE + ROPE)), D ** -0.5, 0.125, ((1, 2),))
    w_latent = centred(key_of[3], (D, LATR), D ** -0.5, 0.125)
    kv_gain = jnp.clip(1.0 + 0.18 * jax.random.normal(key_of[4], (KVR,), jnp.float32), 0.099609375, 1.8984375).astype(jnp.bfloat16)
    w_key_up = centred(key_of[5], (H, KVR, NOPE), NOPE ** -0.5, 0.5, ((0, 2),))
    w_value_up = centred(key_of[6], (H, KVR, VDIM), KVR ** -0.5, 0.25, ((0, 2),))
    w_out = centred(key_of[7], (H * VDIM, D), (H * VDIM) ** -0.5, 0.125, ((0, 2),))
    mlp_gain = jnp.clip(1.0 + 0.18 * jax.random.normal(key_of[8], (D,), jnp.float32), 0.099609375, 1.8984375).astype(jnp.bfloat16)
    w_gate = centred(key_of[9], (D, FF), D ** -0.5, 0.125, ((1, 2),))
    w_up = centred(key_of[10], (D, FF), D ** -0.5, 0.125, ((1, 2),))
    w_down = centred(key_of[11], (FF, D), FF ** -0.5, 0.15625, ((0, 2),))
    page_pool = draw_page_pool(jax.random.fold_in(key_of[16], 71), 0)
    hit_owner_keys = jax.random.split(jax.random.fold_in(key_of[13], 1), GROUPS * HITS // HITS)
    hit_owner_turns = jax.random.permutation(jax.random.fold_in(key_of[13], 3), GROUPS * HITS // HITS)
    hit_owner = jax.vmap(lambda own, number: routed_block(jax.random.fold_in(key_of[13], 2), own, number, HITS, N_STORE, 1, CAP, 1))(hit_owner_keys, hit_owner_turns).reshape((GROUPS, HITS, 1))
    hit_slot = with_ends(jax.random.randint(key_of[14], (GROUPS, HITS), 0, PAGES_DEV), jax.random.fold_in(key_of[14], 1), 0, PAGES_DEV - 1).astype(jnp.int32)
    fetch_count = uneven_parts(key_of[15], GROUPS, GROUPS * HITS * 5 // 8, HITS, 1).astype(jnp.int32)
    return {"tokens": tokens, "attn_gain": attn_gain, "w_query": w_query, "w_latent": w_latent, "kv_gain": kv_gain, "w_key_up": w_key_up, "w_value_up": w_value_up, "w_out": w_out, "mlp_gain": mlp_gain, "w_gate": w_gate, "w_up": w_up, "w_down": w_down, "page_pool": page_pool, "hit_owner": hit_owner, "hit_slot": hit_slot, "fetch_count": fetch_count}


EPSILON = 1e-06
ROTARY_BASE = 10000.0
MASKED_SCORE = -1e+30

def rms_scale(values, gain_vec):
    mean_sq = lax.optimization_barrier(jnp.mean(values * values, axis=-1, keepdims=True))
    return values * lax.rsqrt(mean_sq + EPSILON) * gain_vec.astype(values.dtype)

def angles(position, rot_width):
    half_dim = rot_width // 2
    freq_table = ROTARY_BASE ** (-(jnp.arange(half_dim, dtype=jnp.float32) / half_dim))
    return position[:, None] * freq_table[None, :]

def rotate(values, angle_table):
    half_dim = values.shape[-1] // 2
    lower_half = values[..., :half_dim]
    upper_half = values[..., half_dim:]
    cosine = jnp.cos(angle_table)
    sine_val = jnp.sin(angle_table)
    return jnp.concatenate([lower_half * cosine - upper_half * sine_val, lower_half * sine_val + upper_half * cosine], axis=-1)

def reference(tokens, attn_gain, w_query, w_latent, kv_gain, w_key_up, w_value_up, w_out, mlp_gain, w_gate, w_up, w_down, page_pool, hit_owner, hit_slot, fetch_count):
    span_len = TOK_SECTION * N_SECTION
    score_scale = (NOPE + ROPE) ** (-0.5)
    grouped = tokens.reshape(GROUPS, span_len, D)

    def one_group(group_item):
        tok_rows, prefix_pages, owner_row, slot_row = group_item
        offset = jnp.arange(span_len, dtype=jnp.int32)
        position = (prefix_pages * PAGE + offset).astype(jnp.float32)
        normed = rms_scale(tok_rows.astype(jnp.float32), attn_gain).astype(jnp.bfloat16)
        queries = jnp.dot(normed, w_query, preferred_element_type=jnp.float32).astype(jnp.bfloat16)
        queries = queries.reshape(span_len, H, NOPE + ROPE)
        query_rot = rotate(queries[:, :, NOPE:].astype(jnp.float32), angles(position, ROPE)[:, None, :]).astype(jnp.bfloat16)
        query_lat = jnp.einsum('thn,hcn->thc', queries[:, :, :NOPE].astype(jnp.float32), w_key_up.astype(jnp.float32)).astype(jnp.bfloat16)
        probes = jnp.concatenate([query_lat, query_rot], axis=-1)
        latent_raw = jnp.dot(normed, w_latent, preferred_element_type=jnp.float32)
        latent = rms_scale(latent_raw[:, :KVR], kv_gain)
        key_rot = rotate(latent_raw[:, KVR:], angles(position, ROPE))
        new_latent = jnp.concatenate([latent, key_rot], axis=-1).astype(jnp.bfloat16)
        page_index = owner_row * PAGES_DEV + slot_row
        cached = page_pool[page_index].reshape(HITS * PAGE, KVR + ROPE)
        all_keys = jnp.concatenate([cached, new_latent], axis=0)
        page_live = jnp.repeat(jnp.arange(HITS, dtype=jnp.int32) < prefix_pages, PAGE)
        causal = offset[None, :] <= offset[:, None]
        key_mask = jnp.concatenate([jnp.broadcast_to(page_live[None, :], (span_len, HITS * PAGE)), causal], axis=1)

        def attend_head(head_probe):
            scores = jnp.dot(head_probe, all_keys.T, preferred_element_type=jnp.float32) * score_scale
            scores = jnp.where(key_mask, scores, MASKED_SCORE)
            row_top = lax.optimization_barrier(jnp.max(scores, axis=1, keepdims=True))
            weight = jnp.where(key_mask, jnp.exp(scores - row_top), 0.0)
            row_total = lax.optimization_barrier(jnp.sum(weight, axis=1, keepdims=True))
            summed = jnp.dot(weight.astype(jnp.bfloat16), all_keys[:, :KVR], preferred_element_type=jnp.float32)
            return (summed / row_total).astype(jnp.bfloat16)
        mixed = jnp.swapaxes(lax.map(attend_head, jnp.swapaxes(probes, 0, 1)), 0, 1)
        per_head = jnp.einsum('thc,hcv->thv', mixed.astype(jnp.float32), w_value_up.astype(jnp.float32)).astype(jnp.bfloat16)
        per_head = per_head.reshape(span_len, H * VDIM)
        attended = jnp.dot(per_head, w_out, preferred_element_type=jnp.float32)
        middle = (tok_rows.astype(jnp.float32) + attended).astype(jnp.bfloat16)
        mlp_in = rms_scale(middle.astype(jnp.float32), mlp_gain).astype(jnp.bfloat16)
        gate_act = jnp.dot(mlp_in, w_gate, preferred_element_type=jnp.float32)
        up_act = jnp.dot(mlp_in, w_up, preferred_element_type=jnp.float32)
        hidden = (jax.nn.silu(gate_act) * up_act).astype(jnp.bfloat16)
        down_part = jnp.dot(hidden, w_down, preferred_element_type=jnp.float32)
        layer_out = (middle.astype(jnp.float32) + down_part).astype(jnp.bfloat16)
        return (layer_out, new_latent)
    outputs, latents = lax.map(one_group, (grouped, fetch_count, hit_owner[:, :, 0], hit_slot))
    return (outputs.reshape(TOKENS, D), latents.reshape(TOKENS, KVR + ROPE))
```

```python
import functools
import math

import jax
import jax.numpy as jnp
import numpy as np
from jax import lax
from jax.experimental import pallas as pl
from jax.experimental.pallas import tpu as pltpu
from jax.sharding import PartitionSpec as P

NOPE = 128
ROPE = 64
KVR = 512
PAGE = 256
LAT = KVR + ROPE
WIDE = KVR + 2 * ROPE
MSG = 2 * LAT
VDIM = 128
EPSILON = 1e-06
ROTARY_BASE = 10000.0
MASKED_SCORE = -1e30
SCALE = (NOPE + ROPE) ** (-0.5) / math.log(2.0)
F32 = jnp.float32
BF16 = jnp.bfloat16
MB = 1024 * 1024

VMEM = pl.BlockSpec(memory_space=pltpu.VMEM)
SMEM = pl.BlockSpec(memory_space=pltpu.SMEM)
HBM = pl.BlockSpec(memory_space=pltpu.HBM)


def params(mb):
    return pltpu.CompilerParams(vmem_limit_bytes=mb * MB)


def dot(a, b):
    return jnp.dot(a, b, preferred_element_type=F32)


def dot_nt(a, b):
    return lax.dot_general(a, b, (((1,), (1,)), ((), ())), preferred_element_type=F32)


def rms(values, gain):
    mean_sq = jnp.mean(values * values, axis=-1, keepdims=True)
    return values * lax.rsqrt(mean_sq + EPSILON) * gain


def turn(values, cosine, sine):
    lane = lax.broadcasted_iota(jnp.int32, values.shape, 1)
    low = (lane & (ROPE // 2)) == 0
    partner = jnp.where(
        low, pltpu.roll(values, 128 - ROPE // 2, axis=1), pltpu.roll(values, ROPE // 2, axis=1)
    )
    return values * cosine + partner * sine


def pack_kernel(
    place, owner_src, slot_src, pool_src, out, owner, slot, pool, sems
):
    n_pages, width, page = pool.shape
    n_store, rows, _ = out.shape
    window = 128
    per = window // rows
    pairs = [(owner_src, owner), (slot_src, slot)]
    strip = n_pages // 4
    for k in range(4):
        at = pl.ds(k * strip, strip)
        pairs.append((pool_src.at[at], pool.at[at]))
    copies = [
        pltpu.make_async_copy(src, dst, sems.at[i]) for i, (src, dst) in enumerate(pairs)
    ]
    for copy in copies:
        copy.start()
    for copy in copies:
        copy.wait()
    upper = place[1] >= per
    first = (place[1] % per) * rows
    lane = lax.broadcasted_iota(jnp.int32, (width, window), 1)
    joined = []
    for at in range(0, n_pages, per):
        part = None
        for k in range(per):
            both = pool[at + k]
            moved = jnp.where(upper, both[:, window:], both[:, :window]).astype(F32)
            moved = pltpu.roll(moved, (k * rows - first + window) % window, axis=1)
            part = moved if part is None else jnp.where(lane >= k * rows, moved, part)
        joined.append(part.astype(BF16))
    stage = jnp.concatenate(joined, axis=1)
    total = n_store * rows
    n_list = owner.shape[1]
    held = owner[...] == place[0]
    entry = lax.broadcasted_iota(jnp.int32, held.shape, 1)
    low = jnp.min(jnp.where(held, entry, n_list), axis=1, keepdims=True)
    high = jnp.max(jnp.where(held, entry, -1), axis=1, keepdims=True)
    row = lax.broadcasted_iota(jnp.int32, (rows, 1), 0)
    column = lax.broadcasted_iota(jnp.int32, (total, n_pages * rows), 1)
    taken = []
    for which in (low, high):
        page = jnp.sum(jnp.where(entry == which, slot[...], 0), axis=1, keepdims=True) * rows
        wanted = [jnp.broadcast_to(page[g : g + 1], (rows, 1)) + row for g in range(n_store)]
        wanted = jnp.concatenate(wanted, axis=0)
        choose = jnp.where(column == wanted, 1.0, 0.0).astype(BF16)
        taken.append(dot_nt(choose, stage))
    ropes = jnp.concatenate([part[:, KVR:] for part in taken], axis=1)
    for which, part in enumerate(taken):
        out[:, :, which * KVR : (which + 1) * KVR] = (
            part[:, :KVR].astype(BF16).reshape(n_store, rows, KVR)
        )
    out[:, :, 2 * KVR :] = ropes.astype(BF16).reshape(n_store, rows, 2 * ROPE)


def pack_pages(place, owner, slot, pool_t, rows):
    n_store = owner.shape[0]
    return pl.pallas_call(
        pack_kernel,
        out_shape=jax.ShapeDtypeStruct((n_store, rows, MSG), BF16),
        in_specs=[SMEM] + [HBM] * 3,
        out_specs=VMEM,
        scratch_shapes=[
            pltpu.VMEM(owner.shape, jnp.int32),
            pltpu.VMEM(slot.shape, jnp.int32),
            pltpu.VMEM(pool_t.shape, BF16),
            pltpu.SemaphoreType.DMA((6,)),
        ],
        compiler_params=params(60),
        name="pack_pages",
    )(place, owner, slot, pool_t)


def keys_kernel(place, owner, count, pages, out, seen):
    rows = pages.shape[1]
    group = place[0]
    lane = lax.broadcasted_iota(jnp.int32, (rows, 128), 1)
    for k in range(pages.shape[0]):
        seen[k] = 0
    for j in range(owner.shape[1]):
        source = owner[group, j]
        second = seen[source] > 0
        seen[source] = 1
        bias = jnp.where(j < count[group], 0.0, MASKED_SCORE)
        row = pages[source]
        at = pl.ds(j * rows, rows)
        out[at, :KVR] = jnp.where(second, row[:, KVR : 2 * KVR], row[:, :KVR])
        pair = row[:, 2 * KVR :].astype(F32)
        rot = jnp.where(second, pltpu.roll(pair, ROPE, axis=1), pair)
        last = jnp.where(lane == ROPE, bias, 0.0)
        out[at, KVR:] = jnp.where(lane < ROPE, rot, last).astype(BF16)


def build_keys(place, owner, count, pages):
    n_keys = owner.shape[1] * pages.shape[1]
    return pl.pallas_call(
        keys_kernel,
        out_shape=jax.ShapeDtypeStruct((n_keys, WIDE), BF16),
        in_specs=[SMEM, SMEM, SMEM, VMEM],
        out_specs=VMEM,
        scratch_shapes=[pltpu.SMEM((pages.shape[0],), jnp.int32)],
        compiler_params=params(24),
        name="build_keys",
    )(place, owner, count, pages)


def rotation_table(n_rows):
    half = ROPE // 2
    freq = np.float32(ROTARY_BASE) ** (-(np.arange(half, dtype=np.float32) / np.float32(half)))
    angle = np.arange(n_rows, dtype=np.float32)[:, None] * freq.astype(np.float32)[None, :]
    angle = angle.astype(np.float64)
    parts = [np.cos(angle), np.cos(angle), -np.sin(angle), np.sin(angle)]
    return np.concatenate(parts, axis=1).astype(np.float32)


def project_kernel(
    place, count, tokens_src, gain, table, w_query_src, w_latent_src, kv_gain, query, new_latent, span,
    tokens, turns, w_query, w_latent_t, total, sems
):
    rows = tokens.shape[0]
    start = pl.multiple_of(count[place[0]] * PAGE + place[2] * rows, rows)
    pairs = [(tokens_src, tokens), (table.at[pl.ds(start, rows), :], turns)]
    pieces = 8
    depth = w_query.shape[0] // pieces
    for k in range(pieces):
        at = pl.ds(k * depth, depth)
        pairs.append((w_query_src.at[at, :], w_query.at[at, :]))
    strip = w_latent_t.shape[0] // 4
    for k in range(4):
        at = pl.ds(k * strip, strip)
        pairs.append((w_latent_src.at[at, :], w_latent_t.at[at, :]))
    copies = [
        pltpu.make_async_copy(src, dst, sems.at[i]) for i, (src, dst) in enumerate(pairs)
    ]
    for copy in copies:
        copy.start()
    copies[0].wait()
    normed = rms(tokens[...].astype(F32), gain[...].astype(F32)).astype(BF16)
    copies[1].wait()
    cosine, sine = turns[:, :ROPE], turns[:, ROPE:]
    cosine = jnp.concatenate([cosine, cosine], axis=1)
    sine = jnp.concatenate([sine, sine], axis=1)
    for k in range(0, pieces, 2):
        copies[2 + k].wait()
        copies[3 + k].wait()
        at = slice(k * depth, (k + 2) * depth)
        part = dot(normed[:, at], w_query[at, :])
        total[...] = part if k == 0 else total[...] + part
    head = NOPE + ROPE
    for at in range(0, query.shape[1], 2 * head):
        part = total[:, at : at + 2 * head].astype(BF16).astype(F32)
        query[:, at : at + NOPE] = part[:, :NOPE].astype(BF16)
        query[:, at + NOPE : at + 2 * NOPE] = part[:, head : head + NOPE].astype(BF16)
        pair = jnp.concatenate([part[:, NOPE:head], part[:, head + NOPE :]], axis=1)
        query[:, at + 2 * NOPE : at + 2 * head] = (turn(pair, cosine, sine) * SCALE).astype(BF16)
    for copy in copies[2 + pieces :]:
        copy.wait()
    raw = dot_nt(normed, w_latent_t[...])
    latent = rms(raw[:, :KVR], kv_gain[...].astype(F32)).astype(BF16)
    pair = jnp.concatenate([raw[:, KVR:], raw[:, KVR:]], axis=1)
    turned = turn(pair, cosine, sine)
    new_latent[:KVR, :] = latent.astype(F32).T.astype(BF16)
    new_latent[KVR:, :] = turned.T[:ROPE].astype(BF16)
    lane = lax.broadcasted_iota(jnp.int32, turned.shape, 1)
    span[:, :KVR] = latent
    span[:, KVR:] = jnp.where(lane < ROPE, turned, 0.0).astype(BF16)


def project(place, count, tokens, gain, table, w_query, w_latent_t, kv_gain):
    rows, width = tokens.shape
    cols = w_query.shape[1]
    return pl.pallas_call(
        project_kernel,
        out_shape=[
            jax.ShapeDtypeStruct((rows, cols), BF16),
            jax.ShapeDtypeStruct((LAT, rows), BF16),
            jax.ShapeDtypeStruct((rows, WIDE), BF16),
        ],
        in_specs=[SMEM] * 2 + [HBM, VMEM] + [HBM] * 3 + [VMEM],
        out_specs=[VMEM] * 3,
        scratch_shapes=[
            pltpu.VMEM(tokens.shape, BF16),
            pltpu.VMEM((rows, 2 * ROPE), F32),
            pltpu.VMEM(w_query.shape, BF16),
            pltpu.VMEM(w_latent_t.shape, BF16),
            pltpu.VMEM((rows, cols), F32),
            pltpu.SemaphoreType.DMA((14,)),
        ],
        compiler_params=params(60),
        cost_estimate=pl.CostEstimate(
            flops=2 * rows * width * (cols + LAT),
            bytes_accessed=2 * width * (cols + LAT),
            transcendentals=0,
        ),
        name="project",
    )(place, count, tokens, gain, table, w_query, w_latent_t, kv_gain)


def attend_kernel(by, n_section, place, query, key_up, value_up, near, *refs):
    n_head, rows = key_up.shape[0], query.shape[0]
    if len(refs) == 5:
        arrived, span, out, far, probes = refs
        far[...] = arrived[...]
    else:
        far, span, out, probes = refs
    blocks = (near, far, span)
    lane = lax.broadcasted_iota(jnp.int32, (rows, 128), 1)
    head_pair = 2 * (NOPE + ROPE)
    at_once = 2
    tile = at_once * rows
    steps = n_head // at_once
    width = n_head * NOPE
    for h in range(n_head):
        at = pl.ds(h * rows, rows)
        base = (h // 2) * head_pair
        nope = query[:, base + (h % 2) * NOPE : base + (h % 2 + 1) * NOPE]
        probes[at, :KVR] = (dot_nt(nope, key_up[h]) * SCALE).astype(BF16)
        pair = query[:, base + 2 * NOPE : base + head_pair].astype(F32)
        if h % 2 == 1:
            pair = pltpu.roll(pair, ROPE, axis=1)
        one = jnp.where(lane == ROPE, 1.0, 0.0)
        probes[at, KVR:] = jnp.where(lane < ROPE, pair, one).astype(BF16)

    if by == 0:
        row_of = lax.broadcasted_iota(jnp.int32, (tile, rows), 0) & (rows - 1)
        key_of = lax.broadcasted_iota(jnp.int32, (tile, rows), 1)
        hide = jnp.where(key_of <= row_of, 0.0, MASKED_SCORE)
    else:
        hide = jnp.where(place[2] + by < n_section, 0.0, MASKED_SCORE)

    def score(i):
        probe = probes[i * tile : (i + 1) * tile, :]
        parts = [dot_nt(probe, block[...]) for block in blocks]
        parts[2] = parts[2] + hide
        return parts

    def finish(i, parts, stats):
        tops = [jnp.max(part, axis=1, keepdims=True) for part in parts]
        top = functools.reduce(jnp.maximum, tops)
        total, summed = 0.0, 0.0
        for part, block in zip(parts, blocks):
            weight = jnp.exp2(part - top)
            total = total + jnp.sum(weight, axis=1, keepdims=True)
            summed = summed + dot(weight.astype(BF16), block[:, :KVR])
        mixed = (summed * (1.0 / total)).astype(BF16)
        level = top + jnp.log2(total)
        for k in range(at_once):
            h = i * at_once + k
            value = dot(mixed[k * rows : (k + 1) * rows], value_up[h])
            out[:, h * VDIM : (h + 1) * VDIM] = value.astype(BF16)
            stats = jnp.where(lane == h, level[k * rows : (k + 1) * rows], stats)
        return stats

    stats = jnp.zeros((rows, 128), F32)
    parts = score(0)
    for i in range(steps):
        following = score(i + 1) if i + 1 < steps else None
        stats = finish(i, parts, stats)
        parts = following
    high = stats.astype(BF16).astype(F32)
    rest = stats - high
    mid = rest.astype(BF16).astype(F32)
    joined = high + pltpu.roll(mid, n_head, axis=1) + pltpu.roll(rest - mid, 2 * n_head, axis=1)
    out[:, width:] = joined.astype(BF16)


def attend(by, n_section, place, query, key_up, value_up, near, far, span, keep_far):
    rows, n_head = query.shape[0], key_up.shape[0]
    n_keys = 2 * near.shape[0] + rows
    out_shape = [jax.ShapeDtypeStruct((rows, n_head * VDIM + 128), BF16)]
    if keep_far:
        out_shape.append(jax.ShapeDtypeStruct(far.shape, BF16))
    return pl.pallas_call(
        functools.partial(attend_kernel, by, n_section),
        out_shape=out_shape,
        in_specs=[SMEM] + [VMEM] * 6,
        out_specs=[VMEM] * len(out_shape),
        scratch_shapes=[pltpu.VMEM((n_head * rows, WIDE), BF16)],
        compiler_params=params(28),
        cost_estimate=pl.CostEstimate(
            flops=2 * rows * n_head * n_keys * (WIDE + KVR),
            bytes_accessed=2 * n_keys * WIDE,
            transcendentals=rows * n_head * n_keys,
        ),
        name="attend_%d" % by,
    )(place, query, key_up, value_up, near, far, span)


def output_kernel(n_head, own, one, two, three, weight, exact, send):
    parts = (own, one, two, three)
    width = n_head * VDIM
    levels = []
    for part in parts:
        stat = part[:, width:].astype(F32)
        rest = pltpu.roll(stat, 128 - n_head, axis=1) + pltpu.roll(stat, 128 - 2 * n_head, axis=1)
        levels.append(stat + rest)
    top = functools.reduce(jnp.maximum, levels)
    shares = [jnp.exp2(level - top) for level in levels]
    total = functools.reduce(jnp.add, shares)
    head_of = lax.broadcasted_iota(jnp.int32, (128, width), 0)
    lane_of = lax.broadcasted_iota(jnp.int32, (128, width), 1)
    begin = head_of * VDIM
    spread = jnp.where((lane_of >= begin) & (lane_of < begin + VDIM), 1.0, 0.0).astype(BF16)
    mixed = 0.0
    for part, share in zip(parts, shares):
        share = share / total
        high = share.astype(BF16)
        low = (share - high.astype(F32)).astype(BF16)
        factor = dot(high, spread) + dot(low, spread)
        mixed = mixed + part[:, :width].astype(F32) * factor
    per_head = mixed.astype(BF16)
    block = 512
    for at in range(0, weight.shape[1], block):
        part = dot(per_head, weight[:, at : at + block])
        exact[:, at : at + block] = part
        send[:, at : at + block] = part.astype(BF16)


def project_output(own, one, two, three, w_out):
    rows = own.shape[0]
    depth, cols = w_out.shape
    return pl.pallas_call(
        functools.partial(output_kernel, depth // VDIM),
        out_shape=[
            jax.ShapeDtypeStruct((rows, cols), F32),
            jax.ShapeDtypeStruct((rows, cols), BF16),
        ],
        in_specs=[VMEM] * 5,
        out_specs=[VMEM] * 2,
        compiler_params=params(16),
        name="project_output",
    )(own, one, two, three, w_out)


def expert_kernel(place, tokens, exact, other, gain, w_gate_t, w_up_t, w_down, keep, send):
    half = keep.shape[1]
    middle = tokens[...].astype(F32) + (exact[...] + other[...].astype(F32))
    middle = middle.astype(BF16).astype(F32)
    mlp_in = rms(middle, gain[...].astype(F32)).astype(BF16)
    gate = dot_nt(mlp_in, w_gate_t[...])
    up = dot_nt(mlp_in, w_up_t[...])
    hidden = (gate / (1.0 + jnp.exp(-gate)) * up).astype(BF16)
    low = dot(hidden, w_down[:, :half])
    high = dot(hidden, w_down[:, half:])
    first = place[3] == 0
    keep[...] = jnp.where(first, middle[:, :half] + low, middle[:, half:] + high)
    send[...] = jnp.where(first, high, low).astype(BF16)


def expert(place, tokens, exact, other, gain, w_gate_t, w_up_t, w_down):
    rows, width = tokens.shape
    half = width // 2
    return pl.pallas_call(
        expert_kernel,
        out_shape=[
            jax.ShapeDtypeStruct((rows, half), F32),
            jax.ShapeDtypeStruct((rows, half), BF16),
        ],
        in_specs=[SMEM] + [VMEM] * 7,
        out_specs=[VMEM] * 2,
        compiler_params=params(24),
        name="expert",
    )(place, tokens, exact, other, gain, w_gate_t, w_up_t, w_down)


def on_device(
    tokens,
    attn_gain,
    w_query,
    w_latent,
    kv_gain,
    w_key_up,
    w_value_up,
    w_out,
    mlp_gain,
    w_gate,
    w_up,
    w_down,
    page_pool,
    hit_owner,
    hit_slot,
    fetch_count,
):
    n_store = lax.axis_size("store")
    n_section = lax.axis_size("section")
    n_tp = lax.axis_size("tp")
    group = lax.axis_index("store")
    section = lax.axis_index("section")
    core = lax.axis_index("tp")
    rows = tokens.shape[0]
    share = PAGE // (n_section * n_tp)

    swap = [(0, 1), (1, 0)]
    place = jnp.stack([group, section * n_tp + core, section, core]).astype(jnp.int32)
    owner = hit_owner[:, :, 0]
    outgoing = pack_pages(place, owner, hit_slot, jnp.swapaxes(page_pool, 1, 2), share)
    outgoing, early_tokens = lax.optimization_barrier((outgoing, tokens))
    outgoing = outgoing.reshape(n_store, 2, share // 2, MSG)
    arrived = lax.all_to_all(outgoing, "store", split_axis=0, concat_axis=0, tiled=True)
    arrived = arrived.reshape(n_store, share, MSG)

    def shift(value, by):
        pairs = [((z + by) % n_section, z) for z in range(n_section)]
        return lax.ppermute(value, "section", pairs)

    table = rotation_table((hit_owner.shape[1]) * PAGE + n_section * rows)
    query, new_latent, span = project(
        place,
        fetch_count,
        early_tokens,
        attn_gain.reshape(1, -1),
        jnp.asarray(table),
        w_query,
        w_latent.T,
        kv_gain.reshape(1, -1),
    )
    next_query, last_query = shift(query, 1), shift(query, -1)
    arrived, next_query, last_query, span = lax.optimization_barrier(
        (arrived, next_query, last_query, span)
    )
    cut = rows // 2
    far_low, far_high = shift(next_query[:cut], 1), shift(last_query[cut:], -1)

    near = build_keys(place, owner, fetch_count, arrived)
    far = lax.ppermute(near, "tp", swap)

    def partial_for(by, query, far, keep_far=False):
        return attend(
            by, n_section, place, query, w_key_up, w_value_up, near, far, span, keep_far
        )

    one, far = partial_for(1, next_query, far, True)
    _, far_low, far_high = lax.optimization_barrier((one, far_low, far_high))
    one = shift(one, -1)
    (two,) = partial_for(2, jnp.concatenate([far_low, far_high], axis=0), far)
    _, last_query = lax.optimization_barrier((two, last_query))
    two = shift(two, -2)
    (three,) = partial_for(3, last_query, far)
    _, query = lax.optimization_barrier((three, query))
    three = shift(three, -3)
    (own,) = partial_for(0, query, far)
    exact, send = project_output(own, one, two, three, w_out)
    incoming = lax.ppermute(send, "tp", swap)
    keep, send = expert(
        place,
        tokens,
        exact,
        incoming,
        mlp_gain.reshape(1, -1),
        w_gate.T,
        w_up.T,
        w_down,
    )
    layer_out = (keep + lax.ppermute(send, "tp", swap).astype(F32)).astype(BF16)
    return (layer_out, new_latent.T)


def solution(mesh):
    in_specs = (
        P(("store", "section"), None),
        P(),
        P(None, "tp"),
        P(),
        P(),
        P("tp", None, None),
        P("tp", None, None),
        P("tp", None),
        P(),
        P(None, "tp"),
        P(None, "tp"),
        P("tp", None),
        P("store", None, None),
        P(),
        P(),
        P(),
    )
    out_specs = (P(("store", "section"), "tp"), P(("store", "section"), None))
    return jax.shard_map(
        on_device, mesh=mesh, in_specs=in_specs, out_specs=out_specs, check_vma=False
    )
```

```python
import functools
import math

import jax
import jax.numpy as jnp
import numpy as np
from jax import lax
from jax.experimental import pallas as pl
from jax.experimental.pallas import tpu as pltpu
from jax.sharding import PartitionSpec as P

NOPE = 128
ROPE = 64
KVR = 512
PAGE = 256
LAT = KVR + ROPE
WIDE = KVR + 2 * ROPE
MSG = 2 * LAT
VDIM = 128
EPSILON = 1e-06
ROTARY_BASE = 10000.0
MASKED_SCORE = -1e30
SCALE = (NOPE + ROPE) ** (-0.5) / math.log(2.0)
F32 = jnp.float32
BF16 = jnp.bfloat16
MB = 1024 * 1024

VMEM = pl.BlockSpec(memory_space=pltpu.VMEM)
SMEM = pl.BlockSpec(memory_space=pltpu.SMEM)
HBM = pl.BlockSpec(memory_space=pltpu.HBM)


def params(mb):
    return pltpu.CompilerParams(vmem_limit_bytes=mb * MB)


def dot(a, b):
    return jnp.dot(a, b, preferred_element_type=F32)


def dot_nt(a, b):
    return lax.dot_general(a, b, (((1,), (1,)), ((), ())), preferred_element_type=F32)


def rms(values, gain):
    mean_sq = jnp.mean(values * values, axis=-1, keepdims=True)
    return values * lax.rsqrt(mean_sq + EPSILON) * gain


def turn(values, cosine, sine):
    lane = lax.broadcasted_iota(jnp.int32, values.shape, 1)
    low = (lane & (ROPE // 2)) == 0
    partner = jnp.where(
        low, pltpu.roll(values, 128 - ROPE // 2, axis=1), pltpu.roll(values, ROPE // 2, axis=1)
    )
    return values * cosine + partner * sine


def pack_kernel(
    place, owner_src, slot_src, pool_src, out, owner, slot, pool, sems
):
    n_pages, width, window = pool.shape
    n_store, rows, _ = out.shape
    per = window // rows
    pairs = [(owner_src, owner), (slot_src, slot)]
    part = pl.ds(pl.multiple_of((place[1] // per) * window, window), window)
    strip = n_pages // 4
    for k in range(4):
        at = pl.ds(k * strip, strip)
        pairs.append((pool_src.at[at, :, part], pool.at[at]))
    copies = [
        pltpu.make_async_copy(src, dst, sems.at[i]) for i, (src, dst) in enumerate(pairs)
    ]
    for copy in copies:
        copy.start()
    for copy in copies:
        copy.wait()
    first = (place[1] % per) * rows
    lane = lax.broadcasted_iota(jnp.int32, (width, window), 1)
    joined = []
    for at in range(0, n_pages, per):
        part = None
        for k in range(per):
            moved = pltpu.roll(pool[at + k].astype(F32), (k * rows - first + window) % window, axis=1)
            part = moved if part is None else jnp.where(lane >= k * rows, moved, part)
        joined.append(part.astype(BF16))
    stage = jnp.concatenate(joined, axis=1)
    total = n_store * rows
    n_list = owner.shape[1]
    held = owner[...] == place[0]
    entry = lax.broadcasted_iota(jnp.int32, held.shape, 1)
    low = jnp.min(jnp.where(held, entry, n_list), axis=1, keepdims=True)
    high = jnp.max(jnp.where(held, entry, -1), axis=1, keepdims=True)
    row = lax.broadcasted_iota(jnp.int32, (rows, 1), 0)
    column = lax.broadcasted_iota(jnp.int32, (total, n_pages * rows), 1)
    taken = []
    for which in (low, high):
        page = jnp.sum(jnp.where(entry == which, slot[...], 0), axis=1, keepdims=True) * rows
        wanted = [jnp.broadcast_to(page[g : g + 1], (rows, 1)) + row for g in range(n_store)]
        wanted = jnp.concatenate(wanted, axis=0)
        choose = jnp.where(column == wanted, 1.0, 0.0).astype(BF16)
        taken.append(dot_nt(choose, stage))
    ropes = jnp.concatenate([part[:, KVR:] for part in taken], axis=1)
    for which, part in enumerate(taken):
        out[:, :, which * KVR : (which + 1) * KVR] = (
            part[:, :KVR].astype(BF16).reshape(n_store, rows, KVR)
        )
    out[:, :, 2 * KVR :] = ropes.astype(BF16).reshape(n_store, rows, 2 * ROPE)


def pack_pages(place, owner, slot, pool_t, rows):
    n_store = owner.shape[0]
    return pl.pallas_call(
        pack_kernel,
        out_shape=jax.ShapeDtypeStruct((n_store, rows, MSG), BF16),
        in_specs=[SMEM] + [HBM] * 3,
        out_specs=VMEM,
        scratch_shapes=[
            pltpu.VMEM(owner.shape, jnp.int32),
            pltpu.VMEM(slot.shape, jnp.int32),
            pltpu.VMEM((*pool_t.shape[:2], 128), BF16),
            pltpu.SemaphoreType.DMA((6,)),
        ],
        compiler_params=params(60),
        name="pack_pages",
    )(place, owner, slot, pool_t)


def keys_kernel(place, owner, count, pages, out, seen):
    rows = pages.shape[1]
    group = place[0]
    lane = lax.broadcasted_iota(jnp.int32, (rows, 128), 1)
    for k in range(pages.shape[0]):
        seen[k] = 0
    for j in range(owner.shape[1]):
        source = owner[group, j]
        second = seen[source] > 0
        seen[source] = 1
        bias = jnp.where(j < count[group], 0.0, MASKED_SCORE)
        row = pages[source]
        at = pl.ds(j * rows, rows)
        out[at, :KVR] = jnp.where(second, row[:, KVR : 2 * KVR], row[:, :KVR])
        pair = row[:, 2 * KVR :].astype(F32)
        rot = jnp.where(second, pltpu.roll(pair, ROPE, axis=1), pair)
        last = jnp.where(lane == ROPE, bias, 0.0)
        out[at, KVR:] = jnp.where(lane < ROPE, rot, last).astype(BF16)


def build_keys(place, owner, count, pages):
    n_keys = owner.shape[1] * pages.shape[1]
    return pl.pallas_call(
        keys_kernel,
        out_shape=jax.ShapeDtypeStruct((n_keys, WIDE), BF16),
        in_specs=[SMEM, SMEM, SMEM, VMEM],
        out_specs=VMEM,
        scratch_shapes=[pltpu.SMEM((pages.shape[0],), jnp.int32)],
        compiler_params=params(24),
        name="build_keys",
    )(place, owner, count, pages)


def rotation_table(n_rows):
    half = ROPE // 2
    freq = np.float32(ROTARY_BASE) ** (-(np.arange(half, dtype=np.float32) / np.float32(half)))
    angle = np.arange(n_rows, dtype=np.float32)[:, None] * freq.astype(np.float32)[None, :]
    angle = angle.astype(np.float64)
    parts = [np.cos(angle), np.cos(angle), -np.sin(angle), np.sin(angle)]
    return np.concatenate(parts, axis=1).astype(np.float32)


def project_kernel(
    place, count, tokens_src, gain, table, w_query_src, query, normed, turns, tokens, w_query, total, sems
):
    rows = tokens.shape[0]
    start = pl.multiple_of(count[place[0]] * PAGE + place[2] * rows, rows)
    pairs = [(tokens_src, tokens), (table.at[pl.ds(start, rows), :], turns)]
    pieces = 8
    depth = w_query.shape[0] // pieces
    for k in range(pieces):
        at = pl.ds(k * depth, depth)
        pairs.append((w_query_src.at[at, :], w_query.at[at, :]))
    copies = [
        pltpu.make_async_copy(src, dst, sems.at[i]) for i, (src, dst) in enumerate(pairs)
    ]
    for copy in copies:
        copy.start()
    copies[0].wait()
    normed[...] = rms(tokens[...].astype(F32), gain[...].astype(F32).reshape(1, -1)).astype(BF16)
    copies[1].wait()
    cosine, sine = turns[:, :ROPE], turns[:, ROPE:]
    cosine = jnp.concatenate([cosine, cosine], axis=1)
    sine = jnp.concatenate([sine, sine], axis=1)
    for k in range(0, pieces, 2):
        copies[2 + k].wait()
        copies[3 + k].wait()
        at = slice(k * depth, (k + 2) * depth)
        part = dot(normed[:, at], w_query[at, :])
        total[...] = part if k == 0 else total[...] + part
    head = NOPE + ROPE
    for at in range(0, query.shape[1], 2 * head):
        part = total[:, at : at + 2 * head].astype(BF16).astype(F32)
        query[:, at : at + NOPE] = part[:, :NOPE].astype(BF16)
        query[:, at + NOPE : at + 2 * NOPE] = part[:, head : head + NOPE].astype(BF16)
        pair = jnp.concatenate([part[:, NOPE:head], part[:, head + NOPE :]], axis=1)
        query[:, at + 2 * NOPE : at + 2 * head] = (turn(pair, cosine, sine) * SCALE).astype(BF16)


def project(place, count, tokens, gain, table, w_query):
    rows, width = tokens.shape
    cols = w_query.shape[1]
    return pl.pallas_call(
        project_kernel,
        out_shape=[
            jax.ShapeDtypeStruct((rows, cols), BF16),
            jax.ShapeDtypeStruct(tokens.shape, BF16),
            jax.ShapeDtypeStruct((rows, 2 * ROPE), F32),
        ],
        in_specs=[SMEM] * 2 + [HBM, VMEM] + [HBM] * 2,
        out_specs=[VMEM] * 3,
        scratch_shapes=[
            pltpu.VMEM(tokens.shape, BF16),
            pltpu.VMEM(w_query.shape, BF16),
            pltpu.VMEM((rows, cols), F32),
            pltpu.SemaphoreType.DMA((10,)),
        ],
        compiler_params=params(60),
        name="project",
    )(place, count, tokens, gain, table, w_query)


def latent_kernel(normed, turns, w_latent_t, kv_gain, new_latent, span):
    cosine, sine = turns[:, :ROPE], turns[:, ROPE:]
    cosine = jnp.concatenate([cosine, cosine], axis=1)
    sine = jnp.concatenate([sine, sine], axis=1)
    raw = dot_nt(normed[...], w_latent_t[...])
    latent = rms(raw[:, :KVR], kv_gain[...].astype(F32).reshape(1, -1)).astype(BF16)
    pair = jnp.concatenate([raw[:, KVR:], raw[:, KVR:]], axis=1)
    turned = turn(pair, cosine, sine)
    new_latent[:KVR, :] = latent.astype(F32).T.astype(BF16)
    new_latent[KVR:, :] = turned.T[:ROPE].astype(BF16)
    lane = lax.broadcasted_iota(jnp.int32, turned.shape, 1)
    span[:, :KVR] = latent
    span[:, KVR:] = jnp.where(lane < ROPE, turned, 0.0).astype(BF16)


def project_latent(normed, turns, w_latent_t, kv_gain):
    rows = normed.shape[0]
    return pl.pallas_call(
        latent_kernel,
        out_shape=[
            jax.ShapeDtypeStruct((LAT, rows), BF16),
            jax.ShapeDtypeStruct((rows, WIDE), BF16),
        ],
        in_specs=[VMEM] * 4,
        out_specs=[VMEM] * 2,
        compiler_params=params(16),
        name="project_latent",
    )(normed, turns, w_latent_t, kv_gain)


def attend_kernel(by, n_section, place, query, key_up, value_up, near, *refs):
    n_head, rows = key_up.shape[0], query.shape[0]
    if len(refs) == 5:
        far, span, out, keys, probes = refs
        keys[: near.shape[0], :] = near[...]
        keys[near.shape[0] :, :] = far[...]
    else:
        keys = near
        span, out, probes = refs
    blocks = (keys, span)
    lane = lax.broadcasted_iota(jnp.int32, (rows, 128), 1)
    head_pair = 2 * (NOPE + ROPE)
    at_once = 2
    tile = at_once * rows
    steps = n_head // at_once
    width = n_head * NOPE
    for h in range(n_head):
        at = pl.ds(h * rows, rows)
        base = (h // 2) * head_pair
        nope = query[:, base + (h % 2) * NOPE : base + (h % 2 + 1) * NOPE]
        probes[at, :KVR] = (dot_nt(nope, key_up[h]) * SCALE).astype(BF16)
        pair = query[:, base + 2 * NOPE : base + head_pair].astype(F32)
        if h % 2 == 1:
            pair = pltpu.roll(pair, ROPE, axis=1)
        one = jnp.where(lane == ROPE, 1.0, 0.0)
        probes[at, KVR:] = jnp.where(lane < ROPE, pair, one).astype(BF16)

    if by == 0:
        row_of = lax.broadcasted_iota(jnp.int32, (tile, rows), 0) & (rows - 1)
        key_of = lax.broadcasted_iota(jnp.int32, (tile, rows), 1)
        hide = jnp.where(key_of <= row_of, 0.0, MASKED_SCORE)
    else:
        hide = jnp.where(place[2] + by < n_section, 0.0, MASKED_SCORE)

    def score(i):
        probe = probes[i * tile : (i + 1) * tile, :]
        parts = [dot_nt(probe, block[...]) for block in blocks]
        parts[1] = parts[1] + hide
        return parts

    def finish(i, parts, stats):
        tops = [jnp.max(part, axis=1, keepdims=True) for part in parts]
        top = functools.reduce(jnp.maximum, tops)
        total, summed = 0.0, 0.0
        for part, block in zip(parts, blocks):
            weight = jnp.exp2(part - top)
            total = total + jnp.sum(weight, axis=1, keepdims=True)
            summed = summed + dot(weight.astype(BF16), block[:, :KVR])
        mixed = (summed * (1.0 / total)).astype(BF16)
        level = top + jnp.log2(total)
        for k in range(at_once):
            h = i * at_once + k
            value = dot(mixed[k * rows : (k + 1) * rows], value_up[h])
            out[:, h * VDIM : (h + 1) * VDIM] = value.astype(BF16)
            stats = jnp.where(lane == h, level[k * rows : (k + 1) * rows], stats)
        return stats

    stats = jnp.zeros((rows, 128), F32)
    parts = score(0)
    for i in range(steps):
        following = score(i + 1) if i + 1 < steps else None
        stats = finish(i, parts, stats)
        parts = following
    high = stats.astype(BF16).astype(F32)
    rest = stats - high
    mid = rest.astype(BF16).astype(F32)
    joined = high + pltpu.roll(mid, n_head, axis=1) + pltpu.roll(rest - mid, 2 * n_head, axis=1)
    out[:, width:] = joined.astype(BF16)


def attend(by, n_section, place, query, key_up, value_up, *keys):
    rows, n_head = query.shape[0], key_up.shape[0]
    out_shape = [jax.ShapeDtypeStruct((rows, n_head * VDIM + 128), BF16)]
    if len(keys) == 3:
        out_shape.append(jax.ShapeDtypeStruct((2 * keys[0].shape[0], WIDE), BF16))
    return pl.pallas_call(
        functools.partial(attend_kernel, by, n_section),
        out_shape=out_shape,
        in_specs=[SMEM] + [VMEM] * (3 + len(keys)),
        out_specs=[VMEM] * len(out_shape),
        scratch_shapes=[pltpu.VMEM((n_head * rows, WIDE), BF16)],
        compiler_params=params(28),
        name="attend_%d" % by,
    )(place, query, key_up, value_up, *keys)


def output_kernel(n_head, own, one, two, three, weight, exact, send):
    parts = (own, one, two, three)
    width = n_head * VDIM
    levels = []
    for part in parts:
        stat = part[:, width:].astype(F32)
        rest = pltpu.roll(stat, 128 - n_head, axis=1) + pltpu.roll(stat, 128 - 2 * n_head, axis=1)
        levels.append(stat + rest)
    top = functools.reduce(jnp.maximum, levels)
    shares = [jnp.exp2(level - top) for level in levels]
    total = functools.reduce(jnp.add, shares)
    head_of = lax.broadcasted_iota(jnp.int32, (128, width), 0)
    lane_of = lax.broadcasted_iota(jnp.int32, (128, width), 1)
    begin = head_of * VDIM
    spread = jnp.where((lane_of >= begin) & (lane_of < begin + VDIM), 1.0, 0.0).astype(BF16)
    mixed = 0.0
    for part, share in zip(parts, shares):
        share = share / total
        high = share.astype(BF16)
        low = (share - high.astype(F32)).astype(BF16)
        factor = dot(high, spread) + dot(low, spread)
        mixed = mixed + part[:, :width].astype(F32) * factor
    per_head = mixed.astype(BF16)
    block = 512
    for at in range(0, weight.shape[1], block):
        part = dot(per_head, weight[:, at : at + block])
        exact[:, at : at + block] = part
        send[:, at : at + block] = part.astype(BF16)


def project_output(own, one, two, three, w_out):
    rows = own.shape[0]
    depth, cols = w_out.shape
    return pl.pallas_call(
        functools.partial(output_kernel, depth // VDIM),
        out_shape=[
            jax.ShapeDtypeStruct((rows, cols), F32),
            jax.ShapeDtypeStruct((rows, cols), BF16),
        ],
        in_specs=[VMEM] * 5,
        out_specs=[VMEM] * 2,
        compiler_params=params(16),
        name="project_output",
    )(own, one, two, three, w_out)


def expert_kernel(place, tokens, exact, other, gain, w_gate_t, w_up_t, w_down, keep, send):
    half = keep.shape[1]
    middle = tokens[...].astype(F32) + (exact[...] + other[...].astype(F32))
    middle = middle.astype(BF16).astype(F32)
    mlp_in = rms(middle, gain[...].astype(F32).reshape(1, -1)).astype(BF16)
    gate = dot_nt(mlp_in, w_gate_t[...])
    up = dot_nt(mlp_in, w_up_t[...])
    hidden = (gate / (1.0 + jnp.exp(-gate)) * up).astype(BF16)
    low = dot(hidden, w_down[:, :half])
    high = dot(hidden, w_down[:, half:])
    first = place[3] == 0
    keep[...] = jnp.where(first, middle[:, :half] + low, middle[:, half:] + high)
    send[...] = jnp.where(first, high, low).astype(BF16)


def expert(place, tokens, exact, other, gain, w_gate_t, w_up_t, w_down):
    rows, width = tokens.shape
    half = width // 2
    return pl.pallas_call(
        expert_kernel,
        out_shape=[
            jax.ShapeDtypeStruct((rows, half), F32),
            jax.ShapeDtypeStruct((rows, half), BF16),
        ],
        in_specs=[SMEM] + [VMEM] * 7,
        out_specs=[VMEM] * 2,
        compiler_params=params(24),
        name="expert",
    )(place, tokens, exact, other, gain, w_gate_t, w_up_t, w_down)


def on_device(
    tokens,
    attn_gain,
    w_query,
    w_latent,
    kv_gain,
    w_key_up,
    w_value_up,
    w_out,
    mlp_gain,
    w_gate,
    w_up,
    w_down,
    page_pool,
    hit_owner,
    hit_slot,
    fetch_count,
):
    n_store = lax.axis_size("store")
    n_section = lax.axis_size("section")
    n_tp = lax.axis_size("tp")
    group = lax.axis_index("store")
    section = lax.axis_index("section")
    core = lax.axis_index("tp")
    rows = tokens.shape[0]
    share = PAGE // (n_section * n_tp)

    swap = [(0, 1), (1, 0)]
    place = jnp.stack([group, section * n_tp + core, section, core]).astype(jnp.int32)
    owner = hit_owner[:, :, 0]
    outgoing = pack_pages(place, owner, hit_slot, jnp.swapaxes(page_pool, 1, 2), share)
    outgoing, early_tokens = lax.optimization_barrier((outgoing, tokens))
    outgoing = outgoing.reshape(n_store, 2, share // 2, MSG)
    arrived = lax.all_to_all(outgoing, "store", split_axis=0, concat_axis=0, tiled=True)
    arrived = arrived.reshape(n_store, share, MSG)

    def shift(value, by):
        pairs = [((z + by) % n_section, z) for z in range(n_section)]
        return lax.ppermute(value, "section", pairs)

    table = rotation_table((hit_owner.shape[1]) * PAGE + n_section * rows)
    query, normed, turns = project(
        place, fetch_count, early_tokens, attn_gain, jnp.asarray(table), w_query
    )
    next_query, last_query = shift(query, 1), shift(query, -1)
    new_latent, span = project_latent(normed, turns, w_latent.T, kv_gain)
    arrived, next_query, last_query, span = lax.optimization_barrier(
        (arrived, next_query, last_query, span)
    )
    cut = rows // 2
    far_low, far_high = shift(next_query[:cut], 1), shift(last_query[cut:], -1)

    near = build_keys(place, owner, fetch_count, arrived)
    far = lax.ppermute(near, "tp", swap)

    def partial_for(by, query, *keys):
        return attend(by, n_section, place, query, w_key_up, w_value_up, *keys, span)

    one, keys = partial_for(1, next_query, near, far)
    one, far_low, far_high = lax.optimization_barrier((one, far_low, far_high))
    one = shift(one, -1)
    (two,) = partial_for(2, jnp.concatenate([far_low, far_high], axis=0), keys)
    two, last_query, one = lax.optimization_barrier((two, last_query, one))
    two = shift(two, -1)
    (three,) = partial_for(3, last_query, keys)
    three, query, two = lax.optimization_barrier((three, query, two))
    three = shift(three, -3)
    two = shift(two, -1)
    (own,) = partial_for(0, query, keys)
    exact, send = project_output(own, one, two, three, w_out)
    incoming = lax.ppermute(send, "tp", swap)
    keep, send = expert(
        place,
        tokens,
        exact,
        incoming,
        mlp_gain,
        w_gate.T,
        w_up.T,
        w_down,
    )
    layer_out = (keep + lax.ppermute(send, "tp", swap).astype(F32)).astype(BF16)
    return (layer_out, new_latent.T)


def solution(mesh):
    in_specs = (
        P(("store", "section"), None),
        P(),
        P(None, "tp"),
        P(),
        P(),
        P("tp", None, None),
        P("tp", None, None),
        P("tp", None),
        P(),
        P(None, "tp"),
        P(None, "tp"),
        P("tp", None),
        P("store", None, None),
        P(),
        P(),
        P(),
    )
    out_specs = (P(("store", "section"), "tp"), P(("store", "section"), None))
    return jax.shard_map(
        on_device, mesh=mesh, in_specs=in_specs, out_specs=out_specs, check_vma=False
    )
```

```python
import functools
import math

import jax
import jax.numpy as jnp
import numpy as np
from jax import lax
from jax.experimental import pallas as pl
from jax.experimental.pallas import tpu as pltpu
from jax.sharding import PartitionSpec as P

NOPE = 128
ROPE = 64
KVR = 512
PAGE = 256
LAT = KVR + ROPE
WIDE = KVR + 2 * ROPE
MSG = 2 * LAT
VDIM = 128
EPSILON = 1e-06
ROTARY_BASE = 10000.0
MASKED_SCORE = -1e30
SCALE = (NOPE + ROPE) ** (-0.5) / math.log(2.0)
F32 = jnp.float32
BF16 = jnp.bfloat16
MB = 1024 * 1024

VMEM = pl.BlockSpec(memory_space=pltpu.VMEM)
SMEM = pl.BlockSpec(memory_space=pltpu.SMEM)
HBM = pl.BlockSpec(memory_space=pltpu.HBM)


def params(mb):
    return pltpu.CompilerParams(vmem_limit_bytes=mb * MB)


def dot(a, b):
    return jnp.dot(a, b, preferred_element_type=F32)


def dot_nt(a, b):
    return lax.dot_general(a, b, (((1,), (1,)), ((), ())), preferred_element_type=F32)


def rms(values, gain):
    mean_sq = jnp.mean(values * values, axis=-1, keepdims=True)
    return values * lax.rsqrt(mean_sq + EPSILON) * gain


def turn(values, cosine, sine):
    lane = lax.broadcasted_iota(jnp.int32, values.shape, 1)
    low = (lane & (ROPE // 2)) == 0
    partner = jnp.where(
        low, pltpu.roll(values, 128 - ROPE // 2, axis=1), pltpu.roll(values, ROPE // 2, axis=1)
    )
    return values * cosine + partner * sine


def pack_kernel(
    place, owner_src, slot_src, pool_src, out, owner, slot, pool, sems
):
    n_pages, width, window = pool.shape
    n_store, rows, _ = out.shape
    per = window // rows
    pairs = [(owner_src, owner), (slot_src, slot)]
    part = pl.ds(pl.multiple_of((place[1] // per) * window, window), window)
    strip = n_pages // 4
    for k in range(4):
        at = pl.ds(k * strip, strip)
        pairs.append((pool_src.at[at, :, part], pool.at[at]))
    copies = [
        pltpu.make_async_copy(src, dst, sems.at[i]) for i, (src, dst) in enumerate(pairs)
    ]
    for copy in copies:
        copy.start()
    for copy in copies:
        copy.wait()
    first = (place[1] % per) * rows
    lane = lax.broadcasted_iota(jnp.int32, (width, window), 1)
    joined = []
    for at in range(0, n_pages, per):
        part = None
        for k in range(per):
            moved = pltpu.roll(pool[at + k].astype(F32), (k * rows - first + window) % window, axis=1)
            part = moved if part is None else jnp.where(lane >= k * rows, moved, part)
        joined.append(part.astype(BF16))
    stage = jnp.concatenate(joined, axis=1)
    total = n_store * rows
    n_list = owner.shape[1]
    held = owner[...] == place[0]
    entry = lax.broadcasted_iota(jnp.int32, held.shape, 1)
    low = jnp.min(jnp.where(held, entry, n_list), axis=1, keepdims=True)
    high = jnp.max(jnp.where(held, entry, -1), axis=1, keepdims=True)
    row = lax.broadcasted_iota(jnp.int32, (rows, 1), 0)
    column = lax.broadcasted_iota(jnp.int32, (total, n_pages * rows), 1)
    taken = []
    for which in (low, high):
        page = jnp.sum(jnp.where(entry == which, slot[...], 0), axis=1, keepdims=True) * rows
        wanted = [jnp.broadcast_to(page[g : g + 1], (rows, 1)) + row for g in range(n_store)]
        wanted = jnp.concatenate(wanted, axis=0)
        choose = jnp.where(column == wanted, 1.0, 0.0).astype(BF16)
        taken.append(dot_nt(choose, stage))
    ropes = jnp.concatenate([part[:, KVR:] for part in taken], axis=1)
    for which, part in enumerate(taken):
        out[:, :, which * KVR : (which + 1) * KVR] = (
            part[:, :KVR].astype(BF16).reshape(n_store, rows, KVR)
        )
    out[:, :, 2 * KVR :] = ropes.astype(BF16).reshape(n_store, rows, 2 * ROPE)


def pack_pages(place, owner, slot, pool_t, rows):
    n_store = owner.shape[0]
    return pl.pallas_call(
        pack_kernel,
        out_shape=jax.ShapeDtypeStruct((n_store, rows, MSG), BF16),
        in_specs=[SMEM] + [HBM] * 3,
        out_specs=VMEM,
        scratch_shapes=[
            pltpu.VMEM(owner.shape, jnp.int32),
            pltpu.VMEM(slot.shape, jnp.int32),
            pltpu.VMEM((*pool_t.shape[:2], 128), BF16),
            pltpu.SemaphoreType.DMA((6,)),
        ],
        compiler_params=params(60),
        name="pack_pages",
    )(place, owner, slot, pool_t)


def keys_kernel(place, owner, count, pages, out, seen):
    rows = pages.shape[1]
    group = place[0]
    lane = lax.broadcasted_iota(jnp.int32, (rows, 128), 1)
    for k in range(pages.shape[0]):
        seen[k] = 0
    for j in range(owner.shape[1]):
        source = owner[group, j]
        second = seen[source] > 0
        seen[source] = 1
        bias = jnp.where(j < count[group], 0.0, MASKED_SCORE)
        row = pages[source]
        at = pl.ds(j * rows, rows)
        out[at, :KVR] = jnp.where(second, row[:, KVR : 2 * KVR], row[:, :KVR])
        pair = row[:, 2 * KVR :].astype(F32)
        rot = jnp.where(second, pltpu.roll(pair, ROPE, axis=1), pair)
        last = jnp.where(lane == ROPE, bias, 0.0)
        out[at, KVR:] = jnp.where(lane < ROPE, rot, last).astype(BF16)


def build_keys(place, owner, count, pages):
    n_keys = owner.shape[1] * pages.shape[1]
    return pl.pallas_call(
        keys_kernel,
        out_shape=jax.ShapeDtypeStruct((n_keys, WIDE), BF16),
        in_specs=[SMEM, SMEM, SMEM, VMEM],
        out_specs=VMEM,
        scratch_shapes=[pltpu.SMEM((pages.shape[0],), jnp.int32)],
        compiler_params=params(24),
        name="build_keys",
    )(place, owner, count, pages)


def rotation_table(n_rows):
    half = ROPE // 2
    freq = np.float32(ROTARY_BASE) ** (-(np.arange(half, dtype=np.float32) / np.float32(half)))
    angle = np.arange(n_rows, dtype=np.float32)[:, None] * freq.astype(np.float32)[None, :]
    angle = angle.astype(np.float64)
    parts = [np.cos(angle), np.cos(angle), -np.sin(angle), np.sin(angle)]
    return np.concatenate(parts, axis=1).astype(np.float32)


def project_kernel(
    place, count, tokens_src, gain, table, w_query_src, query, normed, turns, tokens, w_query, total, sems
):
    rows = tokens.shape[0]
    start = pl.multiple_of(count[place[0]] * PAGE + place[2] * rows, rows)
    pairs = [(tokens_src, tokens), (table.at[pl.ds(start, rows), :], turns)]
    pieces = 8
    depth = w_query.shape[0] // pieces
    for k in range(pieces):
        at = pl.ds(k * depth, depth)
        pairs.append((w_query_src.at[at, :], w_query.at[at, :]))
    copies = [
        pltpu.make_async_copy(src, dst, sems.at[i]) for i, (src, dst) in enumerate(pairs)
    ]
    for copy in copies:
        copy.start()
    copies[0].wait()
    normed[...] = rms(tokens[...].astype(F32), gain[...].astype(F32).reshape(1, -1)).astype(BF16)
    copies[1].wait()
    cosine, sine = turns[:, :ROPE], turns[:, ROPE:]
    cosine = jnp.concatenate([cosine, cosine], axis=1)
    sine = jnp.concatenate([sine, sine], axis=1)
    for k in range(0, pieces, 2):
        copies[2 + k].wait()
        copies[3 + k].wait()
        at = slice(k * depth, (k + 2) * depth)
        part = dot(normed[:, at], w_query[at, :])
        total[...] = part if k == 0 else total[...] + part
    head = NOPE + ROPE
    for at in range(0, query.shape[1], 2 * head):
        part = total[:, at : at + 2 * head].astype(BF16).astype(F32)
        query[:, at : at + NOPE] = part[:, :NOPE].astype(BF16)
        query[:, at + NOPE : at + 2 * NOPE] = part[:, head : head + NOPE].astype(BF16)
        pair = jnp.concatenate([part[:, NOPE:head], part[:, head + NOPE :]], axis=1)
        query[:, at + 2 * NOPE : at + 2 * head] = (turn(pair, cosine, sine) * SCALE).astype(BF16)


def project(place, count, tokens, gain, table, w_query):
    rows, width = tokens.shape
    cols = w_query.shape[1]
    return pl.pallas_call(
        project_kernel,
        out_shape=[
            jax.ShapeDtypeStruct((rows, cols), BF16),
            jax.ShapeDtypeStruct(tokens.shape, BF16),
            jax.ShapeDtypeStruct((rows, 2 * ROPE), F32),
        ],
        in_specs=[SMEM] * 2 + [HBM, VMEM] + [HBM] * 2,
        out_specs=[VMEM] * 3,
        scratch_shapes=[
            pltpu.VMEM(tokens.shape, BF16),
            pltpu.VMEM(w_query.shape, BF16),
            pltpu.VMEM((rows, cols), F32),
            pltpu.SemaphoreType.DMA((10,)),
        ],
        compiler_params=params(60),
        name="project",
    )(place, count, tokens, gain, table, w_query)


def latent_kernel(normed, turns, w_latent_t, kv_gain, new_latent, span):
    cosine, sine = turns[:, :ROPE], turns[:, ROPE:]
    cosine = jnp.concatenate([cosine, cosine], axis=1)
    sine = jnp.concatenate([sine, sine], axis=1)
    raw = dot_nt(normed[...], w_latent_t[...])
    latent = rms(raw[:, :KVR], kv_gain[...].astype(F32).reshape(1, -1)).astype(BF16)
    pair = jnp.concatenate([raw[:, KVR:], raw[:, KVR:]], axis=1)
    turned = turn(pair, cosine, sine)
    new_latent[:KVR, :] = latent.astype(F32).T.astype(BF16)
    new_latent[KVR:, :] = turned.T[:ROPE].astype(BF16)
    lane = lax.broadcasted_iota(jnp.int32, turned.shape, 1)
    span[:, :KVR] = latent
    span[:, KVR:] = jnp.where(lane < ROPE, turned, 0.0).astype(BF16)


def project_latent(normed, turns, w_latent_t, kv_gain):
    rows = normed.shape[0]
    return pl.pallas_call(
        latent_kernel,
        out_shape=[
            jax.ShapeDtypeStruct((LAT, rows), BF16),
            jax.ShapeDtypeStruct((rows, WIDE), BF16),
        ],
        in_specs=[VMEM] * 4,
        out_specs=[VMEM] * 2,
        compiler_params=params(16),
        name="project_latent",
    )(normed, turns, w_latent_t, kv_gain)


def attend_kernel(by, n_section, place, query, key_up, value_up, near, *refs):
    n_head, rows = key_up.shape[0], query.shape[0]
    if len(refs) == 5:
        arrived, span, out, far, probes = refs
        far[...] = arrived[...]
    else:
        far, span, out, probes = refs
    blocks = (near, far, span)
    lane = lax.broadcasted_iota(jnp.int32, (rows, 128), 1)
    head_pair = 2 * (NOPE + ROPE)
    at_once = 2
    tile = at_once * rows
    steps = n_head // at_once
    width = n_head * NOPE
    for h in range(n_head):
        at = pl.ds(h * rows, rows)
        base = (h // 2) * head_pair
        nope = query[:, base + (h % 2) * NOPE : base + (h % 2 + 1) * NOPE]
        probes[at, :KVR] = (dot_nt(nope, key_up[h]) * SCALE).astype(BF16)
        pair = query[:, base + 2 * NOPE : base + head_pair].astype(F32)
        if h % 2 == 1:
            pair = pltpu.roll(pair, ROPE, axis=1)
        one = jnp.where(lane == ROPE, 1.0, 0.0)
        probes[at, KVR:] = jnp.where(lane < ROPE, pair, one).astype(BF16)

    if by == 0:
        row_of = lax.broadcasted_iota(jnp.int32, (tile, rows), 0) & (rows - 1)
        key_of = lax.broadcasted_iota(jnp.int32, (tile, rows), 1)
        hide = jnp.where(key_of <= row_of, 0.0, MASKED_SCORE)
    else:
        hide = jnp.where(place[2] + by < n_section, 0.0, MASKED_SCORE)

    pieces, closing = [], []
    for block in blocks:
        step = min(256, block.shape[0])
        for at in range(0, block.shape[0], step):
            pieces.append((block, at, step))
            closing.append(at + step == block.shape[0])

    def lanes(value):
        return [value[:, at : at + 128] for at in range(0, value.shape[1], 128)]

    def score(i, p, peak):
        block, at, step = pieces[p]
        value = dot_nt(probes[i * tile : (i + 1) * tile, :], block[at : at + step, :])
        if block is span:
            value = value + hide
        return value, functools.reduce(jnp.maximum, lanes(value), peak)

    def finish(i, total, summed, stats, top):
        total = jnp.sum(total, axis=1, keepdims=True)
        mixed = (summed * (1.0 / total)).astype(BF16)
        level = top + jnp.log2(total)
        for k in range(at_once):
            h = i * at_once + k
            value = dot(mixed[k * rows : (k + 1) * rows], value_up[h])
            out[:, h * VDIM : (h + 1) * VDIM] = value.astype(BF16)
            stats = jnp.where(lane == h, level[k * rows : (k + 1) * rows], stats)
        return stats

    stats = jnp.zeros((rows, 128), F32)
    lowest = jnp.full((tile, 128), MASKED_SCORE, F32)
    ready, peak = [], lowest
    for p in range(len(pieces)):
        value, peak = score(0, p, peak)
        ready.append(value)
    for i in range(steps):
        top = jnp.max(peak, axis=1, keepdims=True)
        shift = jnp.broadcast_to(top, (tile, 128))
        total, summed = jnp.zeros((tile, 128), F32), 0.0
        coming, peak, weights = [], lowest, []
        for p in range(len(pieces)):
            if i + 1 < steps:
                value, peak = score(i + 1, p, peak)
                coming.append(value)
            for part in lanes(ready[p]):
                weight = jnp.exp2(part - shift)
                total = total + weight
                weights.append(weight.astype(BF16))
            if closing[p]:
                summed = summed + dot(jnp.concatenate(weights, axis=1), pieces[p][0][:, :KVR])
                weights = []
        stats = finish(i, total, summed, stats, top)
        ready = coming
    high = stats.astype(BF16).astype(F32)
    rest = stats - high
    mid = rest.astype(BF16).astype(F32)
    joined = high + pltpu.roll(mid, n_head, axis=1) + pltpu.roll(rest - mid, 2 * n_head, axis=1)
    out[:, width:] = joined.astype(BF16)


def attend(by, n_section, place, query, key_up, value_up, near, far, span, keep_far=False):
    rows, n_head = query.shape[0], key_up.shape[0]
    out_shape = [jax.ShapeDtypeStruct((rows, n_head * VDIM + 128), BF16)]
    if keep_far:
        out_shape.append(jax.ShapeDtypeStruct(far.shape, BF16))
    return pl.pallas_call(
        functools.partial(attend_kernel, by, n_section),
        out_shape=out_shape,
        in_specs=[SMEM] + [VMEM] * 6,
        out_specs=[VMEM] * len(out_shape),
        scratch_shapes=[pltpu.VMEM((n_head * rows, WIDE), BF16)],
        compiler_params=params(28),
        name="attend_%d" % by,
    )(place, query, key_up, value_up, near, far, span)


def output_kernel(n_head, own, one, two, three, weight, exact, send):
    parts = (own, one, two, three)
    width = n_head * VDIM
    levels = []
    for part in parts:
        stat = part[:, width:].astype(F32)
        rest = pltpu.roll(stat, 128 - n_head, axis=1) + pltpu.roll(stat, 128 - 2 * n_head, axis=1)
        levels.append(stat + rest)
    top = functools.reduce(jnp.maximum, levels)
    shares = [jnp.exp2(level - top) for level in levels]
    total = functools.reduce(jnp.add, shares)
    head_of = lax.broadcasted_iota(jnp.int32, (128, width), 0)
    lane_of = lax.broadcasted_iota(jnp.int32, (128, width), 1)
    begin = head_of * VDIM
    spread = jnp.where((lane_of >= begin) & (lane_of < begin + VDIM), 1.0, 0.0).astype(BF16)
    mixed = 0.0
    for part, share in zip(parts, shares):
        share = share / total
        high = share.astype(BF16)
        low = (share - high.astype(F32)).astype(BF16)
        factor = dot(high, spread) + dot(low, spread)
        mixed = mixed + part[:, :width].astype(F32) * factor
    per_head = mixed.astype(BF16)
    block = 512
    for at in range(0, weight.shape[1], block):
        part = dot(per_head, weight[:, at : at + block])
        exact[:, at : at + block] = part
        send[:, at : at + block] = part.astype(BF16)


def project_output(own, one, two, three, w_out):
    rows = own.shape[0]
    depth, cols = w_out.shape
    return pl.pallas_call(
        functools.partial(output_kernel, depth // VDIM),
        out_shape=[
            jax.ShapeDtypeStruct((rows, cols), F32),
            jax.ShapeDtypeStruct((rows, cols), BF16),
        ],
        in_specs=[VMEM] * 5,
        out_specs=[VMEM] * 2,
        compiler_params=params(16),
        name="project_output",
    )(own, one, two, three, w_out)


def expert_kernel(place, tokens, exact, other, gain, w_gate_t, w_up_t, w_down, keep, send):
    half = keep.shape[1]
    middle = tokens[...].astype(F32) + (exact[...] + other[...].astype(F32))
    middle = middle.astype(BF16).astype(F32)
    mlp_in = rms(middle, gain[...].astype(F32).reshape(1, -1)).astype(BF16)
    gate = dot_nt(mlp_in, w_gate_t[...])
    up = dot_nt(mlp_in, w_up_t[...])
    hidden = (gate / (1.0 + jnp.exp(-gate)) * up).astype(BF16)
    low = dot(hidden, w_down[:, :half])
    high = dot(hidden, w_down[:, half:])
    first = place[3] == 0
    keep[...] = jnp.where(first, middle[:, :half] + low, middle[:, half:] + high)
    send[...] = jnp.where(first, high, low).astype(BF16)


def expert(place, tokens, exact, other, gain, w_gate_t, w_up_t, w_down):
    rows, width = tokens.shape
    half = width // 2
    return pl.pallas_call(
        expert_kernel,
        out_shape=[
            jax.ShapeDtypeStruct((rows, half), F32),
            jax.ShapeDtypeStruct((rows, half), BF16),
        ],
        in_specs=[SMEM] + [VMEM] * 7,
        out_specs=[VMEM] * 2,
        compiler_params=params(24),
        name="expert",
    )(place, tokens, exact, other, gain, w_gate_t, w_up_t, w_down)


def on_device(
    tokens,
    attn_gain,
    w_query,
    w_latent,
    kv_gain,
    w_key_up,
    w_value_up,
    w_out,
    mlp_gain,
    w_gate,
    w_up,
    w_down,
    page_pool,
    hit_owner,
    hit_slot,
    fetch_count,
):
    n_store = lax.axis_size("store")
    n_section = lax.axis_size("section")
    n_tp = lax.axis_size("tp")
    group = lax.axis_index("store")
    section = lax.axis_index("section")
    core = lax.axis_index("tp")
    rows = tokens.shape[0]
    share = PAGE // (n_section * n_tp)

    swap = [(0, 1), (1, 0)]
    place = jnp.stack([group, section * n_tp + core, section, core]).astype(jnp.int32)
    owner = hit_owner[:, :, 0]
    outgoing = pack_pages(place, owner, hit_slot, jnp.swapaxes(page_pool, 1, 2), share)
    outgoing, early_tokens = lax.optimization_barrier((outgoing, tokens))
    outgoing = outgoing.reshape(n_store, 2, share // 2, MSG)
    arrived = lax.all_to_all(outgoing, "store", split_axis=0, concat_axis=0, tiled=True)
    arrived = arrived.reshape(n_store, share, MSG)

    def shift(value, by):
        pairs = [((z + by) % n_section, z) for z in range(n_section)]
        return lax.ppermute(value, "section", pairs)

    table = rotation_table((hit_owner.shape[1]) * PAGE + n_section * rows)
    query, normed, turns = project(
        place, fetch_count, early_tokens, attn_gain, jnp.asarray(table), w_query
    )
    next_query, last_query = shift(query, 1), shift(query, -1)
    new_latent, span = project_latent(normed, turns, w_latent.T, kv_gain)
    arrived, next_query, last_query, span = lax.optimization_barrier(
        (arrived, next_query, last_query, span)
    )
    far_query = shift(next_query, 1)

    near = build_keys(place, owner, fetch_count, arrived)
    far = lax.ppermute(near, "tp", swap)

    def partial_for(by, query, far, **flags):
        return attend(by, n_section, place, query, w_key_up, w_value_up, near, far, span, **flags)

    one, far = partial_for(1, next_query, far, keep_far=True)
    one, far_query = lax.optimization_barrier((one, far_query))
    one = shift(one, -1)
    (two,) = partial_for(2, far_query, far)
    two, last_query, one = lax.optimization_barrier((two, last_query, one))
    two = shift(two, -1)
    (three,) = partial_for(3, last_query, far)
    three, query, two = lax.optimization_barrier((three, query, two))
    three = shift(three, -3)
    two = shift(two, -1)
    (own,) = partial_for(0, query, far)
    exact, send = project_output(own, one, two, three, w_out)
    incoming = lax.ppermute(send, "tp", swap)
    keep, send = expert(
        place,
        tokens,
        exact,
        incoming,
        mlp_gain,
        w_gate.T,
        w_up.T,
        w_down,
    )
    layer_out = (keep + lax.ppermute(send, "tp", swap).astype(F32)).astype(BF16)
    return (layer_out, new_latent.T)


def solution(mesh):
    in_specs = (
        P(("store", "section"), None),
        P(),
        P(None, "tp"),
        P(),
        P(),
        P("tp", None, None),
        P("tp", None, None),
        P("tp", None),
        P(),
        P(None, "tp"),
        P(None, "tp"),
        P("tp", None),
        P("store", None, None),
        P(),
        P(),
        P(),
    )
    out_specs = (P(("store", "section"), "tp"), P(("store", "section"), None))
    return jax.shard_map(
        on_device, mesh=mesh, in_specs=in_specs, out_specs=out_specs, check_vma=False
    )
```

```python
import functools
import math

import jax
import jax.numpy as jnp
import numpy as np
from jax import lax
from jax.experimental import pallas as pl
from jax.experimental.pallas import tpu as pltpu
from jax.sharding import PartitionSpec as P

NOPE = 128
ROPE = 64
KVR = 512
PAGE = 256
LAT = KVR + ROPE
WIDE = KVR + 2 * ROPE
MSG = 2 * LAT
VDIM = 128
EPSILON = 1e-06
ROTARY_BASE = 10000.0
MASKED_SCORE = -1e30
SCALE = (NOPE + ROPE) ** (-0.5) / math.log(2.0)
F32 = jnp.float32
BF16 = jnp.bfloat16
MB = 1024 * 1024

VMEM = pl.BlockSpec(memory_space=pltpu.VMEM)
SMEM = pl.BlockSpec(memory_space=pltpu.SMEM)
HBM = pl.BlockSpec(memory_space=pltpu.HBM)


def params(mb):
    return pltpu.CompilerParams(vmem_limit_bytes=mb * MB)


def dot(a, b):
    return jnp.dot(a, b, preferred_element_type=F32)


def dot_nt(a, b):
    return lax.dot_general(a, b, (((1,), (1,)), ((), ())), preferred_element_type=F32)


def rms(values, gain):
    mean_sq = jnp.mean(values * values, axis=-1, keepdims=True)
    return values * lax.rsqrt(mean_sq + EPSILON) * gain


def turn(values, cosine, sine):
    lane = lax.broadcasted_iota(jnp.int32, values.shape, 1)
    low = (lane & (ROPE // 2)) == 0
    partner = jnp.where(
        low, pltpu.roll(values, 128 - ROPE // 2, axis=1), pltpu.roll(values, ROPE // 2, axis=1)
    )
    return values * cosine + partner * sine


def pack_kernel(
    place, owner_src, slot_src, pool_src, out, owner, slot, pool, sems
):
    n_pages, width, window = pool.shape
    n_store, rows, _ = out.shape
    per = window // rows
    pairs = [(owner_src, owner), (slot_src, slot)]
    part = pl.ds(pl.multiple_of((place[1] // per) * window, window), window)
    strip = n_pages // 4
    for k in range(4):
        at = pl.ds(k * strip, strip)
        pairs.append((pool_src.at[at, :, part], pool.at[at]))
    copies = [
        pltpu.make_async_copy(src, dst, sems.at[i]) for i, (src, dst) in enumerate(pairs)
    ]
    for copy in copies:
        copy.start()
    for copy in copies:
        copy.wait()
    first = (place[1] % per) * rows
    lane = lax.broadcasted_iota(jnp.int32, (width, window), 1)
    joined = []
    for at in range(0, n_pages, per):
        part = None
        for k in range(per):
            moved = pltpu.roll(pool[at + k].astype(F32), (k * rows - first + window) % window, axis=1)
            part = moved if part is None else jnp.where(lane >= k * rows, moved, part)
        joined.append(part.astype(BF16))
    stage = jnp.concatenate(joined, axis=1)
    total = n_store * rows
    n_list = owner.shape[1]
    held = owner[...] == place[0]
    entry = lax.broadcasted_iota(jnp.int32, held.shape, 1)
    low = jnp.min(jnp.where(held, entry, n_list), axis=1, keepdims=True)
    high = jnp.max(jnp.where(held, entry, -1), axis=1, keepdims=True)
    row = lax.broadcasted_iota(jnp.int32, (rows, 1), 0)
    column = lax.broadcasted_iota(jnp.int32, (total, n_pages * rows), 1)
    taken = []
    for which in (low, high):
        page = jnp.sum(jnp.where(entry == which, slot[...], 0), axis=1, keepdims=True) * rows
        wanted = [jnp.broadcast_to(page[g : g + 1], (rows, 1)) + row for g in range(n_store)]
        wanted = jnp.concatenate(wanted, axis=0)
        choose = jnp.where(column == wanted, 1.0, 0.0).astype(BF16)
        taken.append(dot_nt(choose, stage))
    ropes = jnp.concatenate([part[:, KVR:] for part in taken], axis=1)
    for which, part in enumerate(taken):
        out[:, :, which * KVR : (which + 1) * KVR] = (
            part[:, :KVR].astype(BF16).reshape(n_store, rows, KVR)
        )
    out[:, :, 2 * KVR :] = ropes.astype(BF16).reshape(n_store, rows, 2 * ROPE)


def pack_pages(place, owner, slot, pool_t, rows):
    n_store = owner.shape[0]
    return pl.pallas_call(
        pack_kernel,
        out_shape=jax.ShapeDtypeStruct((n_store, rows, MSG), BF16),
        in_specs=[SMEM] + [HBM] * 3,
        out_specs=VMEM,
        scratch_shapes=[
            pltpu.VMEM(owner.shape, jnp.int32),
            pltpu.VMEM(slot.shape, jnp.int32),
            pltpu.VMEM((*pool_t.shape[:2], 128), BF16),
            pltpu.SemaphoreType.DMA((6,)),
        ],
        compiler_params=params(60),
        name="pack_pages",
    )(place, owner, slot, pool_t)


def keys_kernel(place, owner, count, pages, out, seen):
    rows = pages.shape[1]
    group = place[0]
    lane = lax.broadcasted_iota(jnp.int32, (rows, 128), 1)
    for k in range(pages.shape[0]):
        seen[k] = 0
    for j in range(owner.shape[1]):
        source = owner[group, j]
        second = seen[source] > 0
        seen[source] = 1
        bias = jnp.where(j < count[group], 0.0, MASKED_SCORE)
        row = pages[source]
        at = pl.ds(j * rows, rows)
        out[at, :KVR] = jnp.where(second, row[:, KVR : 2 * KVR], row[:, :KVR])
        pair = row[:, 2 * KVR :].astype(F32)
        rot = jnp.where(second, pltpu.roll(pair, ROPE, axis=1), pair)
        last = jnp.where(lane == ROPE, bias, 0.0)
        out[at, KVR:] = jnp.where(lane < ROPE, rot, last).astype(BF16)


def build_keys(place, owner, count, pages):
    n_keys = owner.shape[1] * pages.shape[1]
    return pl.pallas_call(
        keys_kernel,
        out_shape=jax.ShapeDtypeStruct((n_keys, WIDE), BF16),
        in_specs=[SMEM, SMEM, SMEM, VMEM],
        out_specs=VMEM,
        scratch_shapes=[pltpu.SMEM((pages.shape[0],), jnp.int32)],
        compiler_params=params(24),
        name="build_keys",
    )(place, owner, count, pages)


def rotation_table(n_rows):
    half = ROPE // 2
    freq = np.float32(ROTARY_BASE) ** (-(np.arange(half, dtype=np.float32) / np.float32(half)))
    angle = np.arange(n_rows, dtype=np.float32)[:, None] * freq.astype(np.float32)[None, :]
    angle = angle.astype(np.float64)
    parts = [np.cos(angle), np.cos(angle), -np.sin(angle), np.sin(angle)]
    return np.concatenate(parts, axis=1).astype(np.float32)


def project_kernel(
    place, count, tokens_src, gain, table, w_query_src, query, normed, turns, tokens, w_query, total, sems
):
    rows = tokens.shape[0]
    start = pl.multiple_of(count[place[0]] * PAGE + place[2] * rows, rows)
    pairs = [(tokens_src, tokens), (table.at[pl.ds(start, rows), :], turns)]
    pieces = 8
    depth = w_query.shape[0] // pieces
    for k in range(pieces):
        at = pl.ds(k * depth, depth)
        pairs.append((w_query_src.at[at, :], w_query.at[at, :]))
    copies = [
        pltpu.make_async_copy(src, dst, sems.at[i]) for i, (src, dst) in enumerate(pairs)
    ]
    for copy in copies:
        copy.start()
    copies[0].wait()
    normed[...] = rms(tokens[...].astype(F32), gain[...].astype(F32).reshape(1, -1)).astype(BF16)
    copies[1].wait()
    cosine, sine = turns[:, :ROPE], turns[:, ROPE:]
    cosine = jnp.concatenate([cosine, cosine], axis=1)
    sine = jnp.concatenate([sine, sine], axis=1)
    for k in range(0, pieces, 2):
        copies[2 + k].wait()
        copies[3 + k].wait()
        at = slice(k * depth, (k + 2) * depth)
        part = dot(normed[:, at], w_query[at, :])
        total[...] = part if k == 0 else total[...] + part
    head = NOPE + ROPE
    for at in range(0, query.shape[1], 2 * head):
        part = total[:, at : at + 2 * head].astype(BF16).astype(F32)
        query[:, at : at + NOPE] = part[:, :NOPE].astype(BF16)
        query[:, at + NOPE : at + 2 * NOPE] = part[:, head : head + NOPE].astype(BF16)
        pair = jnp.concatenate([part[:, NOPE:head], part[:, head + NOPE :]], axis=1)
        query[:, at + 2 * NOPE : at + 2 * head] = (turn(pair, cosine, sine) * SCALE).astype(BF16)


def project(place, count, tokens, gain, table, w_query):
    rows, width = tokens.shape
    cols = w_query.shape[1]
    return pl.pallas_call(
        project_kernel,
        out_shape=[
            jax.ShapeDtypeStruct((rows, cols), BF16),
            jax.ShapeDtypeStruct(tokens.shape, BF16),
            jax.ShapeDtypeStruct((rows, 2 * ROPE), F32),
        ],
        in_specs=[SMEM] * 2 + [HBM, VMEM] + [HBM] * 2,
        out_specs=[VMEM] * 3,
        scratch_shapes=[
            pltpu.VMEM(tokens.shape, BF16),
            pltpu.VMEM(w_query.shape, BF16),
            pltpu.VMEM((rows, cols), F32),
            pltpu.SemaphoreType.DMA((10,)),
        ],
        compiler_params=params(60),
        name="project",
    )(place, count, tokens, gain, table, w_query)


def latent_kernel(normed, turns, w_latent_t, kv_gain, new_latent, span):
    cosine, sine = turns[:, :ROPE], turns[:, ROPE:]
    cosine = jnp.concatenate([cosine, cosine], axis=1)
    sine = jnp.concatenate([sine, sine], axis=1)
    raw = dot_nt(normed[...], w_latent_t[...])
    latent = rms(raw[:, :KVR], kv_gain[...].astype(F32).reshape(1, -1)).astype(BF16)
    pair = jnp.concatenate([raw[:, KVR:], raw[:, KVR:]], axis=1)
    turned = turn(pair, cosine, sine)
    new_latent[:KVR, :] = latent.astype(F32).T.astype(BF16)
    new_latent[KVR:, :] = turned.T[:ROPE].astype(BF16)
    lane = lax.broadcasted_iota(jnp.int32, turned.shape, 1)
    span[:, :KVR] = latent
    span[:, KVR:] = jnp.where(lane < ROPE, turned, 0.0).astype(BF16)


def project_latent(normed, turns, w_latent_t, kv_gain):
    rows = normed.shape[0]
    return pl.pallas_call(
        latent_kernel,
        out_shape=[
            jax.ShapeDtypeStruct((LAT, rows), BF16),
            jax.ShapeDtypeStruct((rows, WIDE), BF16),
        ],
        in_specs=[VMEM] * 4,
        out_specs=[VMEM] * 2,
        compiler_params=params(16),
        name="project_latent",
    )(normed, turns, w_latent_t, kv_gain)


def fill_probes(query, key_up, probes):
    rows = query.shape[0]
    pair_width = 2 * (NOPE + ROPE)
    lane = lax.broadcasted_iota(jnp.int32, (rows, 2 * NOPE), 1)
    rope_lane = lane[:, : 2 * ROPE]
    for h in range(0, key_up.shape[0], 2):
        base = (h // 2) * pair_width
        nope = query[:, base : base + 2 * NOPE].astype(F32)
        both = jnp.concatenate(
            [jnp.where(lane < NOPE, nope, 0.0), jnp.where(lane < NOPE, 0.0, nope)], axis=0
        )
        maps = jnp.concatenate([key_up[h], key_up[h + 1]], axis=1)
        at = pl.ds(h * rows, 2 * rows)
        probes[at, :KVR] = (dot_nt(both.astype(BF16), maps) * SCALE).astype(BF16)
        pair = query[:, base + 2 * NOPE : base + pair_width].astype(F32)
        pair = jnp.concatenate([pair, pltpu.roll(pair, ROPE, axis=1)], axis=0)
        rope_lanes = jnp.concatenate([rope_lane, rope_lane], axis=0)
        one = jnp.where(rope_lanes == ROPE, 1.0, 0.0)
        probes[at, KVR:] = jnp.where(rope_lanes < ROPE, pair, one).astype(BF16)


def probes_kernel(key_up, *refs):
    count = len(refs) // 2
    for query, probes in zip(refs[:count], refs[count:]):
        fill_probes(query, key_up, probes)


def make_probes(key_up, *queries):
    rows = queries[0].shape[0]
    return pl.pallas_call(
        probes_kernel,
        out_shape=[jax.ShapeDtypeStruct((key_up.shape[0] * rows, WIDE), BF16)] * len(queries),
        in_specs=[VMEM] * (1 + len(queries)),
        out_specs=[VMEM] * len(queries),
        compiler_params=params(16),
        name="make_probes",
    )(key_up, *queries)


def attend_kernel(by, n_section, keep_far, place, value_up, near, arrived, span, *refs):
    far = arrived
    if by == 2:
        query, key_up, out, probes = refs
        fill_probes(query, key_up, probes)
    elif keep_far:
        probes, out, far = refs
        far[...] = arrived[...]
    else:
        probes, out = refs
    n_head, rows = value_up.shape[0], out.shape[0]
    blocks = (near, far, span)
    lane = lax.broadcasted_iota(jnp.int32, (rows, 128), 1)
    at_once = 4
    tile = at_once * rows
    steps = n_head // at_once
    width = n_head * NOPE

    if by == 0:
        row_of = lax.broadcasted_iota(jnp.int32, (tile, rows), 0) & (rows - 1)
        key_of = lax.broadcasted_iota(jnp.int32, (tile, rows), 1)
        hide = jnp.where(key_of <= row_of, 0.0, MASKED_SCORE)
    else:
        hide = jnp.where(place[2] + by < n_section, 0.0, MASKED_SCORE)

    pieces, closing = [], []
    for block in blocks:
        step = min(256, block.shape[0])
        for at in range(0, block.shape[0], step):
            pieces.append((block, at, step))
            closing.append(at + step == block.shape[0])

    def lanes(value):
        return [value[:, at : at + 128] for at in range(0, value.shape[1], 128)]

    def score(i, p, peak):
        block, at, step = pieces[p]
        value = dot_nt(probes[i * tile : (i + 1) * tile, :], block[at : at + step, :])
        if block is span:
            value = value + hide
        return value, functools.reduce(jnp.maximum, lanes(value), peak)

    def finish(i, total, summed, stats, top):
        total = jnp.sum(total, axis=1, keepdims=True)
        mixed = (summed * (1.0 / total)).astype(BF16)
        level = top + jnp.log2(total)
        for k in range(0, at_once, 2):
            h = i * at_once + k
            maps = jnp.concatenate([value_up[h], value_up[h + 1]], axis=1)
            value = dot(mixed[k * rows : (k + 2) * rows], maps).astype(BF16)
            out[:, h * VDIM : (h + 1) * VDIM] = value[:rows, :VDIM]
            out[:, (h + 1) * VDIM : (h + 2) * VDIM] = value[rows:, VDIM:]
        for k in range(at_once):
            stats = jnp.where(lane == i * at_once + k, level[k * rows : (k + 1) * rows], stats)
        return stats

    stats = jnp.zeros((rows, 128), F32)
    lowest = jnp.full((tile, 128), MASKED_SCORE, F32)
    ready, peak = [], lowest
    for p in range(len(pieces)):
        value, peak = score(0, p, peak)
        ready.append(value)
    for i in range(steps):
        top = jnp.max(peak, axis=1, keepdims=True)
        shift = jnp.broadcast_to(top, (tile, 128))
        total, summed = jnp.zeros((tile, 128), F32), 0.0
        coming, peak, weights = [], lowest, []
        for p in range(len(pieces)):
            if i + 1 < steps:
                value, peak = score(i + 1, p, peak)
                coming.append(value)
            for part in lanes(ready[p]):
                weight = jnp.exp2(part - shift)
                total = total + weight
                weights.append(weight.astype(BF16))
            if closing[p]:
                summed = summed + dot(jnp.concatenate(weights, axis=1), pieces[p][0][:, :KVR])
                weights = []
        stats = finish(i, total, summed, stats, top)
        ready = coming
    high = stats.astype(BF16).astype(F32)
    rest = stats - high
    mid = rest.astype(BF16).astype(F32)
    joined = high + pltpu.roll(mid, n_head, axis=1) + pltpu.roll(rest - mid, 2 * n_head, axis=1)
    out[:, width:] = joined.astype(BF16)


def attend(by, n_section, place, value_up, near, far, span, *queries, keep_far=False):
    rows, n_head = span.shape[0], value_up.shape[0]
    out_shape = [jax.ShapeDtypeStruct((rows, n_head * VDIM + 128), BF16)]
    if keep_far:
        out_shape.append(jax.ShapeDtypeStruct(far.shape, BF16))
    scratch = [pltpu.VMEM((n_head * rows, WIDE), BF16)] if by == 2 else []
    return pl.pallas_call(
        functools.partial(attend_kernel, by, n_section, keep_far),
        out_shape=out_shape,
        in_specs=[SMEM] + [VMEM] * (4 + len(queries)),
        out_specs=[VMEM] * len(out_shape),
        scratch_shapes=scratch,
        compiler_params=params(32),
        name="attend_%d" % by,
    )(place, value_up, near, far, span, *queries)


def output_kernel(n_head, own, one, two, three, weight, exact, send):
    parts = (own, one, two, three)
    width = n_head * VDIM
    levels = []
    for part in parts:
        stat = part[:, width:].astype(F32)
        rest = pltpu.roll(stat, 128 - n_head, axis=1) + pltpu.roll(stat, 128 - 2 * n_head, axis=1)
        levels.append(stat + rest)
    top = functools.reduce(jnp.maximum, levels)
    shares = [jnp.exp2(level - top) for level in levels]
    total = functools.reduce(jnp.add, shares)
    head_of = lax.broadcasted_iota(jnp.int32, (128, width), 0)
    lane_of = lax.broadcasted_iota(jnp.int32, (128, width), 1)
    begin = head_of * VDIM
    spread = jnp.where((lane_of >= begin) & (lane_of < begin + VDIM), 1.0, 0.0).astype(BF16)
    mixed = 0.0
    for part, share in zip(parts, shares):
        share = share / total
        high = share.astype(BF16)
        low = (share - high.astype(F32)).astype(BF16)
        factor = dot(high, spread) + dot(low, spread)
        mixed = mixed + part[:, :width].astype(F32) * factor
    per_head = mixed.astype(BF16)
    block = 512
    for at in range(0, weight.shape[1], block):
        part = dot(per_head, weight[:, at : at + block])
        exact[:, at : at + block] = part
        send[:, at : at + block] = part.astype(BF16)


def project_output(own, one, two, three, w_out):
    rows = own.shape[0]
    depth, cols = w_out.shape
    return pl.pallas_call(
        functools.partial(output_kernel, depth // VDIM),
        out_shape=[
            jax.ShapeDtypeStruct((rows, cols), F32),
            jax.ShapeDtypeStruct((rows, cols), BF16),
        ],
        in_specs=[VMEM] * 5,
        out_specs=[VMEM] * 2,
        compiler_params=params(16),
        name="project_output",
    )(own, one, two, three, w_out)


def expert_kernel(place, tokens, exact, other, gain, w_gate_t, w_up_t, w_down, keep, send):
    half = keep.shape[1]
    middle = tokens[...].astype(F32) + (exact[...] + other[...].astype(F32))
    middle = middle.astype(BF16).astype(F32)
    mlp_in = rms(middle, gain[...].astype(F32).reshape(1, -1)).astype(BF16)
    gate = dot_nt(mlp_in, w_gate_t[...])
    up = dot_nt(mlp_in, w_up_t[...])
    hidden = (gate / (1.0 + jnp.exp(-gate)) * up).astype(BF16)
    low = dot(hidden, w_down[:, :half])
    high = dot(hidden, w_down[:, half:])
    first = place[3] == 0
    keep[...] = jnp.where(first, middle[:, :half] + low, middle[:, half:] + high)
    send[...] = jnp.where(first, high, low).astype(BF16)


def expert(place, tokens, exact, other, gain, w_gate_t, w_up_t, w_down):
    rows, width = tokens.shape
    half = width // 2
    return pl.pallas_call(
        expert_kernel,
        out_shape=[
            jax.ShapeDtypeStruct((rows, half), F32),
            jax.ShapeDtypeStruct((rows, half), BF16),
        ],
        in_specs=[SMEM] + [VMEM] * 7,
        out_specs=[VMEM] * 2,
        compiler_params=params(24),
        name="expert",
    )(place, tokens, exact, other, gain, w_gate_t, w_up_t, w_down)


def on_device(
    tokens,
    attn_gain,
    w_query,
    w_latent,
    kv_gain,
    w_key_up,
    w_value_up,
    w_out,
    mlp_gain,
    w_gate,
    w_up,
    w_down,
    page_pool,
    hit_owner,
    hit_slot,
    fetch_count,
):
    n_store = lax.axis_size("store")
    n_section = lax.axis_size("section")
    n_tp = lax.axis_size("tp")
    group = lax.axis_index("store")
    section = lax.axis_index("section")
    core = lax.axis_index("tp")
    rows = tokens.shape[0]
    share = PAGE // (n_section * n_tp)

    swap = [(0, 1), (1, 0)]
    place = jnp.stack([group, section * n_tp + core, section, core]).astype(jnp.int32)
    owner = hit_owner[:, :, 0]
    outgoing = pack_pages(place, owner, hit_slot, jnp.swapaxes(page_pool, 1, 2), share)
    outgoing, early_tokens = lax.optimization_barrier((outgoing, tokens))
    outgoing = outgoing.reshape(n_store, 2, share // 2, MSG)
    arrived = lax.all_to_all(outgoing, "store", split_axis=0, concat_axis=0, tiled=True)
    arrived = arrived.reshape(n_store, share, MSG)

    def shift(value, by):
        pairs = [((z + by) % n_section, z) for z in range(n_section)]
        return lax.ppermute(value, "section", pairs)

    table = rotation_table((hit_owner.shape[1]) * PAGE + n_section * rows)
    query, normed, turns = project(
        place, fetch_count, early_tokens, attn_gain, jnp.asarray(table), w_query
    )
    next_query, last_query = shift(query, 1), shift(query, -1)
    new_latent, span = project_latent(normed, turns, w_latent.T, kv_gain)
    arrived, next_query, last_query, span = lax.optimization_barrier(
        (arrived, next_query, last_query, span)
    )
    far_query = shift(next_query, 1)

    near = build_keys(place, owner, fetch_count, arrived)
    far = lax.ppermute(near, "tp", swap)

    own_probes, next_probes, last_probes = make_probes(w_key_up, query, next_query, last_query)

    def partial_for(by, far, *queries, **flags):
        return attend(by, n_section, place, w_value_up, near, far, span, *queries, **flags)

    one, far = partial_for(1, far, next_probes, keep_far=True)
    one, far_query = lax.optimization_barrier((one, far_query))
    one = shift(one, -1)
    (two,) = partial_for(2, far, far_query, w_key_up)
    two, last_probes, one = lax.optimization_barrier((two, last_probes, one))
    two = shift(two, -1)
    (three,) = partial_for(3, far, last_probes)
    three, own_probes, two = lax.optimization_barrier((three, own_probes, two))
    three = shift(three, -3)
    two = shift(two, -1)
    (own,) = partial_for(0, far, own_probes)
    exact, send = project_output(own, one, two, three, w_out)
    incoming = lax.ppermute(send, "tp", swap)
    keep, send = expert(
        place,
        tokens,
        exact,
        incoming,
        mlp_gain,
        w_gate.T,
        w_up.T,
        w_down,
    )
    layer_out = (keep + lax.ppermute(send, "tp", swap).astype(F32)).astype(BF16)
    return (layer_out, new_latent.T)


def solution(mesh):
    in_specs = (
        P(("store", "section"), None),
        P(),
        P(None, "tp"),
        P(),
        P(),
        P("tp", None, None),
        P("tp", None, None),
        P("tp", None),
        P(),
        P(None, "tp"),
        P(None, "tp"),
        P("tp", None),
        P("store", None, None),
        P(),
        P(),
        P(),
    )
    out_specs = (P(("store", "section"), "tp"), P(("store", "section"), None))
    return jax.shard_map(
        on_device, mesh=mesh, in_specs=in_specs, out_specs=out_specs, check_vma=False
    )
```

```python
import functools
import math

import jax
import jax.numpy as jnp
import numpy as np
from jax import lax
from jax.experimental import pallas as pl
from jax.experimental.pallas import tpu as pltpu
from jax.sharding import PartitionSpec as P

NOPE = 128
ROPE = 64
KVR = 512
PAGE = 256
LAT = KVR + ROPE
WIDE = KVR + 2 * ROPE
MSG = 2 * LAT
VDIM = 128
EPSILON = 1e-06
ROTARY_BASE = 10000.0
MASKED_SCORE = -1e30
SCALE = (NOPE + ROPE) ** (-0.5) / math.log(2.0)
F32 = jnp.float32
BF16 = jnp.bfloat16
MB = 1024 * 1024

VMEM = pl.BlockSpec(memory_space=pltpu.VMEM)
SMEM = pl.BlockSpec(memory_space=pltpu.SMEM)
HBM = pl.BlockSpec(memory_space=pltpu.HBM)


def params(mb):
    return pltpu.CompilerParams(vmem_limit_bytes=mb * MB)


def dot(a, b):
    return jnp.dot(a, b, preferred_element_type=F32)


def dot_nt(a, b):
    return lax.dot_general(a, b, (((1,), (1,)), ((), ())), preferred_element_type=F32)


def rms(values, gain):
    mean_sq = jnp.mean(values * values, axis=-1, keepdims=True)
    return values * lax.rsqrt(mean_sq + EPSILON) * gain


def turn(values, cosine, sine):
    lane = lax.broadcasted_iota(jnp.int32, values.shape, 1)
    low = (lane & (ROPE // 2)) == 0
    partner = jnp.where(
        low, pltpu.roll(values, 128 - ROPE // 2, axis=1), pltpu.roll(values, ROPE // 2, axis=1)
    )
    return values * cosine + partner * sine


def pack_kernel(owner_src, slot_src, pool_src, out, owner, slot, pool, message, sems):
    group = lax.axis_index("store")
    shard = lax.axis_index("section") * lax.axis_size("tp") + lax.axis_index("tp")
    n_pages, width, window = pool.shape
    n_store, rows, _ = message.shape
    per = window // rows
    pairs = [(owner_src, owner), (slot_src, slot)]
    part = pl.ds(pl.multiple_of((shard // per) * window, window), window)
    for k in range(n_pages // 2):
        at = pl.ds(2 * k, 2)
        pairs.append((pool_src.at[at, :, part], pool.at[at]))
    copies = [
        pltpu.make_async_copy(src, dst, sems.at[i]) for i, (src, dst) in enumerate(pairs)
    ]
    for copy in copies:
        copy.start()
    copies[0].wait()
    copies[1].wait()
    n_list = owner.shape[1]
    held = owner[...] == group
    entry = lax.broadcasted_iota(jnp.int32, held.shape, 1)
    low = jnp.min(jnp.where(held, entry, n_list), axis=1, keepdims=True)
    high = jnp.max(jnp.where(held, entry, -1), axis=1, keepdims=True)
    at_once = n_store // 2
    row = lax.broadcasted_iota(jnp.int32, (rows, 1), 0)
    column = lax.broadcasted_iota(jnp.int32, (at_once * rows, n_pages * rows), 1)
    chosen = {}
    for which, hit in enumerate((low, high)):
        page = jnp.sum(jnp.where(entry == hit, slot[...], 0), axis=1, keepdims=True) * rows
        for to in range(0, n_store, at_once):
            wanted = [
                jnp.broadcast_to(page[g : g + 1], (rows, 1)) + row for g in range(to, to + at_once)
            ]
            wanted = jnp.concatenate(wanted, axis=0)
            chosen[to, which] = jnp.where(column == wanted, 1.0, 0.0).astype(BF16)
    first = (shard % per) * rows
    lane = lax.broadcasted_iota(jnp.int32, (width, window), 1)
    joined = []
    for at in range(0, n_pages, per):
        part = None
        for k in range(per):
            if k % 2 == 0:
                copies[2 + (at + k) // 2].wait()
            moved = pltpu.roll(pool[at + k].astype(F32), (k * rows - first + window) % window, axis=1)
            part = moved if part is None else jnp.where(lane >= k * rows, moved, part)
        joined.append(part.astype(BF16))
    stage = jnp.concatenate(joined, axis=1)
    sends = []
    for to in range(0, n_store, at_once):
        at = pl.ds(to, at_once)
        taken = [dot_nt(chosen[to, which], stage) for which in range(2)]
        ropes = jnp.concatenate([part[:, KVR:] for part in taken], axis=1)
        for which, part in enumerate(taken):
            message[at, :, which * KVR : (which + 1) * KVR] = (
                part[:, :KVR].astype(BF16).reshape(at_once, rows, KVR)
            )
        message[at, :, 2 * KVR :] = ropes.astype(BF16).reshape(at_once, rows, 2 * ROPE)
        send = pltpu.make_async_copy(message.at[at], out.at[at], sems.at[len(copies) + len(sends)])
        send.start()
        sends.append(send)
    for send in sends:
        send.wait()


def pack_pages(owner, slot, pool_t, rows):
    n_store, n_pages = owner.shape[0], pool_t.shape[0]
    return pl.pallas_call(
        pack_kernel,
        out_shape=jax.ShapeDtypeStruct((n_store, rows, MSG), BF16),
        in_specs=[HBM] * 3,
        out_specs=HBM,
        scratch_shapes=[
            pltpu.VMEM(owner.shape, jnp.int32),
            pltpu.VMEM(slot.shape, jnp.int32),
            pltpu.VMEM((*pool_t.shape[:2], 128), BF16),
            pltpu.VMEM((n_store, rows, MSG), BF16),
            pltpu.SemaphoreType.DMA((4 + n_pages // 2,)),
        ],
        compiler_params=params(60),
        name="pack_pages",
    )(owner, slot, pool_t)


def keys_kernel(owner, count, pages, out, seen):
    rows = pages.shape[1]
    group = lax.axis_index("store")
    lane = lax.broadcasted_iota(jnp.int32, (rows, 128), 1)
    for k in range(pages.shape[0]):
        seen[k] = 0
    for j in range(owner.shape[1]):
        source = owner[group, j]
        second = seen[source] > 0
        seen[source] = 1
        bias = jnp.where(j < count[group], 0.0, MASKED_SCORE)
        row = pages[source]
        at = pl.ds(j * rows, rows)
        out[at, :KVR] = jnp.where(second, row[:, KVR : 2 * KVR], row[:, :KVR])
        pair = row[:, 2 * KVR :].astype(F32)
        rot = jnp.where(second, pltpu.roll(pair, ROPE, axis=1), pair)
        last = jnp.where(lane == ROPE, bias, 0.0)
        out[at, KVR:] = jnp.where(lane < ROPE, rot, last).astype(BF16)


def build_keys(owner, count, pages):
    n_keys = owner.shape[1] * pages.shape[1]
    return pl.pallas_call(
        keys_kernel,
        out_shape=jax.ShapeDtypeStruct((n_keys, WIDE), BF16),
        in_specs=[SMEM, SMEM, VMEM],
        out_specs=VMEM,
        scratch_shapes=[pltpu.SMEM((pages.shape[0],), jnp.int32)],
        compiler_params=params(24),
        name="build_keys",
    )(owner, count, pages)


def rotation_table(n_rows):
    half = ROPE // 2
    freq = np.float32(ROTARY_BASE) ** (-(np.arange(half, dtype=np.float32) / np.float32(half)))
    angle = np.arange(n_rows, dtype=np.float32)[:, None] * freq.astype(np.float32)[None, :]
    angle = angle.astype(np.float64)
    parts = [np.cos(angle), np.cos(angle), -np.sin(angle), np.sin(angle)]
    return np.concatenate(parts, axis=1).astype(np.float32)


def project_kernel(
    count, tokens_src, gain, table, w_query_src, query, normed, turns, tokens, w_query, total, sems
):
    rows = tokens.shape[0]
    group, section = lax.axis_index("store"), lax.axis_index("section")
    start = pl.multiple_of(count[group] * PAGE + section * rows, rows)
    pairs = [(tokens_src, tokens), (table.at[pl.ds(start, rows), :], turns)]
    pieces = 8
    depth = w_query.shape[0] // pieces
    for k in range(pieces):
        at = pl.ds(k * depth, depth)
        pairs.append((w_query_src.at[at, :], w_query.at[at, :]))
    copies = [
        pltpu.make_async_copy(src, dst, sems.at[i]) for i, (src, dst) in enumerate(pairs)
    ]
    for copy in copies:
        copy.start()
    copies[0].wait()
    normed[...] = rms(tokens[...].astype(F32), gain[...].astype(F32).reshape(1, -1)).astype(BF16)
    copies[1].wait()
    cosine, sine = turns[:, :ROPE], turns[:, ROPE:]
    cosine = jnp.concatenate([cosine, cosine], axis=1)
    sine = jnp.concatenate([sine, sine], axis=1)
    for k in range(0, pieces, 2):
        copies[2 + k].wait()
        copies[3 + k].wait()
        at = slice(k * depth, (k + 2) * depth)
        part = dot(normed[:, at], w_query[at, :])
        total[...] = part if k == 0 else total[...] + part
    head = NOPE + ROPE
    for at in range(0, query.shape[1], 2 * head):
        part = total[:, at : at + 2 * head].astype(BF16).astype(F32)
        query[:, at : at + NOPE] = part[:, :NOPE].astype(BF16)
        query[:, at + NOPE : at + 2 * NOPE] = part[:, head : head + NOPE].astype(BF16)
        pair = jnp.concatenate([part[:, NOPE:head], part[:, head + NOPE :]], axis=1)
        query[:, at + 2 * NOPE : at + 2 * head] = (turn(pair, cosine, sine) * SCALE).astype(BF16)


def project(count, tokens, gain, table, w_query):
    rows, width = tokens.shape
    cols = w_query.shape[1]
    return pl.pallas_call(
        project_kernel,
        out_shape=[
            jax.ShapeDtypeStruct((rows, cols), BF16),
            jax.ShapeDtypeStruct(tokens.shape, BF16),
            jax.ShapeDtypeStruct((rows, 2 * ROPE), F32),
        ],
        in_specs=[SMEM, HBM, VMEM] + [HBM] * 2,
        out_specs=[VMEM] * 3,
        scratch_shapes=[
            pltpu.VMEM(tokens.shape, BF16),
            pltpu.VMEM(w_query.shape, BF16),
            pltpu.VMEM((rows, cols), F32),
            pltpu.SemaphoreType.DMA((10,)),
        ],
        compiler_params=params(60),
        name="project",
    )(count, tokens, gain, table, w_query)


def latent_kernel(normed, turns, w_latent_t, kv_gain, new_latent, span):
    cosine, sine = turns[:, :ROPE], turns[:, ROPE:]
    cosine = jnp.concatenate([cosine, cosine], axis=1)
    sine = jnp.concatenate([sine, sine], axis=1)
    raw = dot_nt(normed[...], w_latent_t[...])
    latent = rms(raw[:, :KVR], kv_gain[...].astype(F32).reshape(1, -1)).astype(BF16)
    pair = jnp.concatenate([raw[:, KVR:], raw[:, KVR:]], axis=1)
    turned = turn(pair, cosine, sine)
    new_latent[:KVR, :] = latent.astype(F32).T.astype(BF16)
    new_latent[KVR:, :] = turned.T[:ROPE].astype(BF16)
    lane = lax.broadcasted_iota(jnp.int32, turned.shape, 1)
    span[:, :KVR] = latent
    span[:, KVR:] = jnp.where(lane < ROPE, turned, 0.0).astype(BF16)


def project_latent(normed, turns, w_latent_t, kv_gain):
    rows = normed.shape[0]
    return pl.pallas_call(
        latent_kernel,
        out_shape=[
            jax.ShapeDtypeStruct((LAT, rows), BF16),
            jax.ShapeDtypeStruct((rows, WIDE), BF16),
        ],
        in_specs=[VMEM] * 4,
        out_specs=[VMEM] * 2,
        compiler_params=params(16),
        name="project_latent",
    )(normed, turns, w_latent_t, kv_gain)


def fill_probes(query, key_up, probes):
    rows = query.shape[0]
    pair_width = 2 * (NOPE + ROPE)
    lane = lax.broadcasted_iota(jnp.int32, (rows, 2 * NOPE), 1)
    rope_lane = lane[:, : 2 * ROPE]
    for h in range(0, key_up.shape[0], 2):
        base = (h // 2) * pair_width
        nope = query[:, base : base + 2 * NOPE].astype(F32)
        both = jnp.concatenate(
            [jnp.where(lane < NOPE, nope, 0.0), jnp.where(lane < NOPE, 0.0, nope)], axis=0
        )
        maps = jnp.concatenate([key_up[h], key_up[h + 1]], axis=1)
        at = pl.ds(h * rows, 2 * rows)
        probes[at, :KVR] = (dot_nt(both.astype(BF16), maps) * SCALE).astype(BF16)
        pair = query[:, base + 2 * NOPE : base + pair_width].astype(F32)
        pair = jnp.concatenate([pair, pltpu.roll(pair, ROPE, axis=1)], axis=0)
        rope_lanes = jnp.concatenate([rope_lane, rope_lane], axis=0)
        one = jnp.where(rope_lanes == ROPE, 1.0, 0.0)
        probes[at, KVR:] = jnp.where(rope_lanes < ROPE, pair, one).astype(BF16)


def probes_kernel(key_up, own, ahead, behind, own_probes, ahead_probes, behind_probes, low, high):
    cut = low.shape[0]
    low[...] = ahead[:cut, :]
    high[...] = behind[cut:, :]
    for query, probes in ((own, own_probes), (ahead, ahead_probes), (behind, behind_probes)):
        fill_probes(query, key_up, probes)


def make_probes(key_up, own, ahead, behind):
    rows, width = own.shape
    probes = jax.ShapeDtypeStruct((key_up.shape[0] * rows, WIDE), BF16)
    half = jax.ShapeDtypeStruct((rows // 2, width), BF16)
    return pl.pallas_call(
        probes_kernel,
        out_shape=[probes] * 3 + [half] * 2,
        in_specs=[VMEM] * 4,
        out_specs=[VMEM] * 5,
        compiler_params=params(16),
        name="make_probes",
    )(key_up, own, ahead, behind)


def attend_kernel(by, keep_far, value_up, near, arrived, span, *refs):
    far = arrived
    if by == 2:
        low, high, key_up, out, query, probes = refs
        query[: low.shape[0], :] = low[...]
        query[low.shape[0] :, :] = high[...]
        fill_probes(query, key_up, probes)
    elif keep_far:
        probes, out, far = refs
        far[...] = arrived[...]
    else:
        probes, out = refs
    n_head, rows = value_up.shape[0], out.shape[0]
    blocks = (near, far, span)
    lane = lax.broadcasted_iota(jnp.int32, (rows, 128), 1)
    at_once = 2
    tile = at_once * rows
    steps = n_head // at_once
    width = n_head * NOPE

    if by == 0:
        row_of = lax.broadcasted_iota(jnp.int32, (tile, rows), 0) & (rows - 1)
        key_of = lax.broadcasted_iota(jnp.int32, (tile, rows), 1)
        hide = jnp.where(key_of <= row_of, 0.0, MASKED_SCORE)
    else:
        later = lax.axis_index("section") + by < lax.axis_size("section")
        hide = jnp.where(later, 0.0, MASKED_SCORE)

    pieces, closing = [], []
    for block in blocks:
        step = min(256, block.shape[0])
        for at in range(0, block.shape[0], step):
            pieces.append((block, at, step))
            closing.append(at + step == block.shape[0])

    def lanes(value):
        return [value[:, at : at + 128] for at in range(0, value.shape[1], 128)]

    def score(i, p, peak):
        block, at, size = pieces[p]
        value = dot_nt(probes[i * tile : (i + 1) * tile, :], block[at : at + size, :])
        if block is span:
            value = value + hide
        return value, functools.reduce(jnp.maximum, lanes(value), peak)

    stats = jnp.zeros((rows, 128), F32)
    lowest = jnp.full((tile, 128), MASKED_SCORE, F32)
    ready, peak = [], lowest
    for p in range(len(pieces)):
        value, peak = score(0, p, peak)
        ready.append(value)
    for i in range(steps):
        top = jnp.max(peak, axis=1, keepdims=True)
        shift = jnp.broadcast_to(top, (tile, 128))
        total, summed = jnp.zeros((tile, 128), F32), 0.0
        coming, peak, weights = [], lowest, []
        for p in range(len(pieces)):
            if i + 1 < steps:
                value, peak = score(i + 1, p, peak)
                coming.append(value)
            for part in lanes(ready[p]):
                weight = jnp.exp2(part - shift)
                total = total + weight
                weights.append(weight.astype(BF16))
            if closing[p]:
                summed = summed + dot(jnp.concatenate(weights, axis=1), pieces[p][0][:, :KVR])
                weights = []
        ready = coming
        total = jnp.sum(total, axis=1, keepdims=True)
        mixed = (summed * (1.0 / total)).astype(BF16)
        level = top + jnp.log2(total)
        h = i * at_once
        maps = jnp.concatenate([value_up[h], value_up[h + 1]], axis=1)
        value = dot(mixed, maps).astype(BF16)
        out[:, h * VDIM : (h + 1) * VDIM] = value[:rows, :VDIM]
        out[:, (h + 1) * VDIM : (h + 2) * VDIM] = value[rows:, VDIM:]
        for k in range(at_once):
            stats = jnp.where(lane == h + k, level[k * rows : (k + 1) * rows], stats)
    high = stats.astype(BF16).astype(F32)
    rest = stats - high
    mid = rest.astype(BF16).astype(F32)
    joined = high + pltpu.roll(mid, n_head, axis=1) + pltpu.roll(rest - mid, 2 * n_head, axis=1)
    out[:, width:] = joined.astype(BF16)


def attend(by, value_up, near, far, span, *queries, keep_far=False):
    rows, n_head = span.shape[0], value_up.shape[0]
    out_shape = [jax.ShapeDtypeStruct((rows, n_head * VDIM + 128), BF16)]
    if keep_far:
        out_shape.append(jax.ShapeDtypeStruct(far.shape, BF16))
    scratch = []
    if by == 2:
        scratch.append(pltpu.VMEM((rows, queries[0].shape[1]), BF16))
        scratch.append(pltpu.VMEM((n_head * rows, WIDE), BF16))
    return pl.pallas_call(
        functools.partial(attend_kernel, by, keep_far),
        out_shape=out_shape,
        in_specs=[VMEM] * (4 + len(queries)),
        out_specs=[VMEM] * len(out_shape),
        scratch_shapes=scratch,
        compiler_params=params(32),
        name="attend_%d" % by,
    )(value_up, near, far, span, *queries)


def output_kernel(n_head, own, one, two, three, weight, exact, send):
    parts = (own, one, two, three)
    width = n_head * VDIM
    levels = []
    for part in parts:
        stat = part[:, width:].astype(F32)
        rest = pltpu.roll(stat, 128 - n_head, axis=1) + pltpu.roll(stat, 128 - 2 * n_head, axis=1)
        levels.append(stat + rest)
    top = functools.reduce(jnp.maximum, levels)
    shares = [jnp.exp2(level - top) for level in levels]
    total = functools.reduce(jnp.add, shares)
    head_of = lax.broadcasted_iota(jnp.int32, (128, width), 0)
    lane_of = lax.broadcasted_iota(jnp.int32, (128, width), 1)
    begin = head_of * VDIM
    spread = jnp.where((lane_of >= begin) & (lane_of < begin + VDIM), 1.0, 0.0).astype(BF16)
    mixed = 0.0
    for part, share in zip(parts, shares):
        share = share / total
        high = share.astype(BF16)
        low = (share - high.astype(F32)).astype(BF16)
        factor = dot(high, spread) + dot(low, spread)
        mixed = mixed + part[:, :width].astype(F32) * factor
    per_head = mixed.astype(BF16)
    block = 512
    for at in range(0, weight.shape[1], block):
        part = dot(per_head, weight[:, at : at + block])
        exact[:, at : at + block] = part
        send[:, at : at + block] = part.astype(BF16)


def project_output(own, one, two, three, w_out):
    rows = own.shape[0]
    depth, cols = w_out.shape
    return pl.pallas_call(
        functools.partial(output_kernel, depth // VDIM),
        out_shape=[
            jax.ShapeDtypeStruct((rows, cols), F32),
            jax.ShapeDtypeStruct((rows, cols), BF16),
        ],
        in_specs=[VMEM] * 5,
        out_specs=[VMEM] * 2,
        compiler_params=params(16),
        name="project_output",
    )(own, one, two, three, w_out)


def expert_kernel(tokens, exact, other, gain, w_gate_t, w_up_t, w_down, keep, send):
    half = keep.shape[1]
    middle = tokens[...].astype(F32) + (exact[...] + other[...].astype(F32))
    middle = middle.astype(BF16).astype(F32)
    mlp_in = rms(middle, gain[...].astype(F32).reshape(1, -1)).astype(BF16)
    gate = dot_nt(mlp_in, w_gate_t[...])
    up = dot_nt(mlp_in, w_up_t[...])
    hidden = (gate / (1.0 + jnp.exp(-gate)) * up).astype(BF16)
    low = dot(hidden, w_down[:, :half])
    high = dot(hidden, w_down[:, half:])
    first = lax.axis_index("tp") == 0
    keep[...] = jnp.where(first, middle[:, :half] + low, middle[:, half:] + high)
    send[...] = jnp.where(first, high, low).astype(BF16)


def expert(tokens, exact, other, gain, w_gate_t, w_up_t, w_down):
    rows, width = tokens.shape
    half = width // 2
    return pl.pallas_call(
        expert_kernel,
        out_shape=[
            jax.ShapeDtypeStruct((rows, half), F32),
            jax.ShapeDtypeStruct((rows, half), BF16),
        ],
        in_specs=[VMEM] * 7,
        out_specs=[VMEM] * 2,
        compiler_params=params(24),
        name="expert",
    )(tokens, exact, other, gain, w_gate_t, w_up_t, w_down)


def on_device(
    tokens,
    attn_gain,
    w_query,
    w_latent,
    kv_gain,
    w_key_up,
    w_value_up,
    w_out,
    mlp_gain,
    w_gate,
    w_up,
    w_down,
    page_pool,
    hit_owner,
    hit_slot,
    fetch_count,
):
    n_store = lax.axis_size("store")
    n_section = lax.axis_size("section")
    n_tp = lax.axis_size("tp")
    rows = tokens.shape[0]
    share = PAGE // (n_section * n_tp)

    swap = [(0, 1), (1, 0)]
    owner = hit_owner[:, :, 0]
    outgoing = pack_pages(owner, hit_slot, jnp.swapaxes(page_pool, 1, 2), share)
    outgoing, early_tokens = lax.optimization_barrier((outgoing, tokens))
    outgoing = outgoing.reshape(n_store, 2, share // 2, MSG)
    arrived = lax.all_to_all(outgoing, "store", split_axis=0, concat_axis=0, tiled=True)
    arrived = arrived.reshape(n_store, share, MSG)

    def shift(value, by):
        pairs = [((z + by) % n_section, z) for z in range(n_section)]
        return lax.ppermute(value, "section", pairs)

    table = rotation_table((hit_owner.shape[1]) * PAGE + n_section * rows)
    query, normed, turns = project(
        fetch_count, early_tokens, attn_gain, jnp.asarray(table), w_query
    )
    next_query, last_query = shift(query, 1), shift(query, -1)
    new_latent, span = project_latent(normed, turns, w_latent.T, kv_gain)
    arrived, next_query, last_query, span = lax.optimization_barrier(
        (arrived, next_query, last_query, span)
    )

    near = build_keys(owner, fetch_count, arrived)
    far = lax.ppermute(near, "tp", swap)

    own_probes, next_probes, last_probes, low, high = make_probes(
        w_key_up, query, next_query, last_query
    )
    far_low, far_high = shift(low, 1), shift(high, -1)

    def partial_for(by, far, *queries, **flags):
        return attend(by, w_value_up, near, far, span, *queries, **flags)

    one, far = partial_for(1, far, next_probes, keep_far=True)
    one, far_low, far_high = lax.optimization_barrier((one, far_low, far_high))
    one = shift(one, -1)
    (two,) = partial_for(2, far, far_low, far_high, w_key_up)
    two, last_probes, one = lax.optimization_barrier((two, last_probes, one))
    two = shift(two, -1)
    (three,) = partial_for(3, far, last_probes)
    three, own_probes, two = lax.optimization_barrier((three, own_probes, two))
    three = shift(three, -3)
    two = shift(two, -1)
    (own,) = partial_for(0, far, own_probes)
    exact, send = project_output(own, one, two, three, w_out)
    incoming = lax.ppermute(send, "tp", swap)
    keep, send = expert(
        tokens,
        exact,
        incoming,
        mlp_gain,
        w_gate.T,
        w_up.T,
        w_down,
    )
    layer_out = (keep + lax.ppermute(send, "tp", swap).astype(F32)).astype(BF16)
    return (layer_out, new_latent.T)


def solution(mesh):
    in_specs = (
        P(("store", "section"), None),
        P(),
        P(None, "tp"),
        P(),
        P(),
        P("tp", None, None),
        P("tp", None, None),
        P("tp", None),
        P(),
        P(None, "tp"),
        P(None, "tp"),
        P("tp", None),
        P("store", None, None),
        P(),
        P(),
        P(),
    )
    out_specs = (P(("store", "section"), "tp"), P(("store", "section"), None))
    return jax.shard_map(
        on_device, mesh=mesh, in_specs=in_specs, out_specs=out_specs, check_vma=False
    )
```

```python
import functools
import math

import jax
import jax.numpy as jnp
import numpy as np
from jax import lax
from jax.experimental import pallas as pl
from jax.experimental.pallas import tpu as pltpu
from jax.sharding import PartitionSpec as P

NOPE = 128
ROPE = 64
KVR = 512
PAGE = 256
LAT = KVR + ROPE
WIDE = KVR + 2 * ROPE
MSG = 2 * LAT
VDIM = 128
EPSILON = 1e-06
ROTARY_BASE = 10000.0
MASKED_SCORE = -1e30
SCALE = (NOPE + ROPE) ** (-0.5) / math.log(2.0)
F32 = jnp.float32
BF16 = jnp.bfloat16
MB = 1024 * 1024

VMEM = pl.BlockSpec(memory_space=pltpu.VMEM)
SMEM = pl.BlockSpec(memory_space=pltpu.SMEM)
HBM = pl.BlockSpec(memory_space=pltpu.HBM)


def params(mb):
    return pltpu.CompilerParams(vmem_limit_bytes=mb * MB)


def dot(a, b):
    return jnp.dot(a, b, preferred_element_type=F32)


def dot_nt(a, b):
    return lax.dot_general(a, b, (((1,), (1,)), ((), ())), preferred_element_type=F32)


def rms(values, gain):
    mean_sq = jnp.mean(values * values, axis=-1, keepdims=True)
    return values * lax.rsqrt(mean_sq + EPSILON) * gain


def turn(values, cosine, sine):
    lane = lax.broadcasted_iota(jnp.int32, values.shape, 1)
    low = (lane & (ROPE // 2)) == 0
    partner = jnp.where(
        low, pltpu.roll(values, 128 - ROPE // 2, axis=1), pltpu.roll(values, ROPE // 2, axis=1)
    )
    return values * cosine + partner * sine


def pack_kernel(owner_src, slot_src, pool_src, out, owner, slot, pool, message, sems):
    group = lax.axis_index("store")
    shard = lax.axis_index("section") * lax.axis_size("tp") + lax.axis_index("tp")
    n_pages, width, window = pool.shape
    n_store, rows, _ = message.shape
    per = window // rows
    pairs = [(owner_src, owner), (slot_src, slot)]
    part = pl.ds(pl.multiple_of((shard // per) * window, window), window)
    for k in range(n_pages // 2):
        at = pl.ds(2 * k, 2)
        pairs.append((pool_src.at[at, :, part], pool.at[at]))
    copies = [
        pltpu.make_async_copy(src, dst, sems.at[i]) for i, (src, dst) in enumerate(pairs)
    ]
    for copy in copies:
        copy.start()
    copies[0].wait()
    copies[1].wait()
    n_list = owner.shape[1]
    held = owner[...] == group
    entry = lax.broadcasted_iota(jnp.int32, held.shape, 1)
    low = jnp.min(jnp.where(held, entry, n_list), axis=1, keepdims=True)
    high = jnp.max(jnp.where(held, entry, -1), axis=1, keepdims=True)
    at_once = n_store // 2
    row = lax.broadcasted_iota(jnp.int32, (rows, 1), 0)
    column = lax.broadcasted_iota(jnp.int32, (at_once * rows, n_pages * rows), 1)
    chosen = {}
    for which, hit in enumerate((low, high)):
        page = jnp.sum(jnp.where(entry == hit, slot[...], 0), axis=1, keepdims=True) * rows
        for to in range(0, n_store, at_once):
            wanted = [
                jnp.broadcast_to(page[g : g + 1], (rows, 1)) + row for g in range(to, to + at_once)
            ]
            wanted = jnp.concatenate(wanted, axis=0)
            chosen[to, which] = jnp.where(column == wanted, 1.0, 0.0).astype(BF16)
    first = (shard % per) * rows
    lane = lax.broadcasted_iota(jnp.int32, (width, window), 1)
    joined = []
    for at in range(0, n_pages, per):
        part = None
        for k in range(per):
            if k % 2 == 0:
                copies[2 + (at + k) // 2].wait()
            moved = pltpu.roll(pool[at + k].astype(F32), (k * rows - first + window) % window, axis=1)
            part = moved if part is None else jnp.where(lane >= k * rows, moved, part)
        joined.append(part.astype(BF16))
    stage = jnp.concatenate(joined, axis=1)
    sends = []
    for to in range(0, n_store, at_once):
        at = pl.ds(to, at_once)
        taken = [dot_nt(chosen[to, which], stage) for which in range(2)]
        ropes = jnp.concatenate([part[:, KVR:] for part in taken], axis=1)
        for which, part in enumerate(taken):
            message[at, :, which * KVR : (which + 1) * KVR] = (
                part[:, :KVR].astype(BF16).reshape(at_once, rows, KVR)
            )
        message[at, :, 2 * KVR :] = ropes.astype(BF16).reshape(at_once, rows, 2 * ROPE)
        send = pltpu.make_async_copy(message.at[at], out.at[at], sems.at[len(copies) + len(sends)])
        send.start()
        sends.append(send)
    for send in sends:
        send.wait()


def pack_pages(owner, slot, pool_t, rows):
    n_store, n_pages = owner.shape[0], pool_t.shape[0]
    return pl.pallas_call(
        pack_kernel,
        out_shape=jax.ShapeDtypeStruct((n_store, rows, MSG), BF16),
        in_specs=[HBM] * 3,
        out_specs=HBM,
        scratch_shapes=[
            pltpu.VMEM(owner.shape, jnp.int32),
            pltpu.VMEM(slot.shape, jnp.int32),
            pltpu.VMEM((*pool_t.shape[:2], 128), BF16),
            pltpu.VMEM((n_store, rows, MSG), BF16),
            pltpu.SemaphoreType.DMA((4 + n_pages // 2,)),
        ],
        compiler_params=params(56),
        cost_estimate=pl.CostEstimate(flops=2 * 10**10, bytes_accessed=6 * 10**7, transcendentals=0),
        name="pack_pages",
    )(owner, slot, pool_t)


def keys_kernel(owner, count, pages, out, seen):
    rows = pages.shape[1]
    group = lax.axis_index("store")
    lane = lax.broadcasted_iota(jnp.int32, (rows, 128), 1)
    for k in range(pages.shape[0]):
        seen[k] = 0
    for j in range(owner.shape[1]):
        source = owner[group, j]
        second = seen[source] > 0
        seen[source] = 1
        bias = jnp.where(j < count[group], 0.0, MASKED_SCORE)
        row = pages[source]
        at = pl.ds(j * rows, rows)
        out[at, :KVR] = jnp.where(second, row[:, KVR : 2 * KVR], row[:, :KVR])
        pair = row[:, 2 * KVR :].astype(F32)
        rot = jnp.where(second, pltpu.roll(pair, ROPE, axis=1), pair)
        last = jnp.where(lane == ROPE, bias, 0.0)
        out[at, KVR:] = jnp.where(lane < ROPE, rot, last).astype(BF16)


def build_keys(owner, count, pages):
    n_keys = owner.shape[1] * pages.shape[1]
    return pl.pallas_call(
        keys_kernel,
        out_shape=jax.ShapeDtypeStruct((n_keys, WIDE), BF16),
        in_specs=[SMEM, SMEM, VMEM],
        out_specs=VMEM,
        scratch_shapes=[pltpu.SMEM((pages.shape[0],), jnp.int32)],
        compiler_params=params(24),
        name="build_keys",
    )(owner, count, pages)


def rotation_table(n_rows):
    half = ROPE // 2
    freq = np.float32(ROTARY_BASE) ** (-(np.arange(half, dtype=np.float32) / np.float32(half)))
    angle = np.arange(n_rows, dtype=np.float32)[:, None] * freq.astype(np.float32)[None, :]
    angle = angle.astype(np.float64)
    parts = [np.cos(angle), np.cos(angle), -np.sin(angle), np.sin(angle)]
    return np.concatenate(parts, axis=1).astype(np.float32)


def project_kernel(
    count, tokens_src, gain, table, w_query, query, normed, turns, tokens, total, sems
):
    rows = tokens.shape[0]
    group, section = lax.axis_index("store"), lax.axis_index("section")
    start = pl.multiple_of(count[group] * PAGE + section * rows, rows)
    pairs = [(tokens_src, tokens), (table.at[pl.ds(start, rows), :], turns)]
    copies = [
        pltpu.make_async_copy(src, dst, sems.at[i]) for i, (src, dst) in enumerate(pairs)
    ]
    for copy in copies:
        copy.start()
    copies[0].wait()
    normed[...] = rms(tokens[...].astype(F32), gain[...].astype(F32).reshape(1, -1)).astype(BF16)
    copies[1].wait()
    cosine, sine = turns[:, :ROPE], turns[:, ROPE:]
    cosine = jnp.concatenate([cosine, cosine], axis=1)
    sine = jnp.concatenate([sine, sine], axis=1)
    total[...] = dot(normed[...], w_query[...])
    head = NOPE + ROPE
    for at in range(0, query.shape[1], 2 * head):
        part = total[:, at : at + 2 * head].astype(BF16).astype(F32)
        query[:, at : at + NOPE] = part[:, :NOPE].astype(BF16)
        query[:, at + NOPE : at + 2 * NOPE] = part[:, head : head + NOPE].astype(BF16)
        pair = jnp.concatenate([part[:, NOPE:head], part[:, head + NOPE :]], axis=1)
        query[:, at + 2 * NOPE : at + 2 * head] = (turn(pair, cosine, sine) * SCALE).astype(BF16)


def project(count, tokens, gain, table, w_query):
    rows, width = tokens.shape
    cols = w_query.shape[1]
    return pl.pallas_call(
        project_kernel,
        out_shape=[
            jax.ShapeDtypeStruct((rows, cols), BF16),
            jax.ShapeDtypeStruct(tokens.shape, BF16),
            jax.ShapeDtypeStruct((rows, 2 * ROPE), F32),
        ],
        in_specs=[SMEM, HBM, VMEM, HBM, VMEM],
        out_specs=[VMEM] * 3,
        scratch_shapes=[
            pltpu.VMEM(tokens.shape, BF16),
            pltpu.VMEM((rows, cols), F32),
            pltpu.SemaphoreType.DMA((2,)),
        ],
        compiler_params=params(30),
        name="project",
    )(count, tokens, gain, table, w_query)


def latent_kernel(normed, turns, w_latent_t, kv_gain, new_latent, span):
    cosine, sine = turns[:, :ROPE], turns[:, ROPE:]
    cosine = jnp.concatenate([cosine, cosine], axis=1)
    sine = jnp.concatenate([sine, sine], axis=1)
    raw = dot_nt(normed[...], w_latent_t[...])
    latent = rms(raw[:, :KVR], kv_gain[...].astype(F32).reshape(1, -1)).astype(BF16)
    pair = jnp.concatenate([raw[:, KVR:], raw[:, KVR:]], axis=1)
    turned = turn(pair, cosine, sine)
    new_latent[:KVR, :] = latent.astype(F32).T.astype(BF16)
    new_latent[KVR:, :] = turned.T[:ROPE].astype(BF16)
    lane = lax.broadcasted_iota(jnp.int32, turned.shape, 1)
    span[:, :KVR] = latent
    span[:, KVR:] = jnp.where(lane < ROPE, turned, 0.0).astype(BF16)


def project_latent(normed, turns, w_latent_t, kv_gain):
    rows = normed.shape[0]
    return pl.pallas_call(
        latent_kernel,
        out_shape=[
            jax.ShapeDtypeStruct((LAT, rows), BF16),
            jax.ShapeDtypeStruct((rows, WIDE), BF16),
        ],
        in_specs=[VMEM] * 4,
        out_specs=[VMEM] * 2,
        compiler_params=params(16),
        name="project_latent",
    )(normed, turns, w_latent_t, kv_gain)


def fill_probes(query, key_up, probes):
    rows = query.shape[0]
    pair_width = 2 * (NOPE + ROPE)
    lane = lax.broadcasted_iota(jnp.int32, (rows, 2 * NOPE), 1)
    rope_lane = lane[:, : 2 * ROPE]
    for h in range(0, key_up.shape[0], 2):
        base = (h // 2) * pair_width
        nope = query[:, base : base + 2 * NOPE].astype(F32)
        both = jnp.concatenate(
            [jnp.where(lane < NOPE, nope, 0.0), jnp.where(lane < NOPE, 0.0, nope)], axis=0
        )
        maps = jnp.concatenate([key_up[h], key_up[h + 1]], axis=1)
        at = pl.ds(h * rows, 2 * rows)
        probes[at, :KVR] = (dot_nt(both.astype(BF16), maps) * SCALE).astype(BF16)
        pair = query[:, base + 2 * NOPE : base + pair_width].astype(F32)
        pair = jnp.concatenate([pair, pltpu.roll(pair, ROPE, axis=1)], axis=0)
        rope_lanes = jnp.concatenate([rope_lane, rope_lane], axis=0)
        one = jnp.where(rope_lanes == ROPE, 1.0, 0.0)
        probes[at, KVR:] = jnp.where(rope_lanes < ROPE, pair, one).astype(BF16)


def probes_kernel(
    key_up, own_src, ahead_src, behind_src, own_probes, ahead_probes, behind_probes, low, high,
    own, ahead, behind, sems
):
    pairs = ((ahead_src, ahead), (behind_src, behind), (own_src, own))
    copies = [
        pltpu.make_async_copy(src, dst, sems.at[i]) for i, (src, dst) in enumerate(pairs)
    ]
    for copy in copies:
        copy.start()
    for copy in copies:
        copy.wait()
    cut = low.shape[0]
    low[...] = ahead[:cut, :]
    high[...] = behind[cut:, :]
    for query, probes in ((own, own_probes), (ahead, ahead_probes), (behind, behind_probes)):
        fill_probes(query, key_up, probes)


def make_probes(key_up, own, ahead, behind):
    rows, width = own.shape
    probes = jax.ShapeDtypeStruct((key_up.shape[0] * rows, WIDE), BF16)
    half = jax.ShapeDtypeStruct((rows // 2, width), BF16)
    return pl.pallas_call(
        probes_kernel,
        out_shape=[probes] * 3 + [half] * 2,
        in_specs=[VMEM] + [HBM] * 3,
        out_specs=[VMEM] * 5,
        scratch_shapes=[pltpu.VMEM((rows, width), BF16)] * 3 + [pltpu.SemaphoreType.DMA((3,))],
        compiler_params=params(30),
        name="make_probes",
    )(key_up, own, ahead, behind)


def attend_kernel(by, keep_far, value_up, near, arrived, span, *refs):
    far = arrived
    if by == 2:
        low, high, key_up, out, query, probes = refs
        query[: low.shape[0], :] = low[...]
        query[low.shape[0] :, :] = high[...]
        fill_probes(query, key_up, probes)
    elif keep_far:
        probes, out, far = refs
        far[...] = arrived[...]
    else:
        probes, out = refs
    n_head, rows = value_up.shape[0], out.shape[0]
    blocks = (near, far, span)
    lane = lax.broadcasted_iota(jnp.int32, (rows, 128), 1)
    at_once = 2
    tile = at_once * rows
    steps = n_head // at_once
    width = n_head * NOPE

    if by == 0:
        row_of = lax.broadcasted_iota(jnp.int32, (tile, rows), 0) & (rows - 1)
        key_of = lax.broadcasted_iota(jnp.int32, (tile, rows), 1)
        hide = jnp.where(key_of <= row_of, 0.0, MASKED_SCORE)
    else:
        later = lax.axis_index("section") + by < lax.axis_size("section")
        hide = jnp.where(later, 0.0, MASKED_SCORE)

    pieces, closing = [], []
    for block in blocks:
        step = min(256, block.shape[0])
        for at in range(0, block.shape[0], step):
            pieces.append((block, at, step))
            closing.append(at + step == block.shape[0])

    def lanes(value):
        return [value[:, at : at + 128] for at in range(0, value.shape[1], 128)]

    def score(i, p, peak):
        block, at, size = pieces[p]
        value = dot_nt(probes[i * tile : (i + 1) * tile, :], block[at : at + size, :])
        if block is span:
            value = value + hide
        return value, functools.reduce(jnp.maximum, lanes(value), peak)

    stats = jnp.zeros((rows, 128), F32)
    lowest = jnp.full((tile, 128), MASKED_SCORE, F32)
    ready, peak = [], lowest
    for p in range(len(pieces)):
        value, peak = score(0, p, peak)
        ready.append(value)
    for i in range(steps):
        top = jnp.max(peak, axis=1, keepdims=True)
        shift = jnp.broadcast_to(top, (tile, 128))
        total, summed = jnp.zeros((tile, 128), F32), 0.0
        coming, peak, weights = [], lowest, []
        for p in range(len(pieces)):
            if i + 1 < steps:
                value, peak = score(i + 1, p, peak)
                coming.append(value)
            for part in lanes(ready[p]):
                weight = jnp.exp2(part - shift)
                total = total + weight
                weights.append(weight.astype(BF16))
            if closing[p]:
                summed = summed + dot(jnp.concatenate(weights, axis=1), pieces[p][0][:, :KVR])
                weights = []
        ready = coming
        total = jnp.sum(total, axis=1, keepdims=True)
        mixed = (summed * (1.0 / total)).astype(BF16)
        level = top + jnp.log2(total)
        h = i * at_once
        maps = jnp.concatenate([value_up[h], value_up[h + 1]], axis=1)
        value = dot(mixed, maps).astype(BF16)
        out[:, h * VDIM : (h + 1) * VDIM] = value[:rows, :VDIM]
        out[:, (h + 1) * VDIM : (h + 2) * VDIM] = value[rows:, VDIM:]
        for k in range(at_once):
            stats = jnp.where(lane == h + k, level[k * rows : (k + 1) * rows], stats)
    high = stats.astype(BF16).astype(F32)
    rest = stats - high
    mid = rest.astype(BF16).astype(F32)
    joined = high + pltpu.roll(mid, n_head, axis=1) + pltpu.roll(rest - mid, 2 * n_head, axis=1)
    out[:, width:] = joined.astype(BF16)


def attend(by, value_up, near, far, span, *queries, keep_far=False):
    rows, n_head = span.shape[0], value_up.shape[0]
    out_shape = [jax.ShapeDtypeStruct((rows, n_head * VDIM + 128), BF16)]
    if keep_far:
        out_shape.append(jax.ShapeDtypeStruct(far.shape, BF16))
    scratch = []
    if by == 2:
        scratch.append(pltpu.VMEM((rows, queries[0].shape[1]), BF16))
        scratch.append(pltpu.VMEM((n_head * rows, WIDE), BF16))
    return pl.pallas_call(
        functools.partial(attend_kernel, by, keep_far),
        out_shape=out_shape,
        in_specs=[VMEM] * (4 + len(queries)),
        out_specs=[VMEM] * len(out_shape),
        scratch_shapes=scratch,
        compiler_params=params(32),
        name="attend_%d" % by,
    )(value_up, near, far, span, *queries)


def output_kernel(n_head, own, one, two, three, weight, exact, send):
    parts = (own, one, two, three)
    width = n_head * VDIM
    levels = []
    for part in parts:
        stat = part[:, width:].astype(F32)
        rest = pltpu.roll(stat, 128 - n_head, axis=1) + pltpu.roll(stat, 128 - 2 * n_head, axis=1)
        levels.append(stat + rest)
    top = functools.reduce(jnp.maximum, levels)
    shares = [jnp.exp2(level - top) for level in levels]
    total = functools.reduce(jnp.add, shares)
    head_of = lax.broadcasted_iota(jnp.int32, (128, width), 0)
    lane_of = lax.broadcasted_iota(jnp.int32, (128, width), 1)
    begin = head_of * VDIM
    spread = jnp.where((lane_of >= begin) & (lane_of < begin + VDIM), 1.0, 0.0).astype(BF16)
    mixed = 0.0
    for part, share in zip(parts, shares):
        share = share / total
        high = share.astype(BF16)
        low = (share - high.astype(F32)).astype(BF16)
        factor = dot(high, spread) + dot(low, spread)
        mixed = mixed + part[:, :width].astype(F32) * factor
    per_head = mixed.astype(BF16)
    block = 512
    for at in range(0, weight.shape[1], block):
        part = dot(per_head, weight[:, at : at + block])
        exact[:, at : at + block] = part
        send[:, at : at + block] = part.astype(BF16)


def project_output(own, one, two, three, w_out):
    rows = own.shape[0]
    depth, cols = w_out.shape
    return pl.pallas_call(
        functools.partial(output_kernel, depth // VDIM),
        out_shape=[
            jax.ShapeDtypeStruct((rows, cols), F32),
            jax.ShapeDtypeStruct((rows, cols), BF16),
        ],
        in_specs=[VMEM] * 5,
        out_specs=[VMEM] * 2,
        compiler_params=params(16),
        name="project_output",
    )(own, one, two, three, w_out)


def expert_kernel(tokens, exact, other, gain, w_gate_t, w_up_t, w_down, keep, send):
    half = keep.shape[1]
    middle = tokens[...].astype(F32) + (exact[...] + other[...].astype(F32))
    middle = middle.astype(BF16).astype(F32)
    mlp_in = rms(middle, gain[...].astype(F32).reshape(1, -1)).astype(BF16)
    gate = dot_nt(mlp_in, w_gate_t[...])
    up = dot_nt(mlp_in, w_up_t[...])
    hidden = (gate / (1.0 + jnp.exp(-gate)) * up).astype(BF16)
    low = dot(hidden, w_down[:, :half])
    high = dot(hidden, w_down[:, half:])
    first = lax.axis_index("tp") == 0
    keep[...] = jnp.where(first, middle[:, :half] + low, middle[:, half:] + high)
    send[...] = jnp.where(first, high, low).astype(BF16)


def expert(tokens, exact, other, gain, w_gate_t, w_up_t, w_down):
    rows, width = tokens.shape
    half = width // 2
    return pl.pallas_call(
        expert_kernel,
        out_shape=[
            jax.ShapeDtypeStruct((rows, half), F32),
            jax.ShapeDtypeStruct((rows, half), BF16),
        ],
        in_specs=[VMEM] * 7,
        out_specs=[VMEM] * 2,
        compiler_params=params(24),
        name="expert",
    )(tokens, exact, other, gain, w_gate_t, w_up_t, w_down)


def on_device(
    tokens,
    attn_gain,
    w_query,
    w_latent,
    kv_gain,
    w_key_up,
    w_value_up,
    w_out,
    mlp_gain,
    w_gate,
    w_up,
    w_down,
    page_pool,
    hit_owner,
    hit_slot,
    fetch_count,
):
    n_store = lax.axis_size("store")
    n_section = lax.axis_size("section")
    n_tp = lax.axis_size("tp")
    rows = tokens.shape[0]
    share = PAGE // (n_section * n_tp)

    swap = [(0, 1), (1, 0)]
    owner = hit_owner[:, :, 0]
    outgoing = pack_pages(owner, hit_slot, jnp.swapaxes(page_pool, 1, 2), share)
    outgoing, early_tokens = lax.optimization_barrier((outgoing, tokens))
    outgoing = outgoing.reshape(n_store, 2, share // 2, MSG)
    arrived = lax.all_to_all(outgoing, "store", split_axis=0, concat_axis=0, tiled=True)
    arrived = arrived.reshape(n_store, share, MSG)

    def shift(value, by):
        pairs = [((z + by) % n_section, z) for z in range(n_section)]
        return lax.ppermute(value, "section", pairs)

    table = rotation_table((hit_owner.shape[1]) * PAGE + n_section * rows)
    query, normed, turns = project(
        fetch_count, early_tokens, attn_gain, jnp.asarray(table), w_query
    )
    next_query, last_query = shift(query, 1), shift(query, -1)
    new_latent, span = project_latent(normed, turns, w_latent.T, kv_gain)
    arrived, next_query, last_query, span = lax.optimization_barrier(
        (arrived, next_query, last_query, span)
    )

    near = build_keys(owner, fetch_count, arrived)
    far = lax.ppermute(near, "tp", swap)

    own_probes, next_probes, last_probes, low, high = make_probes(
        w_key_up, query, next_query, last_query
    )
    far_low, far_high = shift(low, 1), shift(high, -1)

    def partial_for(by, far, *queries, **flags):
        return attend(by, w_value_up, near, far, span, *queries, **flags)

    one, far = partial_for(1, far, next_probes, keep_far=True)
    one, far_low, far_high = lax.optimization_barrier((one, far_low, far_high))
    one = shift(one, -1)
    (two,) = partial_for(2, far, far_low, far_high, w_key_up)
    two, last_probes, one = lax.optimization_barrier((two, last_probes, one))
    two = shift(two, -1)
    (three,) = partial_for(3, far, last_probes)
    three, own_probes, two = lax.optimization_barrier((three, own_probes, two))
    three = shift(three, -3)
    two = shift(two, -1)
    (own,) = partial_for(0, far, own_probes)
    exact, send = project_output(own, one, two, three, w_out)
    incoming = lax.ppermute(send, "tp", swap)
    keep, send = expert(
        tokens,
        exact,
        incoming,
        mlp_gain,
        w_gate.T,
        w_up.T,
        w_down,
    )
    layer_out = (keep + lax.ppermute(send, "tp", swap).astype(F32)).astype(BF16)
    return (layer_out, new_latent.T)


def solution(mesh):
    in_specs = (
        P(("store", "section"), None),
        P(),
        P(None, "tp"),
        P(),
        P(),
        P("tp", None, None),
        P("tp", None, None),
        P("tp", None),
        P(),
        P(None, "tp"),
        P(None, "tp"),
        P("tp", None),
        P("store", None, None),
        P(),
        P(),
        P(),
    )
    out_specs = (P(("store", "section"), "tp"), P(("store", "section"), None))
    return jax.shard_map(
        on_device, mesh=mesh, in_specs=in_specs, out_specs=out_specs, check_vma=False
    )
```

```python
import functools
import math

import jax
import jax.numpy as jnp
import numpy as np
from jax import lax
from jax.experimental import pallas as pl
from jax.experimental.pallas import tpu as pltpu
from jax.sharding import PartitionSpec as P

NOPE = 128
ROPE = 64
KVR = 512
PAGE = 256
LAT = KVR + ROPE
WIDE = KVR + 2 * ROPE
MSG = 2 * LAT
VDIM = 128
EPSILON = 1e-06
ROTARY_BASE = 10000.0
MASKED_SCORE = -1e30
SCALE = (NOPE + ROPE) ** (-0.5) / math.log(2.0)
F32 = jnp.float32
BF16 = jnp.bfloat16
MB = 1024 * 1024

VMEM = pl.BlockSpec(memory_space=pltpu.VMEM)
SMEM = pl.BlockSpec(memory_space=pltpu.SMEM)
HBM = pl.BlockSpec(memory_space=pltpu.HBM)
ANY = pl.BlockSpec(memory_space=pl.ANY)


def params(mb):
    return pltpu.CompilerParams(vmem_limit_bytes=mb * MB)


def dot(a, b):
    return jnp.dot(a, b, preferred_element_type=F32)


def dot_nt(a, b):
    return lax.dot_general(a, b, (((1,), (1,)), ((), ())), preferred_element_type=F32)


def rms(values, gain):
    mean_sq = jnp.mean(values * values, axis=-1, keepdims=True)
    return values * lax.rsqrt(mean_sq + EPSILON) * gain


def turn(values, cosine, sine):
    lane = lax.broadcasted_iota(jnp.int32, values.shape, 1)
    low = (lane & (ROPE // 2)) == 0
    partner = jnp.where(
        low, pltpu.roll(values, 128 - ROPE // 2, axis=1), pltpu.roll(values, ROPE // 2, axis=1)
    )
    return values * cosine + partner * sine


def pack_kernel(owner_src, slot_src, pool_src, out, owner, slot, pool, message, sems):
    group = lax.axis_index("store")
    shard = lax.axis_index("section") * lax.axis_size("tp") + lax.axis_index("tp")
    n_pages, width, window = pool.shape
    n_store, rows, _ = message.shape
    per = window // rows
    pairs = [(owner_src, owner), (slot_src, slot)]
    part = pl.ds(pl.multiple_of((shard // per) * window, window), window)
    for k in range(n_pages // 2):
        at = pl.ds(2 * k, 2)
        pairs.append((pool_src.at[at, :, part], pool.at[at]))
    copies = [
        pltpu.make_async_copy(src, dst, sems.at[i]) for i, (src, dst) in enumerate(pairs)
    ]
    for copy in copies:
        copy.start()
    copies[0].wait()
    copies[1].wait()
    n_list = owner.shape[1]
    held = owner[...] == group
    entry = lax.broadcasted_iota(jnp.int32, held.shape, 1)
    low = jnp.min(jnp.where(held, entry, n_list), axis=1, keepdims=True)
    high = jnp.max(jnp.where(held, entry, -1), axis=1, keepdims=True)
    at_once = n_store // 2
    row = lax.broadcasted_iota(jnp.int32, (rows, 1), 0)
    column = lax.broadcasted_iota(jnp.int32, (at_once * rows, n_pages * rows), 1)
    chosen = {}
    for which, hit in enumerate((low, high)):
        page = jnp.sum(jnp.where(entry == hit, slot[...], 0), axis=1, keepdims=True) * rows
        for to in range(0, n_store, at_once):
            wanted = [
                jnp.broadcast_to(page[g : g + 1], (rows, 1)) + row for g in range(to, to + at_once)
            ]
            wanted = jnp.concatenate(wanted, axis=0)
            chosen[to, which] = jnp.where(column == wanted, 1.0, 0.0).astype(BF16)
    first = (shard % per) * rows
    lane = lax.broadcasted_iota(jnp.int32, (width, window), 1)
    joined = []
    for at in range(0, n_pages, per):
        part = None
        for k in range(per):
            if k % 2 == 0:
                copies[2 + (at + k) // 2].wait()
            moved = pltpu.roll(pool[at + k].astype(F32), (k * rows - first + window) % window, axis=1)
            part = moved if part is None else jnp.where(lane >= k * rows, moved, part)
        joined.append(part.astype(BF16))
    stage = jnp.concatenate(joined, axis=1)
    sends = []
    for to in range(0, n_store, at_once):
        at = pl.ds(to, at_once)
        taken = [dot_nt(chosen[to, which], stage) for which in range(2)]
        ropes = jnp.concatenate([part[:, KVR:] for part in taken], axis=1)
        for which, part in enumerate(taken):
            message[at, :, which * KVR : (which + 1) * KVR] = (
                part[:, :KVR].astype(BF16).reshape(at_once, rows, KVR)
            )
        message[at, :, 2 * KVR :] = ropes.astype(BF16).reshape(at_once, rows, 2 * ROPE)
        send = pltpu.make_async_copy(message.at[at], out.at[at], sems.at[len(copies) + len(sends)])
        send.start()
        sends.append(send)
    for send in sends:
        send.wait()


def pack_pages(owner, slot, pool_t, rows):
    n_store, n_pages = owner.shape[0], pool_t.shape[0]
    return pl.pallas_call(
        pack_kernel,
        out_shape=jax.ShapeDtypeStruct((n_store, rows, MSG), BF16),
        in_specs=[HBM] * 3,
        out_specs=HBM,
        scratch_shapes=[
            pltpu.VMEM(owner.shape, jnp.int32),
            pltpu.VMEM(slot.shape, jnp.int32),
            pltpu.VMEM((*pool_t.shape[:2], 128), BF16),
            pltpu.VMEM((n_store, rows, MSG), BF16),
            pltpu.SemaphoreType.DMA((4 + n_pages // 2,)),
        ],
        compiler_params=params(60),
        name="pack_pages",
    )(owner, slot, pool_t)


def keys_kernel(owner, count, pages, out, seen):
    rows = pages.shape[1]
    group = lax.axis_index("store")
    lane = lax.broadcasted_iota(jnp.int32, (rows, 128), 1)
    for k in range(pages.shape[0]):
        seen[k] = 0
    for j in range(owner.shape[1]):
        source = owner[group, j]
        second = seen[source] > 0
        seen[source] = 1
        bias = jnp.where(j < count[group], 0.0, MASKED_SCORE)
        row = pages[source]
        at = pl.ds(j * rows, rows)
        out[at, :KVR] = jnp.where(second, row[:, KVR : 2 * KVR], row[:, :KVR])
        pair = row[:, 2 * KVR :].astype(F32)
        rot = jnp.where(second, pltpu.roll(pair, ROPE, axis=1), pair)
        last = jnp.where(lane == ROPE, bias, 0.0)
        out[at, KVR:] = jnp.where(lane < ROPE, rot, last).astype(BF16)


def build_keys(owner, count, pages):
    n_keys = owner.shape[1] * pages.shape[1]
    return pl.pallas_call(
        keys_kernel,
        out_shape=jax.ShapeDtypeStruct((n_keys, WIDE), BF16),
        in_specs=[SMEM, SMEM, VMEM],
        out_specs=VMEM,
        scratch_shapes=[pltpu.SMEM((pages.shape[0],), jnp.int32)],
        compiler_params=params(24),
        name="build_keys",
    )(owner, count, pages)


def rotation_table(n_rows):
    half = ROPE // 2
    freq = np.float32(ROTARY_BASE) ** (-(np.arange(half, dtype=np.float32) / np.float32(half)))
    angle = np.arange(n_rows, dtype=np.float32)[:, None] * freq.astype(np.float32)[None, :]
    angle = angle.astype(np.float64)
    parts = [np.cos(angle), np.cos(angle), -np.sin(angle), np.sin(angle)]
    return np.concatenate(parts, axis=1).astype(np.float32)


def project_kernel(
    count, tokens_src, gain, table, w_query_src, query, normed, turns, tokens, w_query, total, sems
):
    rows = tokens.shape[0]
    group, section = lax.axis_index("store"), lax.axis_index("section")
    start = pl.multiple_of(count[group] * PAGE + section * rows, rows)
    pairs = [(tokens_src, tokens), (table.at[pl.ds(start, rows), :], turns)]
    pieces = 8
    depth = w_query.shape[0] // pieces
    for k in range(pieces):
        at = pl.ds(k * depth, depth)
        pairs.append((w_query_src.at[at, :], w_query.at[at, :]))
    copies = [
        pltpu.make_async_copy(src, dst, sems.at[i]) for i, (src, dst) in enumerate(pairs)
    ]
    for copy in copies:
        copy.start()
    copies[0].wait()
    normed[...] = rms(tokens[...].astype(F32), gain[...].astype(F32).reshape(1, -1)).astype(BF16)
    copies[1].wait()
    cosine, sine = turns[:, :ROPE], turns[:, ROPE:]
    cosine = jnp.concatenate([cosine, cosine], axis=1)
    sine = jnp.concatenate([sine, sine], axis=1)
    for k in range(0, pieces, 2):
        copies[2 + k].wait()
        copies[3 + k].wait()
        at = slice(k * depth, (k + 2) * depth)
        part = dot(normed[:, at], w_query[at, :])
        total[...] = part if k == 0 else total[...] + part
    head = NOPE + ROPE
    for at in range(0, query.shape[1], 2 * head):
        part = total[:, at : at + 2 * head].astype(BF16).astype(F32)
        query[:, at : at + NOPE] = part[:, :NOPE].astype(BF16)
        query[:, at + NOPE : at + 2 * NOPE] = part[:, head : head + NOPE].astype(BF16)
        pair = jnp.concatenate([part[:, NOPE:head], part[:, head + NOPE :]], axis=1)
        query[:, at + 2 * NOPE : at + 2 * head] = (turn(pair, cosine, sine) * SCALE).astype(BF16)


def project(count, tokens, gain, table, w_query):
    rows, width = tokens.shape
    cols = w_query.shape[1]
    return pl.pallas_call(
        project_kernel,
        out_shape=[
            jax.ShapeDtypeStruct((rows, cols), BF16),
            jax.ShapeDtypeStruct(tokens.shape, BF16),
            jax.ShapeDtypeStruct((rows, 2 * ROPE), F32),
        ],
        in_specs=[SMEM, HBM, VMEM] + [HBM] * 2,
        out_specs=[VMEM] * 3,
        scratch_shapes=[
            pltpu.VMEM(tokens.shape, BF16),
            pltpu.VMEM(w_query.shape, BF16),
            pltpu.VMEM((rows, cols), F32),
            pltpu.SemaphoreType.DMA((10,)),
        ],
        compiler_params=params(60),
        name="project",
    )(count, tokens, gain, table, w_query)


def latent_kernel(
    normed, turns, w_latent_t, kv_gain, query, key_up, new_latent, span, probes
):
    cosine, sine = turns[:, :ROPE], turns[:, ROPE:]
    cosine = jnp.concatenate([cosine, cosine], axis=1)
    sine = jnp.concatenate([sine, sine], axis=1)
    raw = dot_nt(normed[...], w_latent_t[...])
    latent = rms(raw[:, :KVR], kv_gain[...].astype(F32).reshape(1, -1)).astype(BF16)
    pair = jnp.concatenate([raw[:, KVR:], raw[:, KVR:]], axis=1)
    turned = turn(pair, cosine, sine)
    new_latent[:KVR, :] = latent.astype(F32).T.astype(BF16)
    new_latent[KVR:, :] = turned.T[:ROPE].astype(BF16)
    lane = lax.broadcasted_iota(jnp.int32, turned.shape, 1)
    span[:, :KVR] = latent
    span[:, KVR:] = jnp.where(lane < ROPE, turned, 0.0).astype(BF16)
    fill_probes(query, key_up, probes)


def project_latent(normed, turns, w_latent_t, kv_gain, query, key_up):
    rows = normed.shape[0]
    return pl.pallas_call(
        latent_kernel,
        out_shape=[
            jax.ShapeDtypeStruct((LAT, rows), BF16),
            jax.ShapeDtypeStruct((rows, WIDE), BF16),
            jax.ShapeDtypeStruct((key_up.shape[0] * rows, WIDE), BF16),
        ],
        in_specs=[VMEM] * 6,
        out_specs=[VMEM] * 3,
        compiler_params=params(20),
        name="project_latent",
    )(normed, turns, w_latent_t, kv_gain, query, key_up)


def fill_probes(query, key_up, probes):
    rows = query.shape[0]
    pair_width = 2 * (NOPE + ROPE)
    lane = lax.broadcasted_iota(jnp.int32, (rows, 2 * NOPE), 1)
    rope_lane = lane[:, : 2 * ROPE]
    for h in range(0, key_up.shape[0], 2):
        base = (h // 2) * pair_width
        nope = query[:, base : base + 2 * NOPE].astype(F32)
        both = jnp.concatenate(
            [jnp.where(lane < NOPE, nope, 0.0), jnp.where(lane < NOPE, 0.0, nope)], axis=0
        )
        maps = jnp.concatenate([key_up[h], key_up[h + 1]], axis=1)
        at = pl.ds(h * rows, 2 * rows)
        probes[at, :KVR] = (dot_nt(both.astype(BF16), maps) * SCALE).astype(BF16)
        pair = query[:, base + 2 * NOPE : base + pair_width].astype(F32)
        pair = jnp.concatenate([pair, pltpu.roll(pair, ROPE, axis=1)], axis=0)
        rope_lanes = jnp.concatenate([rope_lane, rope_lane], axis=0)
        one = jnp.where(rope_lanes == ROPE, 1.0, 0.0)
        probes[at, KVR:] = jnp.where(rope_lanes < ROPE, pair, one).astype(BF16)


def probes_kernel(key_up, ahead_src, behind_src, ahead_probes, behind_probes, ahead, behind, sems):
    pairs = ((ahead_src, ahead), (behind_src, behind))
    copies = [
        pltpu.make_async_copy(src, dst, sems.at[i]) for i, (src, dst) in enumerate(pairs)
    ]
    for copy in copies:
        copy.start()
    for copy, query, probes in zip(copies, (ahead, behind), (ahead_probes, behind_probes)):
        copy.wait()
        fill_probes(query, key_up, probes)


def make_probes(key_up, ahead, behind):
    rows, width = ahead.shape
    probes = jax.ShapeDtypeStruct((key_up.shape[0] * rows, WIDE), BF16)
    return pl.pallas_call(
        probes_kernel,
        out_shape=[probes] * 2,
        in_specs=[VMEM] + [ANY] * 2,
        out_specs=[VMEM] * 2,
        scratch_shapes=[pltpu.VMEM((rows, width), BF16)] * 2 + [pltpu.SemaphoreType.DMA((2,))],
        compiler_params=params(20),
        name="make_probes",
    )(key_up, ahead, behind)


def attend_kernel(by, keep_far, value_up, near, arrived, span, *refs):
    far = arrived
    if by == 2:
        low, high, key_up, out, query, probes = refs
        query[: low.shape[0], :] = low[...]
        query[low.shape[0] :, :] = high[...]
        fill_probes(query, key_up, probes)
    elif keep_far:
        probes, out, far = refs
        far[...] = arrived[...]
    else:
        probes, out = refs
    n_head, rows = value_up.shape[0], out.shape[0]
    blocks = (near, far, span)
    lane = lax.broadcasted_iota(jnp.int32, (rows, 128), 1)
    at_once = 2
    tile = at_once * rows
    steps = n_head // at_once
    width = n_head * NOPE

    if by == 0:
        row_of = lax.broadcasted_iota(jnp.int32, (tile, rows), 0) & (rows - 1)
        key_of = lax.broadcasted_iota(jnp.int32, (tile, rows), 1)
        hide = jnp.where(key_of <= row_of, 0.0, MASKED_SCORE)
    else:
        later = lax.axis_index("section") + by < lax.axis_size("section")
        hide = jnp.where(later, 0.0, MASKED_SCORE)

    pieces, closing = [], []
    for block in blocks:
        step = min(256, block.shape[0])
        for at in range(0, block.shape[0], step):
            pieces.append((block, at, step))
            closing.append(at + step == block.shape[0])

    def lanes(value):
        return [value[:, at : at + 128] for at in range(0, value.shape[1], 128)]

    def score(i, p, peak):
        block, at, size = pieces[p]
        value = dot_nt(probes[i * tile : (i + 1) * tile, :], block[at : at + size, :])
        if block is span:
            value = value + hide
        return value, functools.reduce(jnp.maximum, lanes(value), peak)

    stats = jnp.zeros((rows, 128), F32)
    lowest = jnp.full((tile, 128), MASKED_SCORE, F32)
    ready, peak = [], lowest
    for p in range(len(pieces)):
        value, peak = score(0, p, peak)
        ready.append(value)
    for i in range(steps):
        top = jnp.max(peak, axis=1, keepdims=True)
        shift = jnp.broadcast_to(top, (tile, 128))
        total, summed = jnp.zeros((tile, 128), F32), 0.0
        coming, peak, weights = [], lowest, []
        for p in range(len(pieces)):
            if i + 1 < steps:
                value, peak = score(i + 1, p, peak)
                coming.append(value)
            for part in lanes(ready[p]):
                weight = jnp.exp2(part - shift)
                total = total + weight
                weights.append(weight.astype(BF16))
            if closing[p]:
                summed = summed + dot(jnp.concatenate(weights, axis=1), pieces[p][0][:, :KVR])
                weights = []
        ready = coming
        total = jnp.sum(total, axis=1, keepdims=True)
        mixed = (summed * (1.0 / total)).astype(BF16)
        level = top + jnp.log2(total)
        h = i * at_once
        maps = jnp.concatenate([value_up[h], value_up[h + 1]], axis=1)
        value = dot(mixed, maps).astype(BF16)
        out[:, h * VDIM : (h + 1) * VDIM] = value[:rows, :VDIM]
        out[:, (h + 1) * VDIM : (h + 2) * VDIM] = value[rows:, VDIM:]
        for k in range(at_once):
            stats = jnp.where(lane == h + k, level[k * rows : (k + 1) * rows], stats)
    high = stats.astype(BF16).astype(F32)
    rest = stats - high
    mid = rest.astype(BF16).astype(F32)
    joined = high + pltpu.roll(mid, n_head, axis=1) + pltpu.roll(rest - mid, 2 * n_head, axis=1)
    out[:, width:] = joined.astype(BF16)


def attend(by, value_up, near, far, span, *queries, keep_far=False):
    rows, n_head = span.shape[0], value_up.shape[0]
    out_shape = [jax.ShapeDtypeStruct((rows, n_head * VDIM + 128), BF16)]
    if keep_far:
        out_shape.append(jax.ShapeDtypeStruct(far.shape, BF16))
    scratch = []
    if by == 2:
        scratch.append(pltpu.VMEM((rows, queries[0].shape[1]), BF16))
        scratch.append(pltpu.VMEM((n_head * rows, WIDE), BF16))
    return pl.pallas_call(
        functools.partial(attend_kernel, by, keep_far),
        out_shape=out_shape,
        in_specs=[VMEM] * (4 + len(queries)),
        out_specs=[VMEM] * len(out_shape),
        scratch_shapes=scratch,
        compiler_params=params(32),
        name="attend_%d" % by,
    )(value_up, near, far, span, *queries)


def output_kernel(n_head, own, one, two, three, weight, exact, send):
    parts = (own, one, two, three)
    width = n_head * VDIM
    levels = []
    for part in parts:
        stat = part[:, width:].astype(F32)
        rest = pltpu.roll(stat, 128 - n_head, axis=1) + pltpu.roll(stat, 128 - 2 * n_head, axis=1)
        levels.append(stat + rest)
    top = functools.reduce(jnp.maximum, levels)
    shares = [jnp.exp2(level - top) for level in levels]
    total = functools.reduce(jnp.add, shares)
    head_of = lax.broadcasted_iota(jnp.int32, (128, width), 0)
    lane_of = lax.broadcasted_iota(jnp.int32, (128, width), 1)
    begin = head_of * VDIM
    spread = jnp.where((lane_of >= begin) & (lane_of < begin + VDIM), 1.0, 0.0).astype(BF16)
    mixed = 0.0
    for part, share in zip(parts, shares):
        share = share / total
        high = share.astype(BF16)
        low = (share - high.astype(F32)).astype(BF16)
        factor = dot(high, spread) + dot(low, spread)
        mixed = mixed + part[:, :width].astype(F32) * factor
    per_head = mixed.astype(BF16)
    block = 512
    for at in range(0, weight.shape[1], block):
        part = dot(per_head, weight[:, at : at + block])
        exact[:, at : at + block] = part
        send[:, at : at + block] = part.astype(BF16)


def project_output(own, one, two, three, w_out):
    rows = own.shape[0]
    depth, cols = w_out.shape
    return pl.pallas_call(
        functools.partial(output_kernel, depth // VDIM),
        out_shape=[
            jax.ShapeDtypeStruct((rows, cols), F32),
            jax.ShapeDtypeStruct((rows, cols), BF16),
        ],
        in_specs=[VMEM] * 5,
        out_specs=[VMEM] * 2,
        compiler_params=params(16),
        name="project_output",
    )(own, one, two, three, w_out)


def expert_kernel(tokens, exact, other, gain, w_gate_t, w_up_t, w_down, keep, send):
    half = keep.shape[1]
    middle = tokens[...].astype(F32) + (exact[...] + other[...].astype(F32))
    middle = middle.astype(BF16).astype(F32)
    mlp_in = rms(middle, gain[...].astype(F32).reshape(1, -1)).astype(BF16)
    gate = dot_nt(mlp_in, w_gate_t[...])
    up = dot_nt(mlp_in, w_up_t[...])
    hidden = (gate / (1.0 + jnp.exp(-gate)) * up).astype(BF16)
    low = dot(hidden, w_down[:, :half])
    high = dot(hidden, w_down[:, half:])
    first = lax.axis_index("tp") == 0
    keep[...] = jnp.where(first, middle[:, :half] + low, middle[:, half:] + high)
    send[...] = jnp.where(first, high, low).astype(BF16)


def expert(tokens, exact, other, gain, w_gate_t, w_up_t, w_down):
    rows, width = tokens.shape
    half = width // 2
    return pl.pallas_call(
        expert_kernel,
        out_shape=[
            jax.ShapeDtypeStruct((rows, half), F32),
            jax.ShapeDtypeStruct((rows, half), BF16),
        ],
        in_specs=[VMEM] * 7,
        out_specs=[VMEM] * 2,
        compiler_params=params(24),
        name="expert",
    )(tokens, exact, other, gain, w_gate_t, w_up_t, w_down)


def on_device(
    tokens,
    attn_gain,
    w_query,
    w_latent,
    kv_gain,
    w_key_up,
    w_value_up,
    w_out,
    mlp_gain,
    w_gate,
    w_up,
    w_down,
    page_pool,
    hit_owner,
    hit_slot,
    fetch_count,
):
    n_store = lax.axis_size("store")
    n_section = lax.axis_size("section")
    n_tp = lax.axis_size("tp")
    rows = tokens.shape[0]
    share = PAGE // (n_section * n_tp)

    swap = [(0, 1), (1, 0)]
    owner = hit_owner[:, :, 0]
    outgoing = pack_pages(owner, hit_slot, jnp.swapaxes(page_pool, 1, 2), share)
    outgoing, early_tokens = lax.optimization_barrier((outgoing, tokens))
    outgoing = outgoing.reshape(n_store, 2, share // 2, MSG)
    arrived = lax.all_to_all(outgoing, "store", split_axis=0, concat_axis=0, tiled=True)
    arrived = arrived.reshape(n_store, share, MSG)

    def shift(value, by):
        pairs = [((z + by) % n_section, z) for z in range(n_section)]
        return lax.ppermute(value, "section", pairs)

    table = rotation_table((hit_owner.shape[1]) * PAGE + n_section * rows)
    query, normed, turns = project(
        fetch_count, early_tokens, attn_gain, jnp.asarray(table), w_query
    )
    next_query, last_query = shift(query, 1), shift(query, -1)
    new_latent, span, own_probes = project_latent(
        normed, turns, w_latent.T, kv_gain, query, w_key_up
    )
    arrived, next_query, last_query, span = lax.optimization_barrier(
        (arrived, next_query, last_query, span)
    )

    cut = rows // 2
    far_low, far_high = shift(next_query[:cut], 1), shift(last_query[cut:], -1)

    near = build_keys(owner, fetch_count, arrived)
    far = lax.ppermute(near, "tp", swap)

    next_probes, last_probes = make_probes(w_key_up, next_query, last_query)

    def partial_for(by, far, *queries, **flags):
        return attend(by, w_value_up, near, far, span, *queries, **flags)

    one, far = partial_for(1, far, next_probes, keep_far=True)
    one, far_low, far_high = lax.optimization_barrier((one, far_low, far_high))
    one = shift(one, -1)
    (two,) = partial_for(2, far, far_low, far_high, w_key_up)
    two, last_probes, one = lax.optimization_barrier((two, last_probes, one))
    two = shift(two, -1)
    (three,) = partial_for(3, far, last_probes)
    three, own_probes, two = lax.optimization_barrier((three, own_probes, two))
    three = shift(three, -3)
    two = shift(two, -1)
    (own,) = partial_for(0, far, own_probes)
    exact, send = project_output(own, one, two, three, w_out)
    incoming = lax.ppermute(send, "tp", swap)
    keep, send = expert(
        tokens,
        exact,
        incoming,
        mlp_gain,
        w_gate.T,
        w_up.T,
        w_down,
    )
    layer_out = (keep + lax.ppermute(send, "tp", swap).astype(F32)).astype(BF16)
    return (layer_out, new_latent.T)


def solution(mesh):
    in_specs = (
        P(("store", "section"), None),
        P(),
        P(None, "tp"),
        P(),
        P(),
        P("tp", None, None),
        P("tp", None, None),
        P("tp", None),
        P(),
        P(None, "tp"),
        P(None, "tp"),
        P("tp", None),
        P("store", None, None),
        P(),
        P(),
        P(),
    )
    out_specs = (P(("store", "section"), "tp"), P(("store", "section"), None))
    return jax.shard_map(
        on_device, mesh=mesh, in_specs=in_specs, out_specs=out_specs, check_vma=False
    )
```

```python
import functools
import math

import jax
import jax.numpy as jnp
import numpy as np
from jax import lax
from jax.experimental import pallas as pl
from jax.experimental.pallas import tpu as pltpu
from jax.sharding import PartitionSpec as P

NOPE = 128
ROPE = 64
KVR = 512
PAGE = 256
LAT = KVR + ROPE
WIDE = KVR + 2 * ROPE
MSG = 2 * LAT
VDIM = 128
EPSILON = 1e-06
ROTARY_BASE = 10000.0
MASKED_SCORE = -1e30
SCALE = (NOPE + ROPE) ** (-0.5) / math.log(2.0)
F32 = jnp.float32
BF16 = jnp.bfloat16
MB = 1024 * 1024

VMEM = pl.BlockSpec(memory_space=pltpu.VMEM)
SMEM = pl.BlockSpec(memory_space=pltpu.SMEM)
HBM = pl.BlockSpec(memory_space=pltpu.HBM)
ANY = pl.BlockSpec(memory_space=pl.ANY)


def params(mb):
    return pltpu.CompilerParams(vmem_limit_bytes=mb * MB)


def dot(a, b):
    return jnp.dot(a, b, preferred_element_type=F32)


def dot_nt(a, b):
    return lax.dot_general(a, b, (((1,), (1,)), ((), ())), preferred_element_type=F32)


def rms(values, gain):
    mean_sq = jnp.mean(values * values, axis=-1, keepdims=True)
    return values * lax.rsqrt(mean_sq + EPSILON) * gain


def turn(values, cosine, sine):
    lane = lax.broadcasted_iota(jnp.int32, values.shape, 1)
    low = (lane & (ROPE // 2)) == 0
    partner = jnp.where(
        low, pltpu.roll(values, 128 - ROPE // 2, axis=1), pltpu.roll(values, ROPE // 2, axis=1)
    )
    return values * cosine + partner * sine


def pack_kernel(owner_src, slot_src, pool_src, out, owner, slot, pool, message, sems):
    group = lax.axis_index("store")
    shard = lax.axis_index("section") * lax.axis_size("tp") + lax.axis_index("tp")
    n_pages, width, window = pool.shape
    n_store, rows, _ = message.shape
    per = window // rows
    pairs = [(owner_src, owner), (slot_src, slot)]
    part = pl.ds(pl.multiple_of((shard // per) * window, window), window)
    for k in range(n_pages // 2):
        at = pl.ds(2 * k, 2)
        pairs.append((pool_src.at[at, :, part], pool.at[at]))
    copies = [
        pltpu.make_async_copy(src, dst, sems.at[i]) for i, (src, dst) in enumerate(pairs)
    ]
    for copy in copies:
        copy.start()
    copies[0].wait()
    copies[1].wait()
    n_list = owner.shape[1]
    held = owner[...] == group
    entry = lax.broadcasted_iota(jnp.int32, held.shape, 1)
    low = jnp.min(jnp.where(held, entry, n_list), axis=1, keepdims=True)
    high = jnp.max(jnp.where(held, entry, -1), axis=1, keepdims=True)
    at_once = n_store // 2
    row = lax.broadcasted_iota(jnp.int32, (rows, 1), 0)
    column = lax.broadcasted_iota(jnp.int32, (at_once * rows, n_pages * rows), 1)
    chosen = {}
    for which, hit in enumerate((low, high)):
        page = jnp.sum(jnp.where(entry == hit, slot[...], 0), axis=1, keepdims=True) * rows
        for to in range(0, n_store, at_once):
            wanted = [
                jnp.broadcast_to(page[g : g + 1], (rows, 1)) + row for g in range(to, to + at_once)
            ]
            wanted = jnp.concatenate(wanted, axis=0)
            chosen[to, which] = jnp.where(column == wanted, 1.0, 0.0).astype(BF16)
    first = (shard % per) * rows
    lane = lax.broadcasted_iota(jnp.int32, (width, window), 1)
    joined = []
    for at in range(0, n_pages, per):
        part = None
        for k in range(per):
            if k % 2 == 0:
                copies[2 + (at + k) // 2].wait()
            moved = pltpu.roll(pool[at + k].astype(F32), (k * rows - first + window) % window, axis=1)
            part = moved if part is None else jnp.where(lane >= k * rows, moved, part)
        joined.append(part.astype(BF16))
    stage = jnp.concatenate(joined, axis=1)
    sends = []
    for to in range(0, n_store, at_once):
        at = pl.ds(to, at_once)
        taken = [dot_nt(chosen[to, which], stage) for which in range(2)]
        ropes = jnp.concatenate([part[:, KVR:] for part in taken], axis=1)
        for which, part in enumerate(taken):
            message[at, :, which * KVR : (which + 1) * KVR] = (
                part[:, :KVR].astype(BF16).reshape(at_once, rows, KVR)
            )
        message[at, :, 2 * KVR :] = ropes.astype(BF16).reshape(at_once, rows, 2 * ROPE)
        send = pltpu.make_async_copy(message.at[at], out.at[at], sems.at[len(copies) + len(sends)])
        send.start()
        sends.append(send)
    for send in sends:
        send.wait()


def pack_pages(owner, slot, pool_t, rows):
    n_store, n_pages = owner.shape[0], pool_t.shape[0]
    return pl.pallas_call(
        pack_kernel,
        out_shape=jax.ShapeDtypeStruct((n_store, rows, MSG), BF16),
        in_specs=[HBM] * 3,
        out_specs=HBM,
        scratch_shapes=[
            pltpu.VMEM(owner.shape, jnp.int32),
            pltpu.VMEM(slot.shape, jnp.int32),
            pltpu.VMEM((*pool_t.shape[:2], 128), BF16),
            pltpu.VMEM((n_store, rows, MSG), BF16),
            pltpu.SemaphoreType.DMA((4 + n_pages // 2,)),
        ],
        compiler_params=params(60),
        name="pack_pages",
    )(owner, slot, pool_t)


def keys_kernel(owner, count, pages, out, seen):
    rows = pages.shape[1]
    group = lax.axis_index("store")
    lane = lax.broadcasted_iota(jnp.int32, (rows, 128), 1)
    for k in range(pages.shape[0]):
        seen[k] = 0
    for j in range(owner.shape[1]):
        source = owner[group, j]
        second = seen[source] > 0
        seen[source] = 1
        bias = jnp.where(j < count[group], 0.0, MASKED_SCORE)
        row = pages[source]
        at = pl.ds(j * rows, rows)
        out[at, :KVR] = jnp.where(second, row[:, KVR : 2 * KVR], row[:, :KVR])
        pair = row[:, 2 * KVR :].astype(F32)
        rot = jnp.where(second, pltpu.roll(pair, ROPE, axis=1), pair)
        last = jnp.where(lane == ROPE, bias, 0.0)
        out[at, KVR:] = jnp.where(lane < ROPE, rot, last).astype(BF16)


def build_keys(owner, count, pages):
    n_keys = owner.shape[1] * pages.shape[1]
    return pl.pallas_call(
        keys_kernel,
        out_shape=jax.ShapeDtypeStruct((n_keys, WIDE), BF16),
        in_specs=[SMEM, SMEM, VMEM],
        out_specs=VMEM,
        scratch_shapes=[pltpu.SMEM((pages.shape[0],), jnp.int32)],
        compiler_params=params(24),
        name="build_keys",
    )(owner, count, pages)


def rotation_table(n_rows):
    half = ROPE // 2
    freq = np.float32(ROTARY_BASE) ** (-(np.arange(half, dtype=np.float32) / np.float32(half)))
    angle = np.arange(n_rows, dtype=np.float32)[:, None] * freq.astype(np.float32)[None, :]
    angle = angle.astype(np.float64)
    parts = [np.cos(angle), np.cos(angle), -np.sin(angle), np.sin(angle)]
    return np.concatenate(parts, axis=1).astype(np.float32)


def project_kernel(
    count, tokens_src, gain, table, w_query_src, query, normed, turns, tokens, w_query, total, sems
):
    rows = tokens.shape[0]
    group, section = lax.axis_index("store"), lax.axis_index("section")
    start = pl.multiple_of(count[group] * PAGE + section * rows, rows)
    pairs = [(tokens_src, tokens), (table.at[pl.ds(start, rows), :], turns)]
    pieces = 8
    depth = w_query.shape[0] // pieces
    for k in range(pieces):
        at = pl.ds(k * depth, depth)
        pairs.append((w_query_src.at[at, :], w_query.at[at, :]))
    copies = [
        pltpu.make_async_copy(src, dst, sems.at[i]) for i, (src, dst) in enumerate(pairs)
    ]
    for copy in copies:
        copy.start()
    copies[0].wait()
    normed[...] = rms(tokens[...].astype(F32), gain[...].astype(F32).reshape(1, -1)).astype(BF16)
    copies[1].wait()
    cosine, sine = turns[:, :ROPE], turns[:, ROPE:]
    cosine = jnp.concatenate([cosine, cosine], axis=1)
    sine = jnp.concatenate([sine, sine], axis=1)
    for k in range(0, pieces, 2):
        copies[2 + k].wait()
        copies[3 + k].wait()
        at = slice(k * depth, (k + 2) * depth)
        part = dot(normed[:, at], w_query[at, :])
        total[...] = part if k == 0 else total[...] + part
    head = NOPE + ROPE
    for at in range(0, query.shape[1], 2 * head):
        part = total[:, at : at + 2 * head].astype(BF16).astype(F32)
        query[:, at : at + NOPE] = part[:, :NOPE].astype(BF16)
        query[:, at + NOPE : at + 2 * NOPE] = part[:, head : head + NOPE].astype(BF16)
        pair = jnp.concatenate([part[:, NOPE:head], part[:, head + NOPE :]], axis=1)
        query[:, at + 2 * NOPE : at + 2 * head] = (turn(pair, cosine, sine) * SCALE).astype(BF16)


def project(count, tokens, gain, table, w_query):
    rows, width = tokens.shape
    cols = w_query.shape[1]
    return pl.pallas_call(
        project_kernel,
        out_shape=[
            jax.ShapeDtypeStruct((rows, cols), BF16),
            jax.ShapeDtypeStruct(tokens.shape, BF16),
            jax.ShapeDtypeStruct((rows, 2 * ROPE), F32),
        ],
        in_specs=[SMEM, HBM, VMEM] + [HBM] * 2,
        out_specs=[VMEM] * 3,
        scratch_shapes=[
            pltpu.VMEM(tokens.shape, BF16),
            pltpu.VMEM(w_query.shape, BF16),
            pltpu.VMEM((rows, cols), F32),
            pltpu.SemaphoreType.DMA((10,)),
        ],
        compiler_params=params(60),
        name="project",
    )(count, tokens, gain, table, w_query)


def latent_kernel(
    normed, turns, w_latent_t, kv_gain, query, key_up, new_latent, span, probes
):
    cosine, sine = turns[:, :ROPE], turns[:, ROPE:]
    cosine = jnp.concatenate([cosine, cosine], axis=1)
    sine = jnp.concatenate([sine, sine], axis=1)
    raw = dot_nt(normed[...], w_latent_t[...])
    latent = rms(raw[:, :KVR], kv_gain[...].astype(F32).reshape(1, -1)).astype(BF16)
    pair = jnp.concatenate([raw[:, KVR:], raw[:, KVR:]], axis=1)
    turned = turn(pair, cosine, sine)
    new_latent[:KVR, :] = latent.astype(F32).T.astype(BF16)
    new_latent[KVR:, :] = turned.T[:ROPE].astype(BF16)
    lane = lax.broadcasted_iota(jnp.int32, turned.shape, 1)
    span[:, :KVR] = latent
    span[:, KVR:] = jnp.where(lane < ROPE, turned, 0.0).astype(BF16)
    fill_probes(query, key_up, probes)


def project_latent(normed, turns, w_latent_t, kv_gain, query, key_up):
    rows = normed.shape[0]
    return pl.pallas_call(
        latent_kernel,
        out_shape=[
            jax.ShapeDtypeStruct((LAT, rows), BF16),
            jax.ShapeDtypeStruct((rows, WIDE), BF16),
            jax.ShapeDtypeStruct((key_up.shape[0] * rows, WIDE), BF16),
        ],
        in_specs=[VMEM] * 6,
        out_specs=[VMEM] * 3,
        compiler_params=params(20),
        name="project_latent",
    )(normed, turns, w_latent_t, kv_gain, query, key_up)


def fill_probes(query, key_up, probes):
    rows = query.shape[0]
    pair_width = 2 * (NOPE + ROPE)
    lane = lax.broadcasted_iota(jnp.int32, (rows, 2 * NOPE), 1)
    rope_lane = lane[:, : 2 * ROPE]
    for h in range(0, key_up.shape[0], 2):
        base = (h // 2) * pair_width
        nope = query[:, base : base + 2 * NOPE].astype(F32)
        both = jnp.concatenate(
            [jnp.where(lane < NOPE, nope, 0.0), jnp.where(lane < NOPE, 0.0, nope)], axis=0
        )
        maps = jnp.concatenate([key_up[h], key_up[h + 1]], axis=1)
        at = pl.ds(h * rows, 2 * rows)
        probes[at, :KVR] = (dot_nt(both.astype(BF16), maps) * SCALE).astype(BF16)
        pair = query[:, base + 2 * NOPE : base + pair_width].astype(F32)
        pair = jnp.concatenate([pair, pltpu.roll(pair, ROPE, axis=1)], axis=0)
        rope_lanes = jnp.concatenate([rope_lane, rope_lane], axis=0)
        one = jnp.where(rope_lanes == ROPE, 1.0, 0.0)
        probes[at, KVR:] = jnp.where(rope_lanes < ROPE, pair, one).astype(BF16)


def attend_kernel(by, keep_far, value_up, near, arrived, span, *refs):
    far = arrived
    if by == 0:
        probes, out = refs
    else:
        count = 2 if by == 2 else 1
        parts, (key_up, out), refs = refs[:count], refs[count : count + 2], refs[count + 2 :]
        if keep_far:
            far, refs = refs[0], refs[1:]
        query, probes, sems = refs
        height = query.shape[0] // count
        copies = [
            pltpu.make_async_copy(part, query.at[pl.ds(k * height, height), :], sems.at[k])
            for k, part in enumerate(parts)
        ]
        for copy in copies:
            copy.start()
        if keep_far:
            far[...] = arrived[...]
        for copy in copies:
            copy.wait()
        fill_probes(query, key_up, probes)
    n_head, rows = value_up.shape[0], out.shape[0]
    blocks = (near, far, span)
    lane = lax.broadcasted_iota(jnp.int32, (rows, 128), 1)
    at_once = 2
    tile = at_once * rows
    steps = n_head // at_once
    width = n_head * NOPE

    if by == 0:
        row_of = lax.broadcasted_iota(jnp.int32, (tile, rows), 0) & (rows - 1)
        key_of = lax.broadcasted_iota(jnp.int32, (tile, rows), 1)
        hide = jnp.where(key_of <= row_of, 0.0, MASKED_SCORE)
    else:
        later = lax.axis_index("section") + by < lax.axis_size("section")
        hide = jnp.where(later, 0.0, MASKED_SCORE)

    pieces, closing = [], []
    for block in blocks:
        step = min(256, block.shape[0])
        for at in range(0, block.shape[0], step):
            pieces.append((block, at, step))
            closing.append(at + step == block.shape[0])

    def lanes(value):
        return [value[:, at : at + 128] for at in range(0, value.shape[1], 128)]

    def score(i, p, peak):
        block, at, size = pieces[p]
        value = dot_nt(probes[i * tile : (i + 1) * tile, :], block[at : at + size, :])
        if block is span:
            value = value + hide
        return value, functools.reduce(jnp.maximum, lanes(value), peak)

    stats = jnp.zeros((rows, 128), F32)
    lowest = jnp.full((tile, 128), MASKED_SCORE, F32)
    ready, peak = [], lowest
    for p in range(len(pieces)):
        value, peak = score(0, p, peak)
        ready.append(value)
    for i in range(steps):
        top = jnp.max(peak, axis=1, keepdims=True)
        shift = jnp.broadcast_to(top, (tile, 128))
        total, summed = jnp.zeros((tile, 128), F32), 0.0
        coming, peak, weights = [], lowest, []
        for p in range(len(pieces)):
            if i + 1 < steps:
                value, peak = score(i + 1, p, peak)
                coming.append(value)
            for part in lanes(ready[p]):
                weight = jnp.exp2(part - shift)
                total = total + weight
                weights.append(weight.astype(BF16))
            if closing[p]:
                summed = summed + dot(jnp.concatenate(weights, axis=1), pieces[p][0][:, :KVR])
                weights = []
        ready = coming
        total = jnp.sum(total, axis=1, keepdims=True)
        mixed = (summed * (1.0 / total)).astype(BF16)
        level = top + jnp.log2(total)
        h = i * at_once
        maps = jnp.concatenate([value_up[h], value_up[h + 1]], axis=1)
        value = dot(mixed, maps).astype(BF16)
        out[:, h * VDIM : (h + 1) * VDIM] = value[:rows, :VDIM]
        out[:, (h + 1) * VDIM : (h + 2) * VDIM] = value[rows:, VDIM:]
        for k in range(at_once):
            stats = jnp.where(lane == h + k, level[k * rows : (k + 1) * rows], stats)
    high = stats.astype(BF16).astype(F32)
    rest = stats - high
    mid = rest.astype(BF16).astype(F32)
    joined = high + pltpu.roll(mid, n_head, axis=1) + pltpu.roll(rest - mid, 2 * n_head, axis=1)
    out[:, width:] = joined.astype(BF16)


def attend(by, value_up, near, far, span, *queries, keep_far=False):
    rows, n_head = span.shape[0], value_up.shape[0]
    out_shape = [jax.ShapeDtypeStruct((rows, n_head * VDIM + 128), BF16)]
    if keep_far:
        out_shape.append(jax.ShapeDtypeStruct(far.shape, BF16))
    specs, scratch = [VMEM], []
    if by != 0:
        specs = [ANY] * (len(queries) - 1) + [VMEM]
        scratch = [
            pltpu.VMEM((rows, queries[0].shape[1]), BF16),
            pltpu.VMEM((n_head * rows, WIDE), BF16),
            pltpu.SemaphoreType.DMA((2,)),
        ]
    return pl.pallas_call(
        functools.partial(attend_kernel, by, keep_far),
        out_shape=out_shape,
        in_specs=[VMEM] * 4 + specs,
        out_specs=[VMEM] * len(out_shape),
        scratch_shapes=scratch,
        compiler_params=params(32),
        name="attend_%d" % by,
    )(value_up, near, far, span, *queries)


def output_kernel(n_head, own, one, two, three, weight, exact, send):
    parts = (own, one, two, three)
    width = n_head * VDIM
    levels = []
    for part in parts:
        stat = part[:, width:].astype(F32)
        rest = pltpu.roll(stat, 128 - n_head, axis=1) + pltpu.roll(stat, 128 - 2 * n_head, axis=1)
        levels.append(stat + rest)
    top = functools.reduce(jnp.maximum, levels)
    shares = [jnp.exp2(level - top) for level in levels]
    total = functools.reduce(jnp.add, shares)
    head_of = lax.broadcasted_iota(jnp.int32, (128, width), 0)
    lane_of = lax.broadcasted_iota(jnp.int32, (128, width), 1)
    begin = head_of * VDIM
    spread = jnp.where((lane_of >= begin) & (lane_of < begin + VDIM), 1.0, 0.0).astype(BF16)
    mixed = 0.0
    for part, share in zip(parts, shares):
        share = share / total
        high = share.astype(BF16)
        low = (share - high.astype(F32)).astype(BF16)
        factor = dot(high, spread) + dot(low, spread)
        mixed = mixed + part[:, :width].astype(F32) * factor
    per_head = mixed.astype(BF16)
    block = 512
    for at in range(0, weight.shape[1], block):
        part = dot(per_head, weight[:, at : at + block])
        exact[:, at : at + block] = part
        send[:, at : at + block] = part.astype(BF16)


def project_output(own, one, two, three, w_out):
    rows = own.shape[0]
    depth, cols = w_out.shape
    return pl.pallas_call(
        functools.partial(output_kernel, depth // VDIM),
        out_shape=[
            jax.ShapeDtypeStruct((rows, cols), F32),
            jax.ShapeDtypeStruct((rows, cols), BF16),
        ],
        in_specs=[VMEM] * 5,
        out_specs=[VMEM] * 2,
        compiler_params=params(16),
        name="project_output",
    )(own, one, two, three, w_out)


def expert_kernel(tokens, exact, other, gain, w_gate_t, w_up_t, w_down, keep, send):
    half = keep.shape[1]
    middle = tokens[...].astype(F32) + (exact[...] + other[...].astype(F32))
    middle = middle.astype(BF16).astype(F32)
    mlp_in = rms(middle, gain[...].astype(F32).reshape(1, -1)).astype(BF16)
    gate = dot_nt(mlp_in, w_gate_t[...])
    up = dot_nt(mlp_in, w_up_t[...])
    hidden = (gate / (1.0 + jnp.exp(-gate)) * up).astype(BF16)
    low = dot(hidden, w_down[:, :half])
    high = dot(hidden, w_down[:, half:])
    first = lax.axis_index("tp") == 0
    keep[...] = jnp.where(first, middle[:, :half] + low, middle[:, half:] + high)
    send[...] = jnp.where(first, high, low).astype(BF16)


def expert(tokens, exact, other, gain, w_gate_t, w_up_t, w_down):
    rows, width = tokens.shape
    half = width // 2
    return pl.pallas_call(
        expert_kernel,
        out_shape=[
            jax.ShapeDtypeStruct((rows, half), F32),
            jax.ShapeDtypeStruct((rows, half), BF16),
        ],
        in_specs=[VMEM] * 7,
        out_specs=[VMEM] * 2,
        compiler_params=params(24),
        name="expert",
    )(tokens, exact, other, gain, w_gate_t, w_up_t, w_down)


def on_device(
    tokens,
    attn_gain,
    w_query,
    w_latent,
    kv_gain,
    w_key_up,
    w_value_up,
    w_out,
    mlp_gain,
    w_gate,
    w_up,
    w_down,
    page_pool,
    hit_owner,
    hit_slot,
    fetch_count,
):
    n_store = lax.axis_size("store")
    n_section = lax.axis_size("section")
    n_tp = lax.axis_size("tp")
    rows = tokens.shape[0]
    share = PAGE // (n_section * n_tp)

    swap = [(0, 1), (1, 0)]
    owner = hit_owner[:, :, 0]
    outgoing = pack_pages(owner, hit_slot, jnp.swapaxes(page_pool, 1, 2), share)
    outgoing, early_tokens = lax.optimization_barrier((outgoing, tokens))
    outgoing = outgoing.reshape(n_store, 2, share // 2, MSG)
    arrived = lax.all_to_all(outgoing, "store", split_axis=0, concat_axis=0, tiled=True)
    arrived = arrived.reshape(n_store, share, MSG)

    def shift(value, by):
        pairs = [((z + by) % n_section, z) for z in range(n_section)]
        return lax.ppermute(value, "section", pairs)

    table = rotation_table((hit_owner.shape[1]) * PAGE + n_section * rows)
    query, normed, turns = project(
        fetch_count, early_tokens, attn_gain, jnp.asarray(table), w_query
    )
    next_query, last_query = shift(query, 1), shift(query, -1)
    new_latent, span, own_probes = project_latent(
        normed, turns, w_latent.T, kv_gain, query, w_key_up
    )
    arrived, next_query, last_query, span = lax.optimization_barrier(
        (arrived, next_query, last_query, span)
    )

    cut = rows // 2
    far_low, far_high = shift(next_query[:cut], 1), shift(last_query[cut:], -1)

    near = build_keys(owner, fetch_count, arrived)
    far = lax.ppermute(near, "tp", swap)


    def partial_for(by, far, *queries, **flags):
        return attend(by, w_value_up, near, far, span, *queries, **flags)

    one, far = partial_for(1, far, next_query, w_key_up, keep_far=True)
    one, far_low, far_high = lax.optimization_barrier((one, far_low, far_high))
    one = shift(one, -1)
    (two,) = partial_for(2, far, far_low, far_high, w_key_up)
    two, last_query, one = lax.optimization_barrier((two, last_query, one))
    two = shift(two, -1)
    (three,) = partial_for(3, far, last_query, w_key_up)
    three, own_probes, two = lax.optimization_barrier((three, own_probes, two))
    three = shift(three, -3)
    two = shift(two, -1)
    (own,) = partial_for(0, far, own_probes)
    exact, send = project_output(own, one, two, three, w_out)
    incoming = lax.ppermute(send, "tp", swap)
    keep, send = expert(
        tokens,
        exact,
        incoming,
        mlp_gain,
        w_gate.T,
        w_up.T,
        w_down,
    )
    layer_out = (keep + lax.ppermute(send, "tp", swap).astype(F32)).astype(BF16)
    return (layer_out, new_latent.T)


def solution(mesh):
    in_specs = (
        P(("store", "section"), None),
        P(),
        P(None, "tp"),
        P(),
        P(),
        P("tp", None, None),
        P("tp", None, None),
        P("tp", None),
        P(),
        P(None, "tp"),
        P(None, "tp"),
        P("tp", None),
        P("store", None, None),
        P(),
        P(),
        P(),
    )
    out_specs = (P(("store", "section"), "tp"), P(("store", "section"), None))
    return jax.shard_map(
        on_device, mesh=mesh, in_specs=in_specs, out_specs=out_specs, check_vma=False
    )
```

```python
import functools
import math

import jax
import jax.numpy as jnp
import numpy as np
from jax import lax
from jax.experimental import pallas as pl
from jax.experimental.pallas import tpu as pltpu
from jax.sharding import PartitionSpec as P

NOPE = 128
ROPE = 64
KVR = 512
PAGE = 256
LAT = KVR + ROPE
WIDE = KVR + 2 * ROPE
MSG = 2 * LAT
VDIM = 128
EPSILON = 1e-06
ROTARY_BASE = 10000.0
MASKED_SCORE = -1e30
SCALE = (NOPE + ROPE) ** (-0.5) / math.log(2.0)
F32 = jnp.float32
BF16 = jnp.bfloat16
MB = 1024 * 1024

VMEM = pl.BlockSpec(memory_space=pltpu.VMEM)
SMEM = pl.BlockSpec(memory_space=pltpu.SMEM)
HBM = pl.BlockSpec(memory_space=pltpu.HBM)
ANY = pl.BlockSpec(memory_space=pl.ANY)


def params(mb):
    return pltpu.CompilerParams(vmem_limit_bytes=mb * MB)


def dot(a, b):
    return jnp.dot(a, b, preferred_element_type=F32)


def dot_nt(a, b):
    return lax.dot_general(a, b, (((1,), (1,)), ((), ())), preferred_element_type=F32)


def rms(values, gain):
    mean_sq = jnp.mean(values * values, axis=-1, keepdims=True)
    return values * lax.rsqrt(mean_sq + EPSILON) * gain


def turn(values, cosine, sine):
    lane = lax.broadcasted_iota(jnp.int32, values.shape, 1)
    low = (lane & (ROPE // 2)) == 0
    partner = jnp.where(
        low, pltpu.roll(values, 128 - ROPE // 2, axis=1), pltpu.roll(values, ROPE // 2, axis=1)
    )
    return values * cosine + partner * sine


def pack_kernel(owner_src, slot_src, pool_src, out, owner, slot, pool, message, sems):
    group = lax.axis_index("store")
    shard = lax.axis_index("section") * lax.axis_size("tp") + lax.axis_index("tp")
    n_pages, width, window = pool.shape
    n_store, rows, _ = message.shape
    per = window // rows
    pairs = [(owner_src, owner), (slot_src, slot)]
    part = pl.ds(pl.multiple_of((shard // per) * window, window), window)
    for k in range(n_pages // 2):
        at = pl.ds(2 * k, 2)
        pairs.append((pool_src.at[at, :, part], pool.at[at]))
    copies = [
        pltpu.make_async_copy(src, dst, sems.at[i]) for i, (src, dst) in enumerate(pairs)
    ]
    for copy in copies:
        copy.start()
    copies[0].wait()
    copies[1].wait()
    n_list = owner.shape[1]
    held = owner[...] == group
    entry = lax.broadcasted_iota(jnp.int32, held.shape, 1)
    low = jnp.min(jnp.where(held, entry, n_list), axis=1, keepdims=True)
    high = jnp.max(jnp.where(held, entry, -1), axis=1, keepdims=True)
    at_once = n_store // 2
    row = lax.broadcasted_iota(jnp.int32, (rows, 1), 0)
    column = lax.broadcasted_iota(jnp.int32, (at_once * rows, n_pages * rows), 1)
    chosen = {}
    for which, hit in enumerate((low, high)):
        page = jnp.sum(jnp.where(entry == hit, slot[...], 0), axis=1, keepdims=True) * rows
        for to in range(0, n_store, at_once):
            wanted = [
                jnp.broadcast_to(page[g : g + 1], (rows, 1)) + row for g in range(to, to + at_once)
            ]
            wanted = jnp.concatenate(wanted, axis=0)
            chosen[to, which] = jnp.where(column == wanted, 1.0, 0.0).astype(BF16)
    first = (shard % per) * rows
    lane = lax.broadcasted_iota(jnp.int32, (width, window), 1)
    joined = []
    for at in range(0, n_pages, per):
        part = None
        for k in range(per):
            if k % 2 == 0:
                copies[2 + (at + k) // 2].wait()
            moved = pltpu.roll(pool[at + k].astype(F32), (k * rows - first + window) % window, axis=1)
            part = moved if part is None else jnp.where(lane >= k * rows, moved, part)
        joined.append(part.astype(BF16))
    stage = jnp.concatenate(joined, axis=1)
    sends = []
    for to in range(0, n_store, at_once):
        at = pl.ds(to, at_once)
        taken = [dot_nt(chosen[to, which], stage) for which in range(2)]
        ropes = jnp.concatenate([part[:, KVR:] for part in taken], axis=1)
        for which, part in enumerate(taken):
            message[at, :, which * KVR : (which + 1) * KVR] = (
                part[:, :KVR].astype(BF16).reshape(at_once, rows, KVR)
            )
        message[at, :, 2 * KVR :] = ropes.astype(BF16).reshape(at_once, rows, 2 * ROPE)
        send = pltpu.make_async_copy(message.at[at], out.at[at], sems.at[len(copies) + len(sends)])
        send.start()
        sends.append(send)
    for send in sends:
        send.wait()


def pack_pages(owner, slot, pool_t, rows):
    n_store, n_pages = owner.shape[0], pool_t.shape[0]
    return pl.pallas_call(
        pack_kernel,
        out_shape=jax.ShapeDtypeStruct((n_store, rows, MSG), BF16),
        in_specs=[HBM] * 3,
        out_specs=HBM,
        scratch_shapes=[
            pltpu.VMEM(owner.shape, jnp.int32),
            pltpu.VMEM(slot.shape, jnp.int32),
            pltpu.VMEM((*pool_t.shape[:2], 128), BF16),
            pltpu.VMEM((n_store, rows, MSG), BF16),
            pltpu.SemaphoreType.DMA((4 + n_pages // 2,)),
        ],
        compiler_params=params(60),
        name="pack_pages",
    )(owner, slot, pool_t)


def keys_kernel(owner, count, pages, out, seen):
    rows = pages.shape[1]
    group = lax.axis_index("store")
    lane = lax.broadcasted_iota(jnp.int32, (rows, 128), 1)
    for k in range(pages.shape[0]):
        seen[k] = 0
    for j in range(owner.shape[1]):
        source = owner[group, j]
        second = seen[source] > 0
        seen[source] = 1
        bias = jnp.where(j < count[group], 0.0, MASKED_SCORE)
        row = pages[source]
        at = pl.ds(j * rows, rows)
        out[at, :KVR] = jnp.where(second, row[:, KVR : 2 * KVR], row[:, :KVR])
        pair = row[:, 2 * KVR :].astype(F32)
        rot = jnp.where(second, pltpu.roll(pair, ROPE, axis=1), pair)
        last = jnp.where(lane == ROPE, bias, 0.0)
        out[at, KVR:] = jnp.where(lane < ROPE, rot, last).astype(BF16)


def build_keys(owner, count, pages):
    n_keys = owner.shape[1] * pages.shape[1]
    return pl.pallas_call(
        keys_kernel,
        out_shape=jax.ShapeDtypeStruct((n_keys, WIDE), BF16),
        in_specs=[SMEM, SMEM, VMEM],
        out_specs=VMEM,
        scratch_shapes=[pltpu.SMEM((pages.shape[0],), jnp.int32)],
        compiler_params=params(24),
        name="build_keys",
    )(owner, count, pages)


def rotation_table(n_rows):
    half = ROPE // 2
    freq = np.float32(ROTARY_BASE) ** (-(np.arange(half, dtype=np.float32) / np.float32(half)))
    angle = np.arange(n_rows, dtype=np.float32)[:, None] * freq.astype(np.float32)[None, :]
    angle = angle.astype(np.float64)
    parts = [np.cos(angle), np.cos(angle), -np.sin(angle), np.sin(angle)]
    return np.concatenate(parts, axis=1).astype(np.float32)


def project_kernel(
    count, tokens_src, gain, table, w_query_src, query, normed, turns, tokens, w_query, total, sems
):
    rows = tokens.shape[0]
    group, section = lax.axis_index("store"), lax.axis_index("section")
    start = pl.multiple_of(count[group] * PAGE + section * rows, rows)
    pairs = [(tokens_src, tokens), (table.at[pl.ds(start, rows), :], turns)]
    pieces = 8
    depth = w_query.shape[0] // pieces
    for k in range(pieces):
        at = pl.ds(k * depth, depth)
        pairs.append((w_query_src.at[at, :], w_query.at[at, :]))
    copies = [
        pltpu.make_async_copy(src, dst, sems.at[i]) for i, (src, dst) in enumerate(pairs)
    ]
    for copy in copies:
        copy.start()
    copies[0].wait()
    normed[...] = rms(tokens[...].astype(F32), gain[...].astype(F32).reshape(1, -1)).astype(BF16)
    copies[1].wait()
    cosine, sine = turns[:, :ROPE], turns[:, ROPE:]
    cosine = jnp.concatenate([cosine, cosine], axis=1)
    sine = jnp.concatenate([sine, sine], axis=1)
    for k in range(0, pieces, 2):
        copies[2 + k].wait()
        copies[3 + k].wait()
        at = slice(k * depth, (k + 2) * depth)
        part = dot(normed[:, at], w_query[at, :])
        total[...] = part if k == 0 else total[...] + part
    head = NOPE + ROPE
    for at in range(0, query.shape[1], 2 * head):
        part = total[:, at : at + 2 * head].astype(BF16).astype(F32)
        query[:, at : at + NOPE] = part[:, :NOPE].astype(BF16)
        query[:, at + NOPE : at + 2 * NOPE] = part[:, head : head + NOPE].astype(BF16)
        pair = jnp.concatenate([part[:, NOPE:head], part[:, head + NOPE :]], axis=1)
        query[:, at + 2 * NOPE : at + 2 * head] = (turn(pair, cosine, sine) * SCALE).astype(BF16)


def project(count, tokens, gain, table, w_query):
    rows, width = tokens.shape
    cols = w_query.shape[1]
    return pl.pallas_call(
        project_kernel,
        out_shape=[
            jax.ShapeDtypeStruct((rows, cols), BF16),
            jax.ShapeDtypeStruct(tokens.shape, BF16),
            jax.ShapeDtypeStruct((rows, 2 * ROPE), F32),
        ],
        in_specs=[SMEM, HBM, VMEM] + [HBM] * 2,
        out_specs=[VMEM] * 3,
        scratch_shapes=[
            pltpu.VMEM(tokens.shape, BF16),
            pltpu.VMEM(w_query.shape, BF16),
            pltpu.VMEM((rows, cols), F32),
            pltpu.SemaphoreType.DMA((10,)),
        ],
        compiler_params=params(60),
        name="project",
    )(count, tokens, gain, table, w_query)


def latent_kernel(
    normed, turns, w_latent_t, kv_gain, query, key_up, new_latent, span, probes
):
    cosine, sine = turns[:, :ROPE], turns[:, ROPE:]
    cosine = jnp.concatenate([cosine, cosine], axis=1)
    sine = jnp.concatenate([sine, sine], axis=1)
    raw = dot_nt(normed[...], w_latent_t[...])
    latent = rms(raw[:, :KVR], kv_gain[...].astype(F32).reshape(1, -1)).astype(BF16)
    pair = jnp.concatenate([raw[:, KVR:], raw[:, KVR:]], axis=1)
    turned = turn(pair, cosine, sine)
    new_latent[:KVR, :] = latent.astype(F32).T.astype(BF16)
    new_latent[KVR:, :] = turned.T[:ROPE].astype(BF16)
    lane = lax.broadcasted_iota(jnp.int32, turned.shape, 1)
    span[:, :KVR] = latent
    span[:, KVR:] = jnp.where(lane < ROPE, turned, 0.0).astype(BF16)
    fill_probes(query, key_up, probes)


def project_latent(normed, turns, w_latent_t, kv_gain, query, key_up):
    rows = normed.shape[0]
    return pl.pallas_call(
        latent_kernel,
        out_shape=[
            jax.ShapeDtypeStruct((LAT, rows), BF16),
            jax.ShapeDtypeStruct((rows, WIDE), BF16),
            jax.ShapeDtypeStruct((key_up.shape[0] * rows, WIDE), BF16),
        ],
        in_specs=[VMEM] * 6,
        out_specs=[VMEM] * 3,
        compiler_params=params(20),
        name="project_latent",
    )(normed, turns, w_latent_t, kv_gain, query, key_up)


def fill_probes(query, key_up, probes):
    rows = query.shape[0]
    pair_width = 2 * (NOPE + ROPE)
    lane = lax.broadcasted_iota(jnp.int32, (rows, 2 * NOPE), 1)
    rope_lane = lane[:, : 2 * ROPE]
    for h in range(0, key_up.shape[0], 2):
        base = (h // 2) * pair_width
        nope = query[:, base : base + 2 * NOPE].astype(F32)
        both = jnp.concatenate(
            [jnp.where(lane < NOPE, nope, 0.0), jnp.where(lane < NOPE, 0.0, nope)], axis=0
        )
        maps = jnp.concatenate([key_up[h], key_up[h + 1]], axis=1)
        at = pl.ds(h * rows, 2 * rows)
        probes[at, :KVR] = (dot_nt(both.astype(BF16), maps) * SCALE).astype(BF16)
        pair = query[:, base + 2 * NOPE : base + pair_width].astype(F32)
        pair = jnp.concatenate([pair, pltpu.roll(pair, ROPE, axis=1)], axis=0)
        rope_lanes = jnp.concatenate([rope_lane, rope_lane], axis=0)
        one = jnp.where(rope_lanes == ROPE, 1.0, 0.0)
        probes[at, KVR:] = jnp.where(rope_lanes < ROPE, pair, one).astype(BF16)


def probes_kernel(key_up, source, probes, query, sem):
    copy = pltpu.make_async_copy(source, query, sem)
    copy.start()
    copy.wait()
    fill_probes(query, key_up, probes)


def make_probes(key_up, query):
    rows, width = query.shape
    return pl.pallas_call(
        probes_kernel,
        out_shape=jax.ShapeDtypeStruct((key_up.shape[0] * rows, WIDE), BF16),
        in_specs=[VMEM, ANY],
        out_specs=VMEM,
        scratch_shapes=[pltpu.VMEM((rows, width), BF16), pltpu.SemaphoreType.DMA],
        compiler_params=params(20),
        name="make_probes",
    )(key_up, query)


def attend_kernel(by, keep_far, value_up, near, arrived, span, *refs):
    far = arrived
    if by == 2:
        low, high, key_up, out, query, probes = refs
        query[: low.shape[0], :] = low[...]
        query[low.shape[0] :, :] = high[...]
        fill_probes(query, key_up, probes)
    elif keep_far:
        probes, out, far = refs
        far[...] = arrived[...]
    else:
        probes, out = refs
    n_head, rows = value_up.shape[0], out.shape[0]
    blocks = (near, far, span)
    lane = lax.broadcasted_iota(jnp.int32, (rows, 128), 1)
    at_once = 2
    tile = at_once * rows
    steps = n_head // at_once
    width = n_head * NOPE

    if by == 0:
        row_of = lax.broadcasted_iota(jnp.int32, (tile, rows), 0) & (rows - 1)
        key_of = lax.broadcasted_iota(jnp.int32, (tile, rows), 1)
        hide = jnp.where(key_of <= row_of, 0.0, MASKED_SCORE)
    else:
        later = lax.axis_index("section") + by < lax.axis_size("section")
        hide = jnp.where(later, 0.0, MASKED_SCORE)

    pieces, closing = [], []
    for block in blocks:
        step = min(256, block.shape[0])
        for at in range(0, block.shape[0], step):
            pieces.append((block, at, step))
            closing.append(at + step == block.shape[0])

    def lanes(value):
        return [value[:, at : at + 128] for at in range(0, value.shape[1], 128)]

    def score(i, p, peak):
        block, at, size = pieces[p]
        value = dot_nt(probes[i * tile : (i + 1) * tile, :], block[at : at + size, :])
        if block is span:
            value = value + hide
        return value, functools.reduce(jnp.maximum, lanes(value), peak)

    stats = jnp.zeros((rows, 128), F32)
    lowest = jnp.full((tile, 128), MASKED_SCORE, F32)
    ready, peak = [], lowest
    for p in range(len(pieces)):
        value, peak = score(0, p, peak)
        ready.append(value)
    for i in range(steps):
        top = jnp.max(peak, axis=1, keepdims=True)
        shift = jnp.broadcast_to(top, (tile, 128))
        total, summed = jnp.zeros((tile, 128), F32), 0.0
        coming, peak, weights = [], lowest, []
        for p in range(len(pieces)):
            if i + 1 < steps:
                value, peak = score(i + 1, p, peak)
                coming.append(value)
            for part in lanes(ready[p]):
                weight = jnp.exp2(part - shift)
                total = total + weight
                weights.append(weight.astype(BF16))
            if closing[p]:
                summed = summed + dot(jnp.concatenate(weights, axis=1), pieces[p][0][:, :KVR])
                weights = []
        ready = coming
        total = jnp.sum(total, axis=1, keepdims=True)
        mixed = (summed * (1.0 / total)).astype(BF16)
        level = top + jnp.log2(total)
        h = i * at_once
        maps = jnp.concatenate([value_up[h], value_up[h + 1]], axis=1)
        value = dot(mixed, maps).astype(BF16)
        out[:, h * VDIM : (h + 1) * VDIM] = value[:rows, :VDIM]
        out[:, (h + 1) * VDIM : (h + 2) * VDIM] = value[rows:, VDIM:]
        for k in range(at_once):
            stats = jnp.where(lane == h + k, level[k * rows : (k + 1) * rows], stats)
    high = stats.astype(BF16).astype(F32)
    rest = stats - high
    mid = rest.astype(BF16).astype(F32)
    joined = high + pltpu.roll(mid, n_head, axis=1) + pltpu.roll(rest - mid, 2 * n_head, axis=1)
    out[:, width:] = joined.astype(BF16)


def attend(by, value_up, near, far, span, *queries, keep_far=False):
    rows, n_head = span.shape[0], value_up.shape[0]
    out_shape = [jax.ShapeDtypeStruct((rows, n_head * VDIM + 128), BF16)]
    if keep_far:
        out_shape.append(jax.ShapeDtypeStruct(far.shape, BF16))
    scratch = []
    if by == 2:
        scratch.append(pltpu.VMEM((rows, queries[0].shape[1]), BF16))
        scratch.append(pltpu.VMEM((n_head * rows, WIDE), BF16))
    return pl.pallas_call(
        functools.partial(attend_kernel, by, keep_far),
        out_shape=out_shape,
        in_specs=[VMEM] * (4 + len(queries)),
        out_specs=[VMEM] * len(out_shape),
        scratch_shapes=scratch,
        compiler_params=params(32),
        name="attend_%d" % by,
    )(value_up, near, far, span, *queries)


def output_kernel(n_head, own, one, two, three, weight, exact, send):
    parts = (own, one, two, three)
    width = n_head * VDIM
    levels = []
    for part in parts:
        stat = part[:, width:].astype(F32)
        rest = pltpu.roll(stat, 128 - n_head, axis=1) + pltpu.roll(stat, 128 - 2 * n_head, axis=1)
        levels.append(stat + rest)
    top = functools.reduce(jnp.maximum, levels)
    shares = [jnp.exp2(level - top) for level in levels]
    total = functools.reduce(jnp.add, shares)
    head_of = lax.broadcasted_iota(jnp.int32, (128, width), 0)
    lane_of = lax.broadcasted_iota(jnp.int32, (128, width), 1)
    begin = head_of * VDIM
    spread = jnp.where((lane_of >= begin) & (lane_of < begin + VDIM), 1.0, 0.0).astype(BF16)
    mixed = 0.0
    for part, share in zip(parts, shares):
        share = share / total
        high = share.astype(BF16)
        low = (share - high.astype(F32)).astype(BF16)
        factor = dot(high, spread) + dot(low, spread)
        mixed = mixed + part[:, :width].astype(F32) * factor
    per_head = mixed.astype(BF16)
    block = 512
    for at in range(0, weight.shape[1], block):
        part = dot(per_head, weight[:, at : at + block])
        exact[:, at : at + block] = part
        send[:, at : at + block] = part.astype(BF16)


def project_output(own, one, two, three, w_out):
    rows = own.shape[0]
    depth, cols = w_out.shape
    return pl.pallas_call(
        functools.partial(output_kernel, depth // VDIM),
        out_shape=[
            jax.ShapeDtypeStruct((rows, cols), F32),
            jax.ShapeDtypeStruct((rows, cols), BF16),
        ],
        in_specs=[VMEM] * 5,
        out_specs=[VMEM] * 2,
        compiler_params=params(16),
        name="project_output",
    )(own, one, two, three, w_out)


def expert_kernel(tokens, exact, other, gain, w_gate_t, w_up_t, w_down, keep, send):
    half = keep.shape[1]
    middle = tokens[...].astype(F32) + (exact[...] + other[...].astype(F32))
    middle = middle.astype(BF16).astype(F32)
    mlp_in = rms(middle, gain[...].astype(F32).reshape(1, -1)).astype(BF16)
    gate = dot_nt(mlp_in, w_gate_t[...])
    up = dot_nt(mlp_in, w_up_t[...])
    hidden = (gate / (1.0 + jnp.exp(-gate)) * up).astype(BF16)
    low = dot(hidden, w_down[:, :half])
    high = dot(hidden, w_down[:, half:])
    first = lax.axis_index("tp") == 0
    keep[...] = jnp.where(first, middle[:, :half] + low, middle[:, half:] + high)
    send[...] = jnp.where(first, high, low).astype(BF16)


def expert(tokens, exact, other, gain, w_gate_t, w_up_t, w_down):
    rows, width = tokens.shape
    half = width // 2
    return pl.pallas_call(
        expert_kernel,
        out_shape=[
            jax.ShapeDtypeStruct((rows, half), F32),
            jax.ShapeDtypeStruct((rows, half), BF16),
        ],
        in_specs=[VMEM] * 7,
        out_specs=[VMEM] * 2,
        compiler_params=params(24),
        name="expert",
    )(tokens, exact, other, gain, w_gate_t, w_up_t, w_down)


def on_device(
    tokens,
    attn_gain,
    w_query,
    w_latent,
    kv_gain,
    w_key_up,
    w_value_up,
    w_out,
    mlp_gain,
    w_gate,
    w_up,
    w_down,
    page_pool,
    hit_owner,
    hit_slot,
    fetch_count,
):
    n_store = lax.axis_size("store")
    n_section = lax.axis_size("section")
    n_tp = lax.axis_size("tp")
    rows = tokens.shape[0]
    share = PAGE // (n_section * n_tp)

    swap = [(0, 1), (1, 0)]
    owner = hit_owner[:, :, 0]
    outgoing = pack_pages(owner, hit_slot, jnp.swapaxes(page_pool, 1, 2), share)
    outgoing, early_tokens = lax.optimization_barrier((outgoing, tokens))
    outgoing = outgoing.reshape(n_store, 2, share // 2, MSG)
    arrived = lax.all_to_all(outgoing, "store", split_axis=0, concat_axis=0, tiled=True)
    arrived = arrived.reshape(n_store, share, MSG)

    def shift(value, by):
        pairs = [((z + by) % n_section, z) for z in range(n_section)]
        return lax.ppermute(value, "section", pairs)

    table = rotation_table((hit_owner.shape[1]) * PAGE + n_section * rows)
    query, normed, turns = project(
        fetch_count, early_tokens, attn_gain, jnp.asarray(table), w_query
    )
    next_query, last_query = shift(query, 1), shift(query, -1)
    new_latent, span, own_probes = project_latent(
        normed, turns, w_latent.T, kv_gain, query, w_key_up
    )
    arrived, next_query, last_query, span = lax.optimization_barrier(
        (arrived, next_query, last_query, span)
    )

    cut = rows // 2
    far_low, far_high = shift(next_query[:cut], 1), shift(last_query[cut:], -1)

    near = build_keys(owner, fetch_count, arrived)
    far = lax.ppermute(near, "tp", swap)

    next_probes = make_probes(w_key_up, next_query)

    def partial_for(by, far, *queries, **flags):
        return attend(by, w_value_up, near, far, span, *queries, **flags)

    one, far = partial_for(1, far, next_probes, keep_far=True)
    one, far_low, far_high = lax.optimization_barrier((one, far_low, far_high))
    one = shift(one, -1)
    (two,) = partial_for(2, far, far_low, far_high, w_key_up)
    two, last_query = lax.optimization_barrier((two, last_query))
    last_probes = make_probes(w_key_up, last_query)
    last_probes, one = lax.optimization_barrier((last_probes, one))
    two = shift(two, -1)
    (three,) = partial_for(3, far, last_probes)
    three, own_probes, two = lax.optimization_barrier((three, own_probes, two))
    three = shift(three, -3)
    two = shift(two, -1)
    (own,) = partial_for(0, far, own_probes)
    exact, send = project_output(own, one, two, three, w_out)
    incoming = lax.ppermute(send, "tp", swap)
    keep, send = expert(
        tokens,
        exact,
        incoming,
        mlp_gain,
        w_gate.T,
        w_up.T,
        w_down,
    )
    layer_out = (keep + lax.ppermute(send, "tp", swap).astype(F32)).astype(BF16)
    return (layer_out, new_latent.T)


def solution(mesh):
    in_specs = (
        P(("store", "section"), None),
        P(),
        P(None, "tp"),
        P(),
        P(),
        P("tp", None, None),
        P("tp", None, None),
        P("tp", None),
        P(),
        P(None, "tp"),
        P(None, "tp"),
        P("tp", None),
        P("store", None, None),
        P(),
        P(),
        P(),
    )
    out_specs = (P(("store", "section"), "tp"), P(("store", "section"), None))
    return jax.shard_map(
        on_device, mesh=mesh, in_specs=in_specs, out_specs=out_specs, check_vma=False
    )
```
